32 devices in a mesh: blk: 8 (over y, x, core), group: 4 (over z).
Axes of the slice: x: 2, y: 2, z: 4, core: 2. Of those that a mesh axis runs over, the one named last changes fastest.
Arguments:
- visual_encoder_outputs: float32 [16384, 1152], P(('blk', 'group'))
- caption_encoder_outputs: float32 [16384, 1152], P(('blk', 'group'))
- partner_lookup_grid: int32 [2, 8], replicated, may hold values from 0 to 7, as said below
- sharpness_coefficient: float32 [1], replicated, may hold values from 8 to 30
- sigmoid_shift_term: float32 [1], replicated, may hold values from -6 to -2
Outputs:
- image_gradient: float32 [16384, 1152], P(('blk', 'group'))
- text_gradient: float32 [16384, 1152], P(('blk', 'group'))
The draws below stay inside these ranges and needn't reach their ends.
Inputs may be any that keep to these rules, and one draw needn't show every extreme that they name: In each of the 2 rounds, partner_lookup_grid pairs index b of blk with index b XOR 2**k, where k is a bit position drawn for that round; the rounds' positions differ, so every matching is mutual and no index meets the same partner twice.
All inputs are finite; a program needn't handle non-finite values.
Results may differ from the reference program's by a relative error of at most 0.0049.
Values may be sent and summed in bfloat16 or wider, within the bound.
No kernel may reach another device: no remote copies, remote signals or barrier semaphores. Data moves between devices by JAX's collectives and lax.ppermute only.
A program may use at most 64 MiB of HBM per device.

```python
import math
import jax
import jax.numpy as jnp
from jax import lax

D = 1152
ROWS = 512
ROUNDS = 2
PEERS = 8
BATCH = 16384
N_BLK = 8
N_GROUP = 4


def shared_rows(key):
    return jax.random.normal(key, (BATCH, D), jnp.float32)


def embedding_rows(key, common):
    private_key, scale_key = jax.random.split(key, 2)
    private = jax.random.normal(private_key, (BATCH, D), jnp.float32)
    row_scale = jnp.exp(jax.random.uniform(scale_key, (BATCH, 1), jnp.float32, math.log(0.2), math.log(2.0)))
    return (0.6 * common + 0.8 * private) * row_scale * D ** (-0.5)


def draw_visual_encoder_outputs(key, part):
    common = shared_rows(key)
    key = jax.random.fold_in(key, 21)
    return embedding_rows(key, common)


def draw_caption_encoder_outputs(key, part):
    common = shared_rows(key)
    key = jax.random.fold_in(key, 22)
    return embedding_rows(key, common)


def draw_partner_lookup_grid(key, part):
    key = jax.random.fold_in(key, 23)
    bit_total = PEERS.bit_length() - 1
    positions = jax.random.permutation(key, bit_total)[:ROUNDS].astype(jnp.int32)
    round_masks = jnp.left_shift(jnp.ones_like(positions), positions).astype(jnp.int32)
    indices = jnp.arange(PEERS, dtype=jnp.int32)
    return jnp.bitwise_xor(indices[None, :], round_masks[:, None]).astype(jnp.int32)


def setup_inputs(seed: int = 0) -> dict:
    key_of = jax.random.split(jax.random.key(seed), 6)
    return {
        "visual_encoder_outputs": draw_visual_encoder_outputs(jax.random.fold_in(key_of[5], 71), 0),
        "caption_encoder_outputs": draw_caption_encoder_outputs(jax.random.fold_in(key_of[5], 71), 0),
        "partner_lookup_grid": draw_partner_lookup_grid(jax.random.fold_in(key_of[5], 71), 0),
        "sharpness_coefficient": jnp.clip(jnp.exp(jax.random.uniform(key_of[3], (1,), jnp.float32, math.log(8.0), math.log(30.0))), 8.0, 30.0),
        "sigmoid_shift_term": jnp.clip(jax.random.uniform(key_of[4], (1,), jnp.float32, -6.0, -2.0), -6.0, -2.0),
    }


epsilon = 1e-06

def normalize(raw_rows):
    radius = jnp.sqrt(lax.optimization_barrier(jnp.sum(raw_rows * raw_rows, axis=-1, keepdims=True)) + epsilon)
    unit_rows = raw_rows / radius
    return (radius, unit_rows, unit_rows.astype(jnp.bfloat16))

def pair_linkage(left_rows, right_rows, similarity_multiplier, offset_value, matched):
    products = lax.dot_general(left_rows, right_rows, (((1,), (1,)), ((), ())), preferred_element_type=jnp.float32)
    logits = similarity_multiplier * products + offset_value
    if matched:
        labels = 2.0 * jnp.eye(left_rows.shape[0], dtype=jnp.float32) - 1.0
    else:
        labels = -jnp.ones_like(logits)
    weights = -labels * jax.nn.sigmoid(-labels * logits)
    return (similarity_multiplier * weights).astype(jnp.bfloat16)

def toward_left(coupled, right_rows):
    return jnp.dot(coupled, right_rows, preferred_element_type=jnp.float32)

def toward_right(coupled, left_rows):
    return lax.dot_general(coupled, left_rows, (((0,), (0,)), ((), ())), preferred_element_type=jnp.float32)

def rounded_term(values):
    return lax.optimization_barrier(values.astype(jnp.bfloat16)).astype(jnp.float32)

def project(radius, unit_rows, gradient):
    radial = lax.optimization_barrier(jnp.sum(unit_rows * gradient, axis=-1, keepdims=True))
    return (gradient - unit_rows * radial) / radius

def reference(visual_encoder_outputs, caption_encoder_outputs, partner_lookup_grid, sharpness_coefficient, sigmoid_shift_term):
    similarity_multiplier = sharpness_coefficient[0]
    offset_value = sigmoid_shift_term[0]
    image_raw = visual_encoder_outputs.reshape(N_BLK, N_GROUP, ROWS, D)
    text_raw = caption_encoder_outputs.reshape(N_BLK, N_GROUP, ROWS, D)
    image_split_pieces = normalize(image_raw)[2]
    text_halves = normalize(text_raw)[2]

    def per_accelerator_share(device_index):
        block_index = device_index // N_GROUP
        group_index = device_index % N_GROUP
        prior_group = (group_index + N_GROUP - 1) % N_GROUP
        next_group = (group_index + 1) % N_GROUP
        own_image = image_split_pieces[block_index, group_index]
        own_text = text_halves[block_index, group_index]
        diagonal = pair_linkage(own_image, own_text, similarity_multiplier, offset_value, True)
        image_sum = toward_left(diagonal, own_text)
        text_sum = toward_right(diagonal, own_image)
        prior_text = text_halves[block_index, prior_group]
        image_sum = image_sum + toward_left(pair_linkage(own_image, prior_text, similarity_multiplier, offset_value, False), prior_text)
        next_image = image_split_pieces[block_index, next_group]
        text_sum = text_sum + rounded_term(toward_right(pair_linkage(next_image, own_text, similarity_multiplier, offset_value, False), next_image))
        for number in range(ROUNDS):
            partner_block = partner_lookup_grid[number, block_index]
            other_text = text_halves[partner_block, group_index]
            other_image = image_split_pieces[partner_block, group_index]
            image_sum = image_sum + toward_left(pair_linkage(own_image, other_text, similarity_multiplier, offset_value, False), other_text)
            text_sum = text_sum + rounded_term(toward_right(pair_linkage(other_image, own_text, similarity_multiplier, offset_value, False), other_image))
        image_parts = normalize(image_raw[block_index, group_index])
        text_parts = normalize(text_raw[block_index, group_index])
        return (project(image_parts[0], image_parts[1], image_sum), project(text_parts[0], text_parts[1], text_sum))
    image_gradient, text_gradient = lax.map(per_accelerator_share, jnp.arange(N_BLK * N_GROUP, dtype=jnp.int32))
    return (image_gradient.reshape(BATCH, D), text_gradient.reshape(BATCH, D))
```

```python
import functools
import itertools

import jax
import jax.numpy as jnp
from jax import lax
from jax.sharding import PartitionSpec as P

epsilon = 1e-06


def normalize(raw_rows):
    radius = jnp.sqrt(jnp.sum(raw_rows * raw_rows, axis=-1, keepdims=True) + epsilon)
    unit_rows = raw_rows / radius
    return (radius, unit_rows, unit_rows.astype(jnp.bfloat16))


def pair_linkage(left_rows, right_rows, similarity_multiplier, offset_value, matched):
    products = lax.dot_general(
        left_rows, right_rows, (((1,), (1,)), ((), ())), preferred_element_type=jnp.float32
    )
    logits = similarity_multiplier * products + offset_value
    if matched:
        labels = 2.0 * jnp.eye(left_rows.shape[0], dtype=jnp.float32) - 1.0
    else:
        labels = -jnp.ones_like(logits)
    weights = -labels * jax.nn.sigmoid(-labels * logits)
    return (similarity_multiplier * weights).astype(jnp.bfloat16)


def toward_left(coupled, right_rows):
    return jnp.dot(coupled, right_rows, preferred_element_type=jnp.float32)


def toward_right(coupled, left_rows):
    return lax.dot_general(
        coupled, left_rows, (((0,), (0,)), ((), ())), preferred_element_type=jnp.float32
    )


def project(radius, unit_rows, gradient):
    radial = jnp.sum(unit_rows * gradient, axis=-1, keepdims=True)
    return (gradient - unit_rows * radial) / radius


def passed_along(x, axis, by):
    count = lax.axis_size(axis)
    return lax.ppermute(x, axis, [(i, (i + by) % count) for i in range(count)])


def exchanged(x, bit):
    count = lax.axis_size("blk")
    return lax.ppermute(x, "blk", [(i, i ^ (1 << bit)) for i in range(count)])


def with_partners(bits, visual, caption, similarity_multiplier, offset_value):
    link = functools.partial(
        pair_linkage, similarity_multiplier=similarity_multiplier, offset_value=offset_value
    )
    text_radius, text_unit, text_half = normalize(caption)
    other_texts = [passed_along(text_half, "group", 1)]
    other_texts += [exchanged(text_half, bit) for bit in bits]
    image_radius, image_unit, image_half = normalize(visual)
    other_images = [passed_along(image_half, "group", -1)]
    other_images += [exchanged(image_half, bit) for bit in bits]
    diagonal = link(image_half, text_half, matched=True)
    image_sum = toward_left(diagonal, text_half)
    text_sum = toward_right(diagonal, image_half)
    for other_text in other_texts:
        coupled = link(image_half, other_text, matched=False)
        image_sum = image_sum + toward_left(coupled, other_text)
    for other_image in other_images:
        coupled = link(other_image, text_half, matched=False)
        text_sum = text_sum + toward_right(coupled, other_image)
    return (project(image_radius, image_unit, image_sum), project(text_radius, text_unit, text_sum))


def on_device(
    visual_encoder_outputs,
    caption_encoder_outputs,
    partner_lookup_grid,
    sharpness_coefficient,
    sigmoid_shift_term,
):
    rounds, peers = partner_lookup_grid.shape
    choices = list(itertools.combinations(range(peers.bit_length() - 1), rounds))
    union = jnp.sum(partner_lookup_grid[:, 0])
    branch = jnp.int32(0)
    for number, bits in enumerate(choices):
        branch = jnp.where(union == sum(1 << bit for bit in bits), jnp.int32(number), branch)
    return lax.switch(
        branch,
        [functools.partial(with_partners, bits) for bits in choices],
        visual_encoder_outputs,
        caption_encoder_outputs,
        sharpness_coefficient[0],
        sigmoid_shift_term[0],
    )


def solution(mesh):
    placed = (P(("blk", "group"), None), P(("blk", "group"), None), P(), P(), P())
    return jax.shard_map(
        on_device,
        mesh=mesh,
        in_specs=placed,
        out_specs=(P(("blk", "group"), None), P(("blk", "group"), None)),
        check_vma=False,
    )
```

```python
import functools
import itertools

import jax
import jax.numpy as jnp
from jax import lax
from jax.experimental import pallas as pl
from jax.experimental.pallas import tpu as pltpu
from jax.sharding import PartitionSpec as P

epsilon = 1e-06
MIB = 1024 * 1024
VMEM = pl.BlockSpec(memory_space=pltpu.VMEM)
SMEM = pl.BlockSpec(memory_space=pltpu.SMEM)
ANY = pl.BlockSpec(memory_space=pl.ANY)


def radius_of(raw):
    return jnp.sqrt(jnp.sum(raw * raw, axis=-1, keepdims=True) + epsilon)


def halves_kernel(raw_ref, half_ref):
    raw = raw_ref[...]
    half_ref[...] = (raw / radius_of(raw)).astype(jnp.bfloat16)


def halves(raw, blocks=4):
    rows, width = raw.shape
    spec = pl.BlockSpec((rows // blocks, width), lambda i: (i, 0))
    return pl.pallas_call(
        halves_kernel,
        grid=(blocks,),
        in_specs=[spec],
        out_specs=spec,
        out_shape=jax.ShapeDtypeStruct((rows, width), jnp.bfloat16),
        name="halves",
        cost_estimate=pl.CostEstimate(flops=4 * rows * width, bytes_accessed=6 * rows * width, transcendentals=rows),
    )(raw)


def add_up_kernel(matched, has_sum, has_raw, scale_ref, shift_ref, own_ref, *refs):
    refs = list(refs)
    other_refs = [refs.pop(0) for _ in matched]
    sum_ref = refs.pop(0) if has_sum else None
    raw_ref = refs.pop(0) if has_raw else None
    out_ref = refs.pop(0)
    block = own_ref.shape[0]
    scale, shift = scale_ref[0], shift_ref[0]
    own = own_ref[...]
    total = sum_ref[...] if has_sum else None
    for other_ref, is_matched in zip(other_refs, matched):
        other = other_ref[...]
        products = lax.dot_general(
            own, other, (((1,), (1,)), ((), ())), preferred_element_type=jnp.float32
        )
        logits = scale * products + shift
        if is_matched:
            row = pl.program_id(0) * block + lax.broadcasted_iota(jnp.int32, logits.shape, 0)
            column = lax.broadcasted_iota(jnp.int32, logits.shape, 1)
            same = row == column
            weights = scale / (1.0 + jnp.exp(jnp.where(same, logits, -logits)))
            weights = jnp.where(same, -weights, weights)
        else:
            weights = scale / (1.0 + jnp.exp(-logits))
        added = jnp.dot(weights.astype(jnp.bfloat16), other, preferred_element_type=jnp.float32)
        total = added if total is None else total + added
    if has_raw:
        raw = raw_ref[...]
        radius = radius_of(raw)
        unit = raw / radius
        radial = jnp.sum(unit * total, axis=-1, keepdims=True)
        total = (total - unit * radial) / radius
    out_ref[...] = total


def add_up(scale, shift, own, others, matched, total=None, raw=None, blocks=2):
    rows, width = own.shape
    spec = pl.BlockSpec((rows // blocks, width), lambda i: (i, 0))
    whole = VMEM
    operands = [own, *others] + [x for x in (total, raw) if x is not None]
    specs = [spec] + [whole] * len(others) + [spec] * (len(operands) - 1 - len(others))
    other_rows = sum(x.shape[0] for x in others)
    return pl.pallas_call(
        functools.partial(add_up_kernel, tuple(matched), total is not None, raw is not None),
        grid=(blocks,),
        in_specs=[SMEM, SMEM] + specs,
        out_specs=spec,
        out_shape=jax.ShapeDtypeStruct((rows, width), jnp.float32),
        name="add_up",
        compiler_params=pltpu.CompilerParams(vmem_limit_bytes=32 * MIB),
        cost_estimate=pl.CostEstimate(
            flops=4 * rows * other_rows * width,
            bytes_accessed=sum(x.size * x.dtype.itemsize for x in operands) + 4 * rows * width,
            transcendentals=2 * rows * other_rows,
        ),
    )(scale, shift, *operands)


def passed_along(x, axis, by):
    count = lax.axis_size(axis)
    return lax.ppermute(x, axis, [(i, (i + by) % count) for i in range(count)])


def exchanged(x, bit):
    count = lax.axis_size("blk")
    return lax.ppermute(x, "blk", [(i, i ^ (1 << bit)) for i in range(count)])


def with_partners(bits, visual, caption, text_half, scale, shift):
    add = functools.partial(add_up, scale, shift)
    other_texts = [passed_along(text_half, "group", 1)]
    other_texts += [exchanged(text_half, bit) for bit in reversed(bits)]
    image_half = halves(visual)
    other_images = [passed_along(image_half, "group", -1)]
    other_images += [exchanged(image_half, bit) for bit in reversed(bits)]
    image_sum = add(image_half, [text_half], [True])
    text_sum = add(text_half, [image_half], [True])
    text_z, *text_p = other_texts
    image_z, *image_p = other_images
    image_gradient = add(image_half, other_texts, [False] * 3, image_sum, visual)
    text_gradient = add(text_half, other_images, [False] * 3, text_sum, caption)
    return image_gradient, text_gradient


def on_device(
    visual_encoder_outputs,
    caption_encoder_outputs,
    partner_lookup_grid,
    sharpness_coefficient,
    sigmoid_shift_term,
):
    rounds, peers = partner_lookup_grid.shape
    choices = list(itertools.combinations(range(peers.bit_length() - 1), rounds))
    union = jnp.sum(partner_lookup_grid[:, 0])
    branch = jnp.int32(0)
    for number, bits in enumerate(choices):
        branch = jnp.where(union == sum(1 << bit for bit in bits), jnp.int32(number), branch)
    text_half = halves(caption_encoder_outputs)
    return lax.switch(
        branch,
        [functools.partial(with_partners, bits) for bits in choices],
        visual_encoder_outputs,
        caption_encoder_outputs,
        text_half,
        sharpness_coefficient,
        sigmoid_shift_term,
    )


def solution(mesh):
    placed = (P(("blk", "group"), None), P(("blk", "group"), None), P(), P(), P())
    return jax.shard_map(
        on_device,
        mesh=mesh,
        in_specs=placed,
        out_specs=(P(("blk", "group"), None), P(("blk", "group"), None)),
        check_vma=False,
    )
```

```python
import functools
import itertools

import jax
import jax.numpy as jnp
from jax import lax
from jax.experimental import pallas as pl
from jax.experimental.pallas import tpu as pltpu
from jax.sharding import PartitionSpec as P

epsilon = 1e-06
log2_e = 1.4426950408889634
MIB = 1024 * 1024
VMEM = pl.BlockSpec(memory_space=pltpu.VMEM)
SMEM = pl.BlockSpec(memory_space=pltpu.SMEM)


def inverse_radius(raw):
    return lax.rsqrt(jnp.sum(raw * raw, axis=-1, keepdims=True) + epsilon)


def halves_kernel(raw_ref, half_ref):
    raw = raw_ref[...]
    half_ref[...] = (raw * inverse_radius(raw)).astype(jnp.bfloat16)


def halves(raw, blocks=4):
    rows, width = raw.shape
    spec = pl.BlockSpec((rows // blocks, width), lambda i: (i, 0))
    return pl.pallas_call(
        halves_kernel,
        grid=(blocks,),
        in_specs=[spec],
        out_specs=spec,
        out_shape=jax.ShapeDtypeStruct((rows, width), jnp.bfloat16),
        name="halves",
        cost_estimate=cost([raw], rows, width, 0),
    )(raw)


def choosing_kernel(unions, grid_ref, raw_ref, half_ref, branch_ref):
    halves_kernel(raw_ref, half_ref)
    union = grid_ref[0, 0]
    for number in range(1, grid_ref.shape[0]):
        union = union + grid_ref[number, 0]
    branch = jnp.int32(0)
    for number, each in enumerate(unions):
        branch = jnp.where(union == each, jnp.int32(number), branch)
    branch_ref[0] = branch


def halves_and_branch(raw, grid, unions, blocks=4):
    rows, width = raw.shape
    spec = pl.BlockSpec((rows // blocks, width), lambda i: (i, 0))
    return pl.pallas_call(
        functools.partial(choosing_kernel, unions),
        grid=(blocks,),
        in_specs=[SMEM, spec],
        out_specs=[spec, SMEM],
        out_shape=[
            jax.ShapeDtypeStruct((rows, width), jnp.bfloat16),
            jax.ShapeDtypeStruct((1,), jnp.int32),
        ],
        name="halves_and_branch",
        cost_estimate=cost([raw], rows, width, 0),
    )(grid, raw)


def coupling(own, other, scale, shift, first_row=None):
    products = lax.dot_general(
        own, other, (((1,), (1,)), ((), ())), preferred_element_type=jnp.float32
    )
    powers = products * (-log2_e * scale) - log2_e * shift
    if first_row is None:
        return (scale / (1.0 + jnp.exp2(powers))).astype(jnp.bfloat16)
    row = first_row + lax.broadcasted_iota(jnp.int32, powers.shape, 0)
    same = row == lax.broadcasted_iota(jnp.int32, powers.shape, 1)
    weights = scale / (1.0 + jnp.exp2(jnp.where(same, -powers, powers)))
    return jnp.where(same, -weights, weights).astype(jnp.bfloat16)


def add_up_kernel(matched, has_sum, blocks, scale_ref, shift_ref, own_ref, *refs):
    refs = list(refs)
    other_refs = [refs.pop(0) for _ in matched]
    sum_ref = refs.pop(0) if has_sum else None
    out_ref = refs.pop(0)
    block = own_ref.shape[0] // blocks
    scale, shift = scale_ref[0], shift_ref[0]
    for number in range(blocks):
        rows = pl.ds(number * block, block)
        own = own_ref[rows, :]
        total = sum_ref[rows, :] if has_sum else None
        for other_ref, is_matched in zip(other_refs, matched):
            other = other_ref[...]
            weights = coupling(own, other, scale, shift, number * block if is_matched else None)
            added = jnp.dot(weights, other, preferred_element_type=jnp.float32)
            total = added if total is None else total + added
        out_ref[rows, :] = total


def finish_kernel(has_sum, scale_ref, shift_ref, own_ref, raw_ref, *refs):
    refs = list(refs)
    out_ref = refs.pop()
    sum_ref = refs.pop() if has_sum else None
    block = out_ref.shape[0]
    rows = pl.ds(pl.multiple_of(pl.program_id(0) * block, block), block)
    scale, shift = scale_ref[0], shift_ref[0]
    own = own_ref[rows, :]
    raw = raw_ref[rows, :]
    total = sum_ref[rows, :] if has_sum else None
    for other_ref in refs:
        other = other_ref[...]
        weights = coupling(own, other, scale, shift)
        added = jnp.dot(weights, other, preferred_element_type=jnp.float32)
        total = added if total is None else total + added
    inverse = inverse_radius(raw)
    unit = raw * inverse
    radial = jnp.sum(unit * total, axis=-1, keepdims=True)
    out_ref[...] = (total - unit * radial) * inverse


def cost(operands, rows, width, other_rows):
    return pl.CostEstimate(
        flops=4 * rows * other_rows * width,
        bytes_accessed=sum(x.size * x.dtype.itemsize for x in operands) + 4 * rows * width,
        transcendentals=2 * rows * other_rows,
    )


def add_up(scale, shift, own, others, total=None, matched=False, blocks=1):
    rows, width = own.shape
    operands = [own, *others] + ([] if total is None else [total])
    return pl.pallas_call(
        functools.partial(
            add_up_kernel, (matched,) * len(others), total is not None, blocks
        ),
        in_specs=[SMEM, SMEM] + [VMEM] * len(operands),
        out_specs=VMEM,
        out_shape=jax.ShapeDtypeStruct((rows, width), jnp.float32),
        name="add_up",
        compiler_params=pltpu.CompilerParams(vmem_limit_bytes=24 * MIB),
        cost_estimate=cost(operands, rows, width, sum(x.shape[0] for x in others)),
    )(scale, shift, *operands)


def finish(scale, shift, own, raw, others, total, blocks=2):
    rows, width = own.shape
    operands = [own, raw, *others] + ([] if total is None else [total])
    return pl.pallas_call(
        functools.partial(finish_kernel, total is not None),
        grid=(blocks,),
        in_specs=[SMEM, SMEM] + [VMEM] * len(operands),
        out_specs=pl.BlockSpec((rows // blocks, width), lambda i: (i, 0)),
        out_shape=jax.ShapeDtypeStruct((rows, width), jnp.float32),
        name="finish",
        compiler_params=pltpu.CompilerParams(vmem_limit_bytes=24 * MIB),
        cost_estimate=cost(operands, rows, width, sum(x.shape[0] for x in others)),
    )(scale, shift, *operands)


def passed_along(x, axis, by):
    count = lax.axis_size(axis)
    return lax.ppermute(x, axis, [(i, (i + by) % count) for i in range(count)])


def exchanged(x, bit):
    count = lax.axis_size("blk")
    return lax.ppermute(x, "blk", [(i, i ^ (1 << bit)) for i in range(count)])


def with_partners(bits, visual, caption, text_half, scale, shift):
    texts = [exchanged(text_half, bit) for bit in bits]
    texts += [passed_along(text_half, "group", 1)]
    image_half = halves(visual)
    image_sum = add_up(scale, shift, image_half, [text_half], matched=True)
    text_sum = add_up(scale, shift, text_half, [image_half], matched=True)
    image_half, texts, image_sum, text_sum = lax.optimization_barrier(
        (image_half, texts, image_sum, text_sum)
    )
    images = [exchanged(image_half, bit) for bit in bits]
    images += [passed_along(image_half, "group", -1)]
    image_gradient = finish(scale, shift, image_half, visual, texts, image_sum)
    text_gradient = finish(scale, shift, text_half, caption, images, text_sum)
    return image_gradient, text_gradient


def on_device(
    visual_encoder_outputs,
    caption_encoder_outputs,
    partner_lookup_grid,
    sharpness_coefficient,
    sigmoid_shift_term,
):
    rounds, peers = partner_lookup_grid.shape
    choices = list(itertools.combinations(range(peers.bit_length() - 1), rounds))
    unions = [sum(1 << bit for bit in bits) for bits in choices]
    text_half, branch = halves_and_branch(caption_encoder_outputs, partner_lookup_grid, unions)
    return lax.switch(
        branch[0],
        [functools.partial(with_partners, bits) for bits in choices],
        visual_encoder_outputs,
        caption_encoder_outputs,
        text_half,
        sharpness_coefficient,
        sigmoid_shift_term,
    )


def solution(mesh):
    placed = (P(("blk", "group"), None), P(("blk", "group"), None), P(), P(), P())
    return jax.shard_map(
        on_device,
        mesh=mesh,
        in_specs=placed,
        out_specs=(P(("blk", "group"), None), P(("blk", "group"), None)),
        check_vma=False,
    )
```

```python
import functools
import itertools

import jax
import jax.numpy as jnp
from jax import lax
from jax.experimental import pallas as pl
from jax.experimental.pallas import tpu as pltpu
from jax.sharding import PartitionSpec as P

epsilon = 1e-06
log2_e = 1.4426950408889634
MIB = 1024 * 1024
VMEM = pl.BlockSpec(memory_space=pltpu.VMEM)
SMEM = pl.BlockSpec(memory_space=pltpu.SMEM)
BLOCK = 256


def cost(rows, other_rows, width):
    return pl.CostEstimate(
        flops=4 * rows * max(other_rows, 1) * width,
        bytes_accessed=8 * rows * width,
        transcendentals=2 * rows * other_rows,
    )


def call(body, name, operands, outs, work, smem=2, grid=None, out_specs=None):
    return pl.pallas_call(
        body,
        grid=grid or (),
        in_specs=[SMEM] * smem + [VMEM] * (len(operands) - smem),
        out_specs=out_specs or [VMEM] * len(outs),
        out_shape=[jax.ShapeDtypeStruct(shape, dtype) for shape, dtype in outs],
        name=name,
        compiler_params=pltpu.CompilerParams(vmem_limit_bytes=24 * MIB),
        cost_estimate=cost(*work),
    )(*operands)


def inverse_radius(raw):
    return lax.rsqrt(jnp.sum(raw * raw, axis=-1, keepdims=True) + epsilon)


def halves_kernel(cuts, raw_ref, *half_refs):
    raw = raw_ref[...]
    half = (raw * inverse_radius(raw)).astype(jnp.bfloat16)
    half_refs[0][...] = half
    for half_ref, first, last in zip(half_refs[1:], cuts[:-1], cuts[1:]):
        half_ref[...] = half[first:last]


def halves(raw, cuts):
    rows, width = raw.shape
    counts = [rows] + [last - first for first, last in zip(cuts[:-1], cuts[1:])]
    return call(
        functools.partial(halves_kernel, cuts),
        "halves",
        [raw],
        [((count, width), jnp.bfloat16) for count in counts],
        (rows, 1, width),
        smem=0,
    )


def coupling(own, other, scale, shift, first_row=None):
    products = lax.dot_general(
        own, other, (((1,), (1,)), ((), ())), preferred_element_type=jnp.float32
    )
    powers = products * (-log2_e * scale) - log2_e * shift
    if first_row is not None:
        row = first_row + lax.broadcasted_iota(jnp.int32, powers.shape, 0)
        same = row == lax.broadcasted_iota(jnp.int32, powers.shape, 1)
        powers = jnp.where(same, -powers, powers)
    below = 1.0 + jnp.exp2(powers)
    inverse = pl.reciprocal(below, approx=True)
    weights = scale * (inverse * (2.0 - below * inverse))
    if first_row is not None:
        weights = jnp.where(same, -weights, weights)
    return weights.astype(jnp.bfloat16)


def added(own, other, scale, shift):
    weights = coupling(own, other, scale, shift)
    return jnp.dot(weights, other, preferred_element_type=jnp.float32)


def is_drawn(grid_ref, bit):
    drawn = jnp.bool_(False)
    for number in range(grid_ref.shape[0]):
        drawn = drawn | (grid_ref[number, 0] == (1 << bit))
    return drawn


def row_blocks(rows, body):
    def step(number, carry):
        body(pl.multiple_of(number * BLOCK, BLOCK))
        return carry

    lax.fori_loop(0, rows // BLOCK, step, 0)


def diagonal_kernel(
    cut, scale_ref, shift_ref, raw_ref, text_ref,
    image_ref, both_ref, first_ref, last_ref, image_sum_ref, text_sum_ref, weights_ref,
):
    scale, shift = scale_ref[0], shift_ref[0]
    row_count = raw_ref.shape[0]
    raw = raw_ref[...]
    image_ref[...] = (raw * inverse_radius(raw)).astype(jnp.bfloat16)
    both_ref[:row_count, :] = text_ref[...]
    both_ref[row_count:, :] = image_ref[...]
    first_ref[...] = image_ref[:cut, :]
    last_ref[...] = image_ref[cut:, :]

    def for_images(first):
        rows = pl.ds(first, BLOCK)
        weights = coupling(image_ref[rows, :], text_ref[...], scale, shift, first)
        weights_ref[rows, :] = weights
        image_sum_ref[rows, :] = jnp.dot(
            weights, text_ref[...], preferred_element_type=jnp.float32
        )

    def for_texts(first):
        rows = pl.ds(first, BLOCK)
        text_sum_ref[rows, :] = lax.dot_general(
            weights_ref[:, rows], image_ref[...], (((0,), (0,)), ((), ())),
            preferred_element_type=jnp.float32,
        )

    row_blocks(row_count, for_images)
    for first in range(0, row_count, BLOCK):
        for_texts(first)


def diagonal(scale, shift, raw, text_half, cut):
    rows, width = raw.shape
    half, full = jnp.bfloat16, jnp.float32
    outs = [(rows, half), (2 * rows, half), (cut, half), (rows - cut, half), (rows, full), (rows, full)]
    return pl.pallas_call(
        functools.partial(diagonal_kernel, cut),
        in_specs=[SMEM, SMEM, VMEM, VMEM],
        out_specs=[VMEM] * len(outs),
        out_shape=[jax.ShapeDtypeStruct((count, width), dtype) for count, dtype in outs],
        scratch_shapes=[pltpu.VMEM((rows, rows), jnp.bfloat16)],
        name="diagonal",
        compiler_params=pltpu.CompilerParams(vmem_limit_bytes=24 * MIB),
        cost_estimate=cost(rows, 2 * rows, width),
    )(scale, shift, raw, text_half)


def add_up_kernel(bits, scale_ref, shift_ref, grid_ref, own_ref, sum_ref, *refs):
    other_refs, out_ref = refs[:-1], refs[-1]
    scale, shift = scale_ref[0], shift_ref[0]

    def body(first):
        rows = pl.ds(first, BLOCK)
        own = own_ref[rows, :]
        done = False
        for other_ref, bit in zip(other_refs, bits):
            if bit is None:
                before = out_ref[rows, :] if done else sum_ref[rows, :]
                out_ref[rows, :] = before + added(own, other_ref[...], scale, shift)
                done = True
        if not done:
            out_ref[rows, :] = sum_ref[rows, :]
        for other_ref, bit in zip(other_refs, bits):
            if bit is not None:
                @pl.when(is_drawn(grid_ref, bit))
                def _():
                    out_ref[rows, :] += added(own, other_ref[...], scale, shift)

    row_blocks(own_ref.shape[0], body)


def add_up(scale, shift, grid, own, total, others, bits):
    rows, width = own.shape
    return call(
        functools.partial(add_up_kernel, tuple(bits)),
        "add_up",
        [scale, shift, grid, own, total, *others],
        [((rows, width), jnp.float32)],
        (rows, sum(x.shape[0] for x in others), width),
        smem=3,
    )[0]


def near_kernel(
    scale_ref, shift_ref, image_ref, text_ref, both_ref, image_sum_ref, text_sum_ref,
    image_out_ref, text_out_ref,
):
    scale, shift = scale_ref[0], shift_ref[0]
    row_count = image_ref.shape[0]

    def body(first):
        rows = pl.ds(first, BLOCK)
        texts, images = both_ref[:row_count, :], both_ref[row_count:, :]
        image_out_ref[rows, :] = image_sum_ref[rows, :] + added(
            image_ref[rows, :], texts, scale, shift
        )
        text_out_ref[rows, :] = text_sum_ref[rows, :] + added(
            text_ref[rows, :], images, scale, shift
        )

    row_blocks(row_count, body)


def with_near(bit, scale, shift, image_half, text_half, both, image_sum, text_sum):
    rows, width = image_half.shape
    return tuple(call(
        near_kernel,
        "add_near",
        [scale, shift, image_half, text_half, exchanged(both, bit), image_sum, text_sum],
        [((rows, width), jnp.float32)] * 2,
        (rows, 2 * rows, width),
    ))


def finish_kernel(bits, scale_ref, shift_ref, grid_ref, own_ref, raw_ref, sum_ref, *refs):
    other_refs, out_ref = refs[:-1], refs[-1]
    block = out_ref.shape[0]
    rows = pl.ds(pl.multiple_of(pl.program_id(0) * block, block), block)
    scale, shift = scale_ref[0], shift_ref[0]
    own = own_ref[rows, :]
    total = sum_ref[rows, :]
    for other_ref, bit in zip(other_refs, bits):
        if bit is None:
            total = total + added(own, other_ref[...], scale, shift)
    out_ref[...] = total
    for other_ref, bit in zip(other_refs, bits):
        if bit is not None:
            @pl.when(is_drawn(grid_ref, bit))
            def _():
                out_ref[...] += added(own, other_ref[...], scale, shift)
    total = out_ref[...]
    raw = raw_ref[rows, :]
    inverse = inverse_radius(raw)
    unit = raw * inverse
    radial = jnp.sum(unit * total, axis=-1, keepdims=True)
    out_ref[...] = (total - unit * radial) * inverse


def finish(scale, shift, grid, own, raw, total, others, bits):
    rows, width = own.shape
    return call(
        functools.partial(finish_kernel, tuple(bits)),
        "finish",
        [scale, shift, grid, own, raw, total, *others],
        [((rows, width), jnp.float32)],
        (rows, sum(x.shape[0] for x in others), width),
        smem=3,
        grid=(rows // BLOCK,),
        out_specs=[pl.BlockSpec((BLOCK, width), lambda i: (i, 0))],
    )[0]


def passed_along(x, axis, by):
    count = lax.axis_size(axis)
    return lax.ppermute(x, axis, [(i, (i + by) % count) for i in range(count)])


def exchanged(x, bit):
    count = lax.axis_size("blk")
    return lax.ppermute(x, "blk", [(i, i ^ (1 << bit)) for i in range(count)])


def with_partners(bits, visual, caption, grid, scale, shift):
    rows = visual.shape[0]
    cut = rows * 3 // 4
    cuts = (0, cut, rows)
    near, far = [bit for bit in bits if bit == 0], [bit for bit in bits if bit != 0]
    text_half, text_first, text_last = halves(caption, cuts)
    far_texts = [exchanged(text_half, bit) for bit in far]
    text_z_last = passed_along(text_last, "group", 1)
    text_z_first = passed_along(text_first, "group", 1)
    image_half, both, image_first, image_last, image_sum, text_sum = diagonal(
        scale, shift, visual, text_half, cut
    )
    for bit in near:
        image_sum, text_sum = lax.cond(
            jnp.any(grid[:, 0] == (1 << bit)),
            functools.partial(with_near, bit),
            lambda scale, shift, image_half, text_half, both, *sums: sums,
            scale, shift, image_half, text_half, both, image_sum, text_sum,
        )
    image_first, image_sum, text_sum, text_z_first = lax.optimization_barrier(
        (image_first, image_sum, text_sum, text_z_first)
    )
    image_z_first = passed_along(image_first, "group", -1)
    image_first, far_texts, text_z_last = lax.optimization_barrier(
        (image_first, far_texts, text_z_last)
    )
    far_images_first = [exchanged(image_first, bit) for bit in far]
    image_gradient = finish(
        scale, shift, grid, image_half, visual, image_sum,
        [text_z_first, text_z_last, *far_texts], [None, None, *far],
    )
    image_last, image_gradient = lax.optimization_barrier((image_last, image_gradient))
    far_images_last = [exchanged(image_last, bit) for bit in far]
    image_z_last = passed_along(image_last, "group", -1)
    text_sum = add_up(
        scale, shift, grid, text_half, text_sum,
        [image_z_first, *far_images_first], [None, *far],
    )
    text_gradient = finish(
        scale, shift, grid, text_half, caption, text_sum,
        [image_z_last, *far_images_last], [None, *far],
    )
    return image_gradient, text_gradient


def on_device(
    visual_encoder_outputs,
    caption_encoder_outputs,
    partner_lookup_grid,
    sharpness_coefficient,
    sigmoid_shift_term,
):
    rounds, peers = partner_lookup_grid.shape
    bits = range(peers.bit_length() - 1)
    operands = (
        visual_encoder_outputs,
        caption_encoder_outputs,
        partner_lookup_grid,
        sharpness_coefficient,
        sigmoid_shift_term,
    )
    if len(bits) <= rounds + 1:
        return with_partners(bits, *operands)
    choices = list(itertools.combinations(bits, rounds))
    union = jnp.sum(partner_lookup_grid[:, 0])
    branch = jnp.int32(0)
    for number, choice in enumerate(choices):
        branch = jnp.where(union == sum(1 << bit for bit in choice), jnp.int32(number), branch)
    return lax.switch(
        branch, [functools.partial(with_partners, choice) for choice in choices], *operands
    )


def solution(mesh):
    placed = (P(("blk", "group"), None), P(("blk", "group"), None), P(), P(), P())
    return jax.shard_map(
        on_device,
        mesh=mesh,
        in_specs=placed,
        out_specs=(P(("blk", "group"), None), P(("blk", "group"), None)),
        check_vma=False,
    )
```

```python
import functools
import itertools

import jax
import jax.numpy as jnp
from jax import lax
from jax.experimental import pallas as pl
from jax.experimental.pallas import tpu as pltpu
from jax.sharding import PartitionSpec as P

epsilon = 1e-06
log2_e = 1.4426950408889634
MIB = 1024 * 1024
VMEM = pl.BlockSpec(memory_space=pltpu.VMEM)
SMEM = pl.BlockSpec(memory_space=pltpu.SMEM)
BLOCK, STRIP, COLUMNS, SMALL = 256, 256, 384, 32


def cost(rows, other_rows, width):
    return pl.CostEstimate(
        flops=4 * rows * max(other_rows, 1) * width,
        bytes_accessed=8 * rows * width,
        transcendentals=2 * rows * other_rows,
    )


def call(body, name, operands, outs, work, smem=2, grid=None, out_specs=None, scratch=()):
    return pl.pallas_call(
        body,
        grid=grid or (),
        in_specs=[SMEM] * smem + [VMEM] * (len(operands) - smem),
        out_specs=out_specs or [VMEM] * len(outs),
        out_shape=[jax.ShapeDtypeStruct(shape, dtype) for shape, dtype in outs],
        scratch_shapes=list(scratch),
        name=name,
        compiler_params=pltpu.CompilerParams(vmem_limit_bytes=24 * MIB),
        cost_estimate=cost(*work),
    )(*operands)


def inverse_radius(raw):
    return lax.rsqrt(jnp.sum(raw * raw, axis=-1, keepdims=True) + epsilon)


def strips(count, size):
    return [(first, min(first + size, count)) for first in range(0, count, size)]


def row_blocks(rows, block, body, unroll=1):
    def step(number, carry):
        body(pl.ds(pl.multiple_of(number * block, block), block))
        return carry

    lax.fori_loop(0, rows // block, step, 0, unroll=unroll)


def normalize_rows(raw_ref, half_ref):
    def body(rows):
        raw = raw_ref[rows, :]
        half_ref[rows, :] = (raw * inverse_radius(raw)).astype(jnp.bfloat16)

    row_blocks(raw_ref.shape[0], SMALL, body, 2)


def halves(raw):
    rows, width = raw.shape
    return call(
        normalize_rows, "halves", [raw], [((rows, width), jnp.bfloat16)], (rows, 1, width), smem=0
    )[0]


def coupling(own, other, scale, shift, places=None):
    products = lax.dot_general(
        own, other, (((1,), (1,)), ((), ())), preferred_element_type=jnp.float32
    )
    powers = products * (-log2_e * scale) - log2_e * shift
    if places is not None:
        row = places[0] + lax.broadcasted_iota(jnp.int32, powers.shape, 0)
        column = places[1] + lax.broadcasted_iota(jnp.int32, powers.shape, 1)
        same = row == column
        powers = jnp.where(same, -powers, powers)
    below = 1.0 + jnp.exp2(powers)
    inverse = pl.reciprocal(below, approx=True)
    weights = scale * (inverse * (2.0 - below * inverse))
    if places is not None:
        weights = jnp.where(same, -weights, weights)
    return weights.astype(jnp.bfloat16)


def weigh(own, other_ref, scale, shift, weights_ref, first_row=None):
    for first, last in strips(other_ref.shape[0], STRIP):
        places = None if first_row is None else (first_row, first)
        weights_ref[:, first:last] = coupling(own, other_ref[first:last, :], scale, shift, places)


def add_products(before_ref, before_rows, weights_ref, other_ref, out_ref, out_rows):
    count, width = other_ref.shape
    weights = weights_ref[:, :count]
    for first, last in strips(width, COLUMNS):
        total = jnp.dot(weights, other_ref[:, first:last], preferred_element_type=jnp.float32)
        if before_ref is not None:
            total = before_ref[before_rows, first:last] + total
        out_ref[out_rows, first:last] = total


def is_drawn(grid_ref, bit):
    drawn = jnp.bool_(False)
    for number in range(grid_ref.shape[0]):
        drawn = drawn | (grid_ref[number, 0] == (1 << bit))
    return drawn


def diagonal_kernel(
    cut, scale_ref, shift_ref, raw_ref, text_ref,
    image_ref, both_ref, first_ref, last_ref, image_sum_ref, text_sum_ref, weights_ref,
):
    scale, shift = scale_ref[0], shift_ref[0]
    row_count, width = raw_ref.shape
    normalize_rows(raw_ref, image_ref)
    both_ref[:row_count, :] = text_ref[...]
    both_ref[row_count:, :] = image_ref[...]
    first_ref[...] = image_ref[:cut, :]
    last_ref[...] = image_ref[cut:, :]

    def for_images(rows):
        weigh(image_ref[rows, :], text_ref, scale, shift, weights_ref.at[rows, :], rows.start)
        add_products(None, None, weights_ref.at[rows, :], text_ref, image_sum_ref, rows)

    row_blocks(row_count, BLOCK, for_images)
    for first, last in strips(row_count, STRIP):
        for left, right in strips(width, COLUMNS):
            text_sum_ref[first:last, left:right] = lax.dot_general(
                weights_ref[:, first:last], image_ref[:, left:right], (((0,), (0,)), ((), ())),
                preferred_element_type=jnp.float32,
            )


def diagonal(scale, shift, raw, text_half, cut):
    rows, width = raw.shape
    half, full = jnp.bfloat16, jnp.float32
    outs = [(rows, half), (2 * rows, half), (cut, half), (rows - cut, half), (rows, full), (rows, full)]
    return call(
        functools.partial(diagonal_kernel, cut),
        "diagonal",
        [scale, shift, raw, text_half],
        [((count, width), dtype) for count, dtype in outs],
        (rows, 2 * rows, width),
        scratch=[pltpu.VMEM((rows, rows), jnp.bfloat16)],
    )


def near_kernel(
    scale_ref, shift_ref, image_ref, text_ref, both_ref, image_sum_ref, text_sum_ref,
    image_out_ref, text_out_ref, weights_ref,
):
    scale, shift = scale_ref[0], shift_ref[0]
    row_count = image_ref.shape[0]

    def body(rows):
        for own_ref, other_ref, sum_ref, out_ref in (
            (image_ref, both_ref.at[:row_count, :], image_sum_ref, image_out_ref),
            (text_ref, both_ref.at[row_count:, :], text_sum_ref, text_out_ref),
        ):
            weigh(own_ref[rows, :], other_ref, scale, shift, weights_ref)
            add_products(sum_ref, rows, weights_ref, other_ref, out_ref, rows)

    row_blocks(row_count, BLOCK, body)


def with_near(bit, scale, shift, image_half, text_half, both, image_sum, text_sum):
    rows, width = image_half.shape
    return tuple(call(
        near_kernel,
        "add_near",
        [scale, shift, image_half, text_half, exchanged(both, bit), image_sum, text_sum],
        [((rows, width), jnp.float32)] * 2,
        (rows, 2 * rows, width),
        scratch=[pltpu.VMEM((BLOCK, rows), jnp.bfloat16)],
    ))


def add_pairs(bits, other_refs, own, sum_ref, rows, out_ref, out_rows, weights_ref, scale, shift, grid_ref):
    for number, (other_ref, bit) in enumerate(zip(other_refs, bits)):
        def add(before_ref, before_rows):
            weigh(own, other_ref, scale, shift, weights_ref)
            add_products(before_ref, before_rows, weights_ref, other_ref, out_ref, out_rows)

        if bit is None:
            add(*((sum_ref, rows) if number == 0 else (out_ref, out_rows)))
        else:
            pl.when(is_drawn(grid_ref, bit))(functools.partial(add, out_ref, out_rows))


def add_up_kernel(bits, scale_ref, shift_ref, grid_ref, own_ref, sum_ref, *refs):
    *other_refs, out_ref, weights_ref = refs
    scale, shift = scale_ref[0], shift_ref[0]

    def body(rows):
        add_pairs(
            bits, other_refs, own_ref[rows, :], sum_ref, rows, out_ref, rows, weights_ref,
            scale, shift, grid_ref,
        )

    row_blocks(own_ref.shape[0], BLOCK, body)


def add_up(scale, shift, grid, own, total, others, bits):
    rows, width = own.shape
    return call(
        functools.partial(add_up_kernel, tuple(bits)),
        "add_up",
        [scale, shift, grid, own, total, *others],
        [((rows, width), jnp.float32)],
        (rows, sum(x.shape[0] for x in others), width),
        smem=3,
        scratch=[pltpu.VMEM((BLOCK, rows), jnp.bfloat16)],
    )[0]


def finish_kernel(bits, scale_ref, shift_ref, grid_ref, own_ref, raw_ref, sum_ref, *refs):
    *other_refs, out_ref, weights_ref = refs
    block = out_ref.shape[0]
    start = pl.multiple_of(pl.program_id(0) * block, block)
    rows = pl.ds(start, block)
    add_pairs(
        bits, other_refs, own_ref[rows, :], sum_ref, rows, out_ref, pl.ds(0, block), weights_ref,
        scale_ref[0], shift_ref[0], grid_ref,
    )

    def project(rows):
        raw = raw_ref[pl.ds(start + rows.start, SMALL), :]
        total = out_ref[rows, :]
        inverse = inverse_radius(raw)
        unit = raw * inverse
        radial = jnp.sum(unit * total, axis=-1, keepdims=True)
        out_ref[rows, :] = (total - unit * radial) * inverse

    row_blocks(block, SMALL, project, 2)


def finish(scale, shift, grid, own, raw, total, others, bits, block):
    rows, width = own.shape
    return call(
        functools.partial(finish_kernel, tuple(bits)),
        "finish",
        [scale, shift, grid, own, raw, total, *others],
        [((rows, width), jnp.float32)],
        (rows, sum(x.shape[0] for x in others), width),
        smem=3,
        grid=(rows // block,),
        out_specs=[pl.BlockSpec((block, width), lambda i: (i, 0))],
        scratch=[pltpu.VMEM((block, rows), jnp.bfloat16)],
    )[0]


def passed_along(x, axis, by):
    count = lax.axis_size(axis)
    return lax.ppermute(x, axis, [(i, (i + by) % count) for i in range(count)])


def exchanged(x, bit):
    count = lax.axis_size("blk")
    return lax.ppermute(x, "blk", [(i, i ^ (1 << bit)) for i in range(count)])


def with_partners(bits, visual, caption, grid, scale, shift):
    rows = visual.shape[0]
    cut = rows * 3 // 4
    near, far = [bit for bit in bits if bit == 0], [bit for bit in bits if bit != 0]
    text_half = halves(caption)
    text_z = passed_along(text_half, "group", 1)
    far_texts = [exchanged(text_half, bit) for bit in far]
    image_half, both, image_first, image_last, image_sum, text_sum = diagonal(
        scale, shift, visual, text_half, cut
    )
    for bit in near:
        image_sum, text_sum = lax.cond(
            jnp.any(grid[:, 0] == (1 << bit)),
            functools.partial(with_near, bit),
            lambda scale, shift, image_half, text_half, both, *sums: sums,
            scale, shift, image_half, text_half, both, image_sum, text_sum,
        )
    image_first, image_last, image_sum, text_sum, text_z = lax.optimization_barrier(
        (image_first, image_last, image_sum, text_sum, text_z)
    )
    image_z_first = passed_along(image_first, "group", -1)
    image_first, image_last, far_texts = lax.optimization_barrier(
        (image_first, image_last, far_texts)
    )
    far_images_first = [exchanged(image_first, bit) for bit in far]
    image_gradient = finish(
        scale, shift, grid, image_half, visual, image_sum,
        [text_z, *far_texts], [None, *far], BLOCK,
    )
    image_last, image_gradient = lax.optimization_barrier((image_last, image_gradient))
    far_images_last = [exchanged(image_last, bit) for bit in far]
    image_z_last = passed_along(image_last, "group", -1)
    text_sum = add_up(
        scale, shift, grid, text_half, text_sum,
        [image_z_first, *far_images_first], [None, *far],
    )
    text_gradient = finish(
        scale, shift, grid, text_half, caption, text_sum,
        [image_z_last, *far_images_last], [None, *far], BLOCK // 2,
    )
    return image_gradient, text_gradient


def on_device(
    visual_encoder_outputs,
    caption_encoder_outputs,
    partner_lookup_grid,
    sharpness_coefficient,
    sigmoid_shift_term,
):
    rounds, peers = partner_lookup_grid.shape
    bits = range(peers.bit_length() - 1)
    operands = (
        visual_encoder_outputs,
        caption_encoder_outputs,
        partner_lookup_grid,
        sharpness_coefficient,
        sigmoid_shift_term,
    )
    if len(bits) <= rounds + 1:
        return with_partners(bits, *operands)
    choices = list(itertools.combinations(bits, rounds))
    union = jnp.sum(partner_lookup_grid[:, 0])
    branch = jnp.int32(0)
    for number, choice in enumerate(choices):
        branch = jnp.where(union == sum(1 << bit for bit in choice), jnp.int32(number), branch)
    return lax.switch(
        branch, [functools.partial(with_partners, choice) for choice in choices], *operands
    )


def solution(mesh):
    placed = (P(("blk", "group"), None), P(("blk", "group"), None), P(), P(), P())
    return jax.shard_map(
        on_device,
        mesh=mesh,
        in_specs=placed,
        out_specs=(P(("blk", "group"), None), P(("blk", "group"), None)),
        check_vma=False,
    )
```

```python
import functools
import itertools

import jax
import jax.numpy as jnp
from jax import lax
from jax.experimental import pallas as pl
from jax.experimental.pallas import tpu as pltpu
from jax.sharding import PartitionSpec as P

epsilon = 1e-06
log2_e = 1.4426950408889634
MIB = 1024 * 1024
VMEM = pl.BlockSpec(memory_space=pltpu.VMEM)
SMEM = pl.BlockSpec(memory_space=pltpu.SMEM)
BLOCK, STRIP, COLUMNS = 256, 256, 384


def cost(rows, other_rows, width):
    return pl.CostEstimate(
        flops=4 * rows * max(other_rows, 1) * width,
        bytes_accessed=8 * rows * width,
        transcendentals=2 * rows * other_rows,
    )


def call(body, name, operands, outs, work, smem=2, grid=None, out_specs=None, scratch=()):
    return pl.pallas_call(
        body,
        grid=grid or (),
        in_specs=[SMEM] * smem + [VMEM] * (len(operands) - smem),
        out_specs=out_specs or [VMEM] * len(outs),
        out_shape=[jax.ShapeDtypeStruct(shape, dtype) for shape, dtype in outs],
        scratch_shapes=list(scratch),
        name=name,
        compiler_params=pltpu.CompilerParams(vmem_limit_bytes=24 * MIB),
        cost_estimate=cost(*work),
    )(*operands)


def strips(count, size):
    return [(first, min(first + size, count)) for first in range(0, count, size)]


def normalized(raw):
    total = jnp.sum(raw * raw, axis=-1, keepdims=True)
    return (raw * lax.rsqrt(total + epsilon)).astype(jnp.bfloat16)


def coupling(own, other, scale, factor, shift, places=None):
    products = lax.dot_general(
        own, other, (((1,), (1,)), ((), ())), preferred_element_type=jnp.float32
    )
    powers = products * (-log2_e * scale) - log2_e * shift
    if places is not None:
        row = places[0] + lax.broadcasted_iota(jnp.int32, powers.shape, 0)
        column = places[1] + lax.broadcasted_iota(jnp.int32, powers.shape, 1)
        same = row == column
        powers = jnp.where(same, -powers, powers)
    below = 1.0 + jnp.exp2(powers)
    inverse = pl.reciprocal(below, approx=True)
    weights = factor * (inverse * (2.0 - below * inverse))
    if places is not None:
        weights = jnp.where(same, -weights, weights)
    return weights.astype(jnp.bfloat16)


def is_drawn(grid_ref, bit):
    drawn = jnp.bool_(False)
    for number in range(grid_ref.shape[0]):
        drawn = drawn | (grid_ref[number, 0] == (1 << bit))
    return drawn


def add_pairs(scales, shift, own_ref, rows, others, before_ref, out_ref, weights_ref, matched=False):
    first, block = rows
    rows = slice(first, first + block)
    own = own_ref[rows, :]
    places, left = [], 0
    for (scale, factor), other_ref in zip(scales, others):
        count, width = other_ref.shape
        for top, bottom in strips(count, STRIP):
            weights_ref[rows, left + top : left + bottom] = coupling(
                own, other_ref[top:bottom, :], scale, factor, shift, (first, top) if matched else None
            )
        places.append(slice(left, left + count))
        left += count
    for top, bottom in strips(width, COLUMNS):
        total = None if before_ref is None else before_ref[rows, top:bottom]
        for place, other_ref in zip(places, others):
            added = jnp.dot(
                weights_ref[rows, place], other_ref[:, top:bottom], preferred_element_type=jnp.float32
            )
            total = added if total is None else total + added
        out_ref[rows, top:bottom] = total


def blocks_of(count):
    return [(first, min(BLOCK, count - first)) for first in range(0, count, BLOCK)]


def scales_of(bits, scale_ref, grid_ref):
    scale = scale_ref[0]
    return [
        (scale, scale if bit is None else jnp.where(is_drawn(grid_ref, bit), scale, 0.0))
        for bit in bits
    ]


def diagonal_kernel(scale_ref, shift_ref, image_ref, text_ref, image_sum_ref, text_sum_ref, weights_ref):
    scale, shift = scale_ref[0], shift_ref[0]
    row_count, width = image_ref.shape
    for rows in blocks_of(row_count):
        add_pairs(
            [(scale, scale)], shift, image_ref, rows, [text_ref], None, image_sum_ref, weights_ref, True
        )
    for first, last in strips(row_count, STRIP):
        for left, right in strips(width, COLUMNS):
            text_sum_ref[first:last, left:right] = lax.dot_general(
                weights_ref[:, first:last], image_ref[:, left:right], (((0,), (0,)), ((), ())),
                preferred_element_type=jnp.float32,
            )


def diagonal(scale, shift, image_half, text_half):
    rows, width = image_half.shape
    return call(
        diagonal_kernel,
        "diagonal",
        [scale, shift, image_half, text_half],
        [((rows, width), jnp.float32)] * 2,
        (rows, 2 * rows, width),
        scratch=[pltpu.VMEM((rows, rows), jnp.bfloat16)],
    )


def near_kernel(
    scale_ref, shift_ref, image_ref, text_ref, both_ref, image_sum_ref, text_sum_ref,
    image_out_ref, text_out_ref, weights_ref,
):
    scales, shift = [(scale_ref[0], scale_ref[0])], shift_ref[0]
    row_count = image_ref.shape[0]
    texts_ref, images_ref = both_ref.at[:row_count, :], both_ref.at[row_count:, :]
    for rows in blocks_of(row_count):
        add_pairs(
            scales, shift, image_ref, rows, [texts_ref], image_sum_ref, image_out_ref, weights_ref
        )
    for rows in blocks_of(row_count):
        add_pairs(
            scales, shift, text_ref, rows, [images_ref], text_sum_ref, text_out_ref, weights_ref
        )


def with_near(bit, scale, shift, image_half, text_half):
    rows, width = image_half.shape
    both = exchanged(jnp.concatenate([text_half, image_half]), bit)
    image_sum, text_sum = diagonal(scale, shift, image_half, text_half)
    return tuple(call(
        near_kernel,
        "add_near",
        [scale, shift, image_half, text_half, both, image_sum, text_sum],
        [((rows, width), jnp.float32)] * 2,
        (rows, 2 * rows, width),
        scratch=[pltpu.VMEM((rows, rows), jnp.bfloat16)],
    ))


def without_near(scale, shift, image_half, text_half):
    return tuple(diagonal(scale, shift, image_half, text_half))


def add_up_kernel(bits, scale_ref, shift_ref, grid_ref, own_ref, sum_ref, *refs):
    *other_refs, out_ref, weights_ref = refs
    scales = scales_of(bits, scale_ref, grid_ref)
    for rows in blocks_of(own_ref.shape[0]):
        add_pairs(scales, shift_ref[0], own_ref, rows, other_refs, sum_ref, out_ref, weights_ref)


def add_up(scale, shift, grid, own, total, others, bits):
    rows, width = own.shape
    count = sum(x.shape[0] for x in others)
    return call(
        functools.partial(add_up_kernel, tuple(bits)),
        "add_up",
        [scale, shift, grid, own, total, *others],
        [((rows, width), jnp.float32)],
        (rows, count, width),
        smem=3,
        scratch=[pltpu.VMEM((rows, count), jnp.bfloat16)],
    )[0]


def finish_kernel(bits, scale_ref, shift_ref, grid_ref, own_ref, raw_ref, sum_ref, *refs):
    *other_refs, out_ref, weights_ref, total_ref, sems = refs
    scales = scales_of(bits, scale_ref, grid_ref)
    copies = []
    for number, (first, block) in enumerate(blocks_of(own_ref.shape[0])):
        add_pairs(
            scales, shift_ref[0], own_ref, (first, block), other_refs, sum_ref, total_ref, weights_ref
        )
        rows = pl.ds(first, block)
        raw, total = raw_ref[rows, :], total_ref[rows, :]
        inverse = lax.rsqrt(jnp.sum(raw * raw, axis=-1, keepdims=True) + epsilon)
        unit = raw * inverse
        radial = jnp.sum(unit * total, axis=-1, keepdims=True)
        total_ref[rows, :] = (total - unit * radial) * inverse
        copy = pltpu.make_async_copy(total_ref.at[rows, :], out_ref.at[rows, :], sems.at[number])
        copy.start()
        copies.append(copy)
    for copy in copies:
        copy.wait()


def finish(scale, shift, grid, own, raw, total, others, bits):
    rows, width = own.shape
    count = sum(x.shape[0] for x in others)
    return call(
        functools.partial(finish_kernel, tuple(bits)),
        "finish",
        [scale, shift, grid, own, raw, total, *others],
        [((rows, width), jnp.float32)],
        (rows, count, width),
        smem=3,
        out_specs=[pl.BlockSpec(memory_space=pl.ANY)],
        scratch=[
            pltpu.VMEM((rows, count), jnp.bfloat16),
            pltpu.VMEM((rows, width), jnp.float32),
            pltpu.SemaphoreType.DMA((len(blocks_of(rows)),)),
        ],
    )[0]


def passed_along(x, axis, by):
    count = lax.axis_size(axis)
    return lax.ppermute(x, axis, [(i, (i + by) % count) for i in range(count)])


def exchanged(x, bit):
    count = lax.axis_size("blk")
    return lax.ppermute(x, "blk", [(i, i ^ (1 << bit)) for i in range(count)])


def with_partners(bits, visual, caption, grid, scale, shift):
    cut = visual.shape[0] * 3 // 4
    near, far = [bit for bit in bits if bit == 0], [bit for bit in bits if bit != 0]
    text_half = normalized(caption)
    text_z = passed_along(text_half, "group", 1)
    far_texts = [exchanged(text_half, bit) for bit in far]
    image_half = normalized(visual)
    operands = (scale, shift, image_half, text_half)
    if near:
        image_sum, text_sum = lax.cond(
            jnp.any(grid[:, 0] == (1 << near[0])),
            functools.partial(with_near, near[0]),
            without_near,
            *operands,
        )
    else:
        image_sum, text_sum = without_near(*operands)
    image_first, image_last = image_half[:cut], image_half[cut:]
    image_first, image_last, text_z, image_sum, text_sum = lax.optimization_barrier(
        (image_first, image_last, text_z, image_sum, text_sum)
    )
    image_z_first = passed_along(image_first, "group", -1)
    image_z_last = passed_along(image_last, "group", -1)
    image_first, image_last, far_texts = lax.optimization_barrier(
        (image_first, image_last, far_texts)
    )
    far_images_first = [exchanged(image_first, bit) for bit in far]
    image_gradient = finish(
        scale, shift, grid, image_half, visual, image_sum, [*far_texts, text_z], [*far, None]
    )
    text_sum, image_last, image_gradient = lax.optimization_barrier(
        (text_sum, image_last, image_gradient)
    )
    far_images_last = [exchanged(image_last, bit) for bit in far[:1]]
    image_last, image_z_first = lax.optimization_barrier((image_last, image_z_first))
    far_images_last += [exchanged(image_last, bit) for bit in far[1:]]
    text_sum = add_up(
        scale, shift, grid, text_half, text_sum, [*far_images_first, image_z_first], [*far, None]
    )
    text_gradient = finish(
        scale, shift, grid, text_half, caption, text_sum,
        [*far_images_last, image_z_last], [*far, None],
    )
    return image_gradient, text_gradient


def on_device(
    visual_encoder_outputs,
    caption_encoder_outputs,
    partner_lookup_grid,
    sharpness_coefficient,
    sigmoid_shift_term,
):
    rounds, peers = partner_lookup_grid.shape
    bits = range(peers.bit_length() - 1)
    operands = (
        visual_encoder_outputs,
        caption_encoder_outputs,
        partner_lookup_grid,
        sharpness_coefficient,
        sigmoid_shift_term,
    )
    if len(bits) <= rounds + 1:
        return with_partners(bits, *operands)
    choices = list(itertools.combinations(bits, rounds))
    union = jnp.sum(partner_lookup_grid[:, 0])
    branch = jnp.int32(0)
    for number, choice in enumerate(choices):
        branch = jnp.where(union == sum(1 << bit for bit in choice), jnp.int32(number), branch)
    return lax.switch(
        branch, [functools.partial(with_partners, choice) for choice in choices], *operands
    )


def solution(mesh):
    placed = (P(("blk", "group"), None), P(("blk", "group"), None), P(), P(), P())
    return jax.shard_map(
        on_device,
        mesh=mesh,
        in_specs=placed,
        out_specs=(P(("blk", "group"), None), P(("blk", "group"), None)),
        check_vma=False,
    )
```

```python
import functools
import itertools

import jax
import jax.numpy as jnp
from jax import lax
from jax.experimental import pallas as pl
from jax.experimental.pallas import tpu as pltpu
from jax.sharding import PartitionSpec as P

epsilon = 1e-06
log2_e = 1.4426950408889634
MIB = 1024 * 1024
VMEM = pl.BlockSpec(memory_space=pltpu.VMEM)
SMEM = pl.BlockSpec(memory_space=pltpu.SMEM)
BLOCK, STRIP, COLUMNS = 256, 256, 384


def cost(rows, other_rows, width):
    return pl.CostEstimate(
        flops=4 * rows * max(other_rows, 1) * width,
        bytes_accessed=8 * rows * width,
        transcendentals=2 * rows * other_rows,
    )


def call(body, name, operands, outs, work, smem=2, grid=None, out_specs=None, scratch=()):
    return pl.pallas_call(
        body,
        grid=grid or (),
        in_specs=[SMEM] * smem + [VMEM] * (len(operands) - smem),
        out_specs=out_specs or [VMEM] * len(outs),
        out_shape=[jax.ShapeDtypeStruct(shape, dtype) for shape, dtype in outs],
        scratch_shapes=list(scratch),
        name=name,
        compiler_params=pltpu.CompilerParams(vmem_limit_bytes=24 * MIB),
        cost_estimate=cost(*work),
    )(*operands)


def strips(count, size):
    return [(first, min(first + size, count)) for first in range(0, count, size)]


def normalized(raw):
    total = jnp.sum(raw * raw, axis=-1, keepdims=True)
    return (raw * lax.rsqrt(total + epsilon)).astype(jnp.bfloat16)


def coupling(own, other, scale, factor, shift, places=None):
    products = lax.dot_general(
        own, other, (((1,), (1,)), ((), ())), preferred_element_type=jnp.float32
    )
    powers = products * (-log2_e * scale) - log2_e * shift
    if places is not None:
        row = places[0] + lax.broadcasted_iota(jnp.int32, powers.shape, 0)
        column = places[1] + lax.broadcasted_iota(jnp.int32, powers.shape, 1)
        same = row == column
        powers = jnp.where(same, -powers, powers)
    below = 1.0 + jnp.exp2(powers)
    inverse = pl.reciprocal(below, approx=True)
    weights = factor * (inverse * (2.0 - below * inverse))
    if places is not None:
        weights = jnp.where(same, -weights, weights)
    return weights.astype(jnp.bfloat16)


def is_drawn(grid_ref, bit):
    drawn = jnp.bool_(False)
    for number in range(grid_ref.shape[0]):
        drawn = drawn | (grid_ref[number, 0] == (1 << bit))
    return drawn


def add_pairs(scales, shift, own_ref, rows, others, before_ref, out_ref, weights_ref, matched=False):
    first, block = rows
    rows = slice(first, first + block)
    own = own_ref[rows, :]
    places, left = [], 0
    for (scale, factor), other_ref in zip(scales, others):
        count, width = other_ref.shape
        for top, bottom in strips(count, STRIP):
            weights_ref[rows, left + top : left + bottom] = coupling(
                own, other_ref[top:bottom, :], scale, factor, shift, (first, top) if matched else None
            )
        places.append(slice(left, left + count))
        left += count
    for top, bottom in strips(width, COLUMNS):
        total = None if before_ref is None else before_ref[rows, top:bottom]
        for place, other_ref in zip(places, others):
            added = jnp.dot(
                weights_ref[rows, place], other_ref[:, top:bottom], preferred_element_type=jnp.float32
            )
            total = added if total is None else total + added
        out_ref[rows, top:bottom] = total


def blocks_of(count):
    return [(first, min(BLOCK, count - first)) for first in range(0, count, BLOCK)]


def scales_of(bits, scale_ref, grid_ref):
    scale = scale_ref[0]
    return [
        (scale, scale if bit is None else jnp.where(is_drawn(grid_ref, bit), scale, 0.0))
        for bit in bits
    ]


def diagonal_kernel(scale_ref, shift_ref, image_ref, text_ref, image_sum_ref, text_sum_ref, weights_ref):
    scale, shift = scale_ref[0], shift_ref[0]
    row_count, width = image_ref.shape
    for rows in blocks_of(row_count):
        add_pairs(
            [(scale, scale)], shift, image_ref, rows, [text_ref], None, image_sum_ref, weights_ref, True
        )
    for first, last in strips(row_count, STRIP):
        for left, right in strips(width, COLUMNS):
            text_sum_ref[first:last, left:right] = lax.dot_general(
                weights_ref[:, first:last], image_ref[:, left:right], (((0,), (0,)), ((), ())),
                preferred_element_type=jnp.float32,
            )


def diagonal(scale, shift, image_half, text_half):
    rows, width = image_half.shape
    return call(
        diagonal_kernel,
        "diagonal",
        [scale, shift, image_half, text_half],
        [((rows, width), jnp.float32)] * 2,
        (rows, 2 * rows, width),
        scratch=[pltpu.VMEM((rows, rows), jnp.bfloat16)],
    )


def near_kernel(
    bit, scale_ref, shift_ref, grid_ref, image_ref, text_ref, image_sum_ref, text_sum_ref, texts_ref,
    images_ref, image_out_ref, text_out_ref, weights_ref,
):
    scales, shift = scales_of([bit], scale_ref, grid_ref), shift_ref[0]
    row_count = image_ref.shape[0]
    for rows in blocks_of(row_count):
        add_pairs(
            scales, shift, image_ref, rows, [texts_ref], image_sum_ref, image_out_ref, weights_ref
        )
    for rows in blocks_of(row_count):
        add_pairs(
            scales, shift, text_ref, rows, [images_ref], text_sum_ref, text_out_ref, weights_ref
        )


def add_near(scale, shift, grid, image_half, text_half, image_sum, text_sum, texts, images, bit):
    rows, width = image_half.shape
    return call(
        functools.partial(near_kernel, bit),
        "add_near",
        [scale, shift, grid, image_half, text_half, image_sum, text_sum, texts, images],
        [((rows, width), jnp.float32)] * 2,
        (rows, 2 * rows, width),
        smem=3,
        scratch=[pltpu.VMEM((rows, rows), jnp.bfloat16)],
    )


def add_up_kernel(bits, scale_ref, shift_ref, grid_ref, own_ref, sum_ref, *refs):
    *other_refs, out_ref, weights_ref = refs
    scales = scales_of(bits, scale_ref, grid_ref)
    for rows in blocks_of(own_ref.shape[0]):
        add_pairs(scales, shift_ref[0], own_ref, rows, other_refs, sum_ref, out_ref, weights_ref)


def add_up(scale, shift, grid, own, total, others, bits):
    rows, width = own.shape
    count = sum(x.shape[0] for x in others)
    return call(
        functools.partial(add_up_kernel, tuple(bits)),
        "add_up",
        [scale, shift, grid, own, total, *others],
        [((rows, width), jnp.float32)],
        (rows, count, width),
        smem=3,
        scratch=[pltpu.VMEM((rows, count), jnp.bfloat16)],
    )[0]


def finish_kernel(bits, scale_ref, shift_ref, grid_ref, own_ref, raw_ref, sum_ref, *refs):
    *other_refs, out_ref, weights_ref, total_ref, sems = refs
    scales = scales_of(bits, scale_ref, grid_ref)
    copies = []
    for number, (first, block) in enumerate(blocks_of(own_ref.shape[0])):
        add_pairs(
            scales, shift_ref[0], own_ref, (first, block), other_refs, sum_ref, total_ref, weights_ref
        )
        rows = pl.ds(first, block)
        raw, total = raw_ref[rows, :], total_ref[rows, :]
        inverse = lax.rsqrt(jnp.sum(raw * raw, axis=-1, keepdims=True) + epsilon)
        unit = raw * inverse
        radial = jnp.sum(unit * total, axis=-1, keepdims=True)
        total_ref[rows, :] = (total - unit * radial) * inverse
        copy = pltpu.make_async_copy(total_ref.at[rows, :], out_ref.at[rows, :], sems.at[number])
        copy.start()
        copies.append(copy)
    for copy in copies:
        copy.wait()


def finish(scale, shift, grid, own, raw, total, others, bits):
    rows, width = own.shape
    count = sum(x.shape[0] for x in others)
    return call(
        functools.partial(finish_kernel, tuple(bits)),
        "finish",
        [scale, shift, grid, own, raw, total, *others],
        [((rows, width), jnp.float32)],
        (rows, count, width),
        smem=3,
        out_specs=[pl.BlockSpec(memory_space=pl.ANY)],
        scratch=[
            pltpu.VMEM((rows, count), jnp.bfloat16),
            pltpu.VMEM((rows, width), jnp.float32),
            pltpu.SemaphoreType.DMA((len(blocks_of(rows)),)),
        ],
    )[0]


def passed_along(x, axis, by):
    count = lax.axis_size(axis)
    return lax.ppermute(x, axis, [(i, (i + by) % count) for i in range(count)])


def exchanged(x, bit):
    count = lax.axis_size("blk")
    return lax.ppermute(x, "blk", [(i, i ^ (1 << bit)) for i in range(count)])


def with_partners(bits, visual, caption, grid, scale, shift):
    cut = visual.shape[0] * 3 // 4
    near, far = [bit for bit in bits if bit == 0], [bit for bit in bits if bit != 0]
    text_half = normalized(caption)
    text_z = passed_along(text_half, "group", 1)
    far_texts = [exchanged(text_half, bit) for bit in far]
    image_half = normalized(visual)
    image_first, image_last = image_half[:cut], image_half[cut:]
    boths = [(exchanged(text_half, bit), exchanged(image_half, bit)) for bit in near]
    image_sum, text_sum = diagonal(scale, shift, image_half, text_half)
    image_first, image_last, text_z, image_sum, text_sum = lax.optimization_barrier(
        (image_first, image_last, text_z, image_sum, text_sum)
    )
    image_z_first = passed_along(image_first, "group", -1)
    image_z_last = passed_along(image_last, "group", -1)
    image_first, image_last, far_texts = lax.optimization_barrier(
        (image_first, image_last, far_texts)
    )
    far_images_first = [exchanged(image_first, bit) for bit in far]
    for (texts, images), bit in zip(boths, near):
        image_sum, text_sum = add_near(
            scale, shift, grid, image_half, text_half, image_sum, text_sum, texts, images, bit
        )
    image_gradient = finish(
        scale, shift, grid, image_half, visual, image_sum, [*far_texts, text_z], [*far, None]
    )
    text_sum, image_last, image_gradient = lax.optimization_barrier(
        (text_sum, image_last, image_gradient)
    )
    far_images_last = [exchanged(image_last, bit) for bit in far[:1]]
    image_last, image_z_first = lax.optimization_barrier((image_last, image_z_first))
    far_images_last += [exchanged(image_last, bit) for bit in far[1:]]
    text_sum = add_up(
        scale, shift, grid, text_half, text_sum, [*far_images_first, image_z_first], [*far, None]
    )
    text_gradient = finish(
        scale, shift, grid, text_half, caption, text_sum,
        [*far_images_last, image_z_last], [*far, None],
    )
    return image_gradient, text_gradient


def on_device(
    visual_encoder_outputs,
    caption_encoder_outputs,
    partner_lookup_grid,
    sharpness_coefficient,
    sigmoid_shift_term,
):
    rounds, peers = partner_lookup_grid.shape
    bits = range(peers.bit_length() - 1)
    operands = (
        visual_encoder_outputs,
        caption_encoder_outputs,
        partner_lookup_grid,
        sharpness_coefficient,
        sigmoid_shift_term,
    )
    if len(bits) <= rounds + 1:
        return with_partners(bits, *operands)
    choices = list(itertools.combinations(bits, rounds))
    union = jnp.sum(partner_lookup_grid[:, 0])
    branch = jnp.int32(0)
    for number, choice in enumerate(choices):
        branch = jnp.where(union == sum(1 << bit for bit in choice), jnp.int32(number), branch)
    return lax.switch(
        branch, [functools.partial(with_partners, choice) for choice in choices], *operands
    )


def solution(mesh):
    placed = (P(("blk", "group"), None), P(("blk", "group"), None), P(), P(), P())
    return jax.shard_map(
        on_device,
        mesh=mesh,
        in_specs=placed,
        out_specs=(P(("blk", "group"), None), P(("blk", "group"), None)),
        check_vma=False,
    )
```

```python
import functools
import itertools

import jax
import jax.numpy as jnp
from jax import lax
from jax.experimental import pallas as pl
from jax.experimental.pallas import tpu as pltpu
from jax.sharding import PartitionSpec as P

epsilon = 1e-06
log2_e = 1.4426950408889634
MIB = 1024 * 1024
VMEM = pl.BlockSpec(memory_space=pltpu.VMEM)
SMEM = pl.BlockSpec(memory_space=pltpu.SMEM)
BLOCK, STRIP, COLUMNS = 256, 256, 384


def cost(rows, other_rows, width):
    return pl.CostEstimate(
        flops=4 * rows * max(other_rows, 1) * width,
        bytes_accessed=8 * rows * width,
        transcendentals=2 * rows * other_rows,
    )


def call(body, name, operands, outs, work, smem=2, grid=None, out_specs=None, scratch=()):
    return pl.pallas_call(
        body,
        grid=grid or (),
        in_specs=[SMEM] * smem + [VMEM] * (len(operands) - smem),
        out_specs=out_specs or [VMEM] * len(outs),
        out_shape=[jax.ShapeDtypeStruct(shape, dtype) for shape, dtype in outs],
        scratch_shapes=list(scratch),
        name=name,
        compiler_params=pltpu.CompilerParams(vmem_limit_bytes=24 * MIB),
        cost_estimate=cost(*work),
    )(*operands)


def strips(count, size):
    return [(first, min(first + size, count)) for first in range(0, count, size)]


def normalized(raw):
    total = jnp.sum(raw * raw, axis=-1, keepdims=True)
    return (raw * lax.rsqrt(total + epsilon)).astype(jnp.bfloat16)


def coupling(own, other, scale, factor, shift, places=None):
    products = lax.dot_general(
        own, other, (((1,), (1,)), ((), ())), preferred_element_type=jnp.float32
    )
    powers = products * (-log2_e * scale) - log2_e * shift
    if places is not None:
        row = places[0] + lax.broadcasted_iota(jnp.int32, powers.shape, 0)
        column = places[1] + lax.broadcasted_iota(jnp.int32, powers.shape, 1)
        same = row == column
        powers = jnp.where(same, -powers, powers)
    below = 1.0 + jnp.exp2(powers)
    inverse = pl.reciprocal(below, approx=True)
    weights = factor * (inverse * (2.0 - below * inverse))
    if places is not None:
        weights = jnp.where(same, -weights, weights)
    return weights.astype(jnp.bfloat16)


def is_drawn(grid_ref, bit):
    drawn = jnp.bool_(False)
    for number in range(grid_ref.shape[0]):
        drawn = drawn | (grid_ref[number, 0] == (1 << bit))
    return drawn


def add_pairs(scales, shift, own_ref, rows, others, before_ref, out_ref, weights_ref, matched=False):
    first, block = rows
    rows = slice(first, first + block)
    own = own_ref[rows, :]
    places, left = [], 0
    for (scale, factor), other_ref in zip(scales, others):
        count, width = other_ref.shape
        for top, bottom in strips(count, STRIP):
            weights_ref[rows, left + top : left + bottom] = coupling(
                own, other_ref[top:bottom, :], scale, factor, shift, (first, top) if matched else None
            )
        places.append(slice(left, left + count))
        left += count
    for top, bottom in strips(width, COLUMNS):
        total = None if before_ref is None else before_ref[rows, top:bottom]
        for place, other_ref in zip(places, others):
            added = jnp.dot(
                weights_ref[rows, place], other_ref[:, top:bottom], preferred_element_type=jnp.float32
            )
            total = added if total is None else total + added
        out_ref[rows, top:bottom] = total


def blocks_of(count):
    return [(first, min(BLOCK, count - first)) for first in range(0, count, BLOCK)]


def scales_of(bits, scale_ref, grid_ref):
    scale = scale_ref[0]
    return [
        (scale, scale if bit is None else jnp.where(is_drawn(grid_ref, bit), scale, 0.0))
        for bit in bits
    ]


def diagonal_kernel(scale_ref, shift_ref, image_ref, text_ref, image_sum_ref, text_sum_ref, weights_ref):
    scale, shift = scale_ref[0], shift_ref[0]
    row_count, width = image_ref.shape
    for rows in blocks_of(row_count):
        add_pairs(
            [(scale, scale)], shift, image_ref, rows, [text_ref], None, image_sum_ref, weights_ref, True
        )
    for first, last in strips(row_count, STRIP):
        for left, right in strips(width, COLUMNS):
            text_sum_ref[first:last, left:right] = lax.dot_general(
                weights_ref[:, first:last], image_ref[:, left:right], (((0,), (0,)), ((), ())),
                preferred_element_type=jnp.float32,
            )


def diagonal(scale, shift, image_half, text_half):
    rows, width = image_half.shape
    return call(
        diagonal_kernel,
        "diagonal",
        [scale, shift, image_half, text_half],
        [((rows, width), jnp.float32)] * 2,
        (rows, 2 * rows, width),
        scratch=[pltpu.VMEM((rows, rows), jnp.bfloat16)],
    )


def near_kernel(
    bit, scale_ref, shift_ref, grid_ref, image_ref, text_ref, image_sum_ref, text_sum_ref, texts_ref,
    images_ref, image_out_ref, text_out_ref, weights_ref,
):
    scales, shift = scales_of([bit], scale_ref, grid_ref), shift_ref[0]
    row_count = image_ref.shape[0]
    for rows in blocks_of(row_count):
        add_pairs(
            scales, shift, image_ref, rows, [texts_ref], image_sum_ref, image_out_ref, weights_ref
        )
    for rows in blocks_of(row_count):
        add_pairs(
            scales, shift, text_ref, rows, [images_ref], text_sum_ref, text_out_ref, weights_ref
        )


def add_near(scale, shift, grid, image_half, text_half, image_sum, text_sum, texts, images, bit):
    rows, width = image_half.shape
    return call(
        functools.partial(near_kernel, bit),
        "add_near",
        [scale, shift, grid, image_half, text_half, image_sum, text_sum, texts, images],
        [((rows, width), jnp.float32)] * 2,
        (rows, 2 * rows, width),
        smem=3,
        scratch=[pltpu.VMEM((rows, rows), jnp.bfloat16)],
    )


def add_up_kernel(bits, scale_ref, shift_ref, grid_ref, own_ref, sum_ref, *refs):
    *other_refs, out_ref, weights_ref = refs
    scales = scales_of(bits, scale_ref, grid_ref)
    for rows in blocks_of(own_ref.shape[0]):
        add_pairs(scales, shift_ref[0], own_ref, rows, other_refs, sum_ref, out_ref, weights_ref)


def add_up(scale, shift, grid, own, total, others, bits):
    rows, width = own.shape
    count = sum(x.shape[0] for x in others)
    return call(
        functools.partial(add_up_kernel, tuple(bits)),
        "add_up",
        [scale, shift, grid, own, total, *others],
        [((rows, width), jnp.float32)],
        (rows, count, width),
        smem=3,
        scratch=[pltpu.VMEM((rows, count), jnp.bfloat16)],
    )[0]


def finish_kernel(bits, scale_ref, shift_ref, grid_ref, own_ref, raw_ref, sum_ref, *refs):
    *other_refs, out_ref, weights_ref, total_ref, sems = refs
    scales = scales_of(bits, scale_ref, grid_ref)
    copies = []
    for number, (first, block) in enumerate(blocks_of(own_ref.shape[0])):
        add_pairs(
            scales, shift_ref[0], own_ref, (first, block), other_refs, sum_ref, total_ref, weights_ref
        )
        rows = pl.ds(first, block)
        raw, total = raw_ref[rows, :], total_ref[rows, :]
        inverse = lax.rsqrt(jnp.sum(raw * raw, axis=-1, keepdims=True) + epsilon)
        unit = raw * inverse
        radial = jnp.sum(unit * total, axis=-1, keepdims=True)
        total_ref[rows, :] = (total - unit * radial) * inverse
        copy = pltpu.make_async_copy(total_ref.at[rows, :], out_ref.at[rows, :], sems.at[number])
        copy.start()
        copies.append(copy)
    for copy in copies:
        copy.wait()


def finish(scale, shift, grid, own, raw, total, others, bits):
    rows, width = own.shape
    count = sum(x.shape[0] for x in others)
    return call(
        functools.partial(finish_kernel, tuple(bits)),
        "finish",
        [scale, shift, grid, own, raw, total, *others],
        [((rows, width), jnp.float32)],
        (rows, count, width),
        smem=3,
        out_specs=[pl.BlockSpec(memory_space=pl.ANY)],
        scratch=[
            pltpu.VMEM((rows, count), jnp.bfloat16),
            pltpu.VMEM((rows, width), jnp.float32),
            pltpu.SemaphoreType.DMA((len(blocks_of(rows)),)),
        ],
    )[0]


def passed_along(x, axis, by):
    count = lax.axis_size(axis)
    return lax.ppermute(x, axis, [(i, (i + by) % count) for i in range(count)])


def exchanged(x, bit):
    count = lax.axis_size("blk")
    return lax.ppermute(x, "blk", [(i, i ^ (1 << bit)) for i in range(count)])


def with_partners(bits, visual, caption, grid, scale, shift):
    cut = visual.shape[0] * 3 // 4
    near, far = [bit for bit in bits if bit == 0], [bit for bit in bits if bit != 0]
    text_half = normalized(caption)
    text_z = passed_along(text_half, "group", 1)
    far_texts = [exchanged(text_half, bit) for bit in far]
    image_half = normalized(visual)
    image_first, image_last = image_half[:cut], image_half[cut:]
    boths = [(exchanged(text_half, bit), exchanged(image_half, bit)) for bit in near]
    image_sum, text_sum = diagonal(scale, shift, image_half, text_half)
    far_first, boths = lax.optimization_barrier((image_first, boths))
    image_first, image_last, text_z, image_sum, text_sum = lax.optimization_barrier(
        (image_first, image_last, text_z, image_sum, text_sum)
    )
    image_z_first = passed_along(image_first, "group", -1)
    far_images_first = [exchanged(far_first, bit) for bit in far]
    for (texts, images), bit in zip(boths, near):
        image_sum, text_sum = add_near(
            scale, shift, grid, image_half, text_half, image_sum, text_sum, texts, images, bit
        )
    image_last, far_texts = lax.optimization_barrier((image_last, far_texts))
    far_images_last = [exchanged(image_last, bit) for bit in far]
    image_gradient = finish(
        scale, shift, grid, image_half, visual, image_sum, [*far_texts, text_z], [*far, None]
    )
    text_sum, image_last, far_images_first, image_gradient = lax.optimization_barrier(
        (text_sum, image_last, far_images_first, image_gradient)
    )
    image_z_last = passed_along(image_last, "group", -1)
    if far:
        text_sum = add_up(scale, shift, grid, text_half, text_sum, far_images_first, far)
    text_sum = add_up(
        scale, shift, grid, text_half, text_sum, [*far_images_last, image_z_first], [*far, None]
    )
    text_gradient = finish(
        scale, shift, grid, text_half, caption, text_sum, [image_z_last], [None]
    )
    return image_gradient, text_gradient


def on_device(
    visual_encoder_outputs,
    caption_encoder_outputs,
    partner_lookup_grid,
    sharpness_coefficient,
    sigmoid_shift_term,
):
    rounds, peers = partner_lookup_grid.shape
    bits = range(peers.bit_length() - 1)
    operands = (
        visual_encoder_outputs,
        caption_encoder_outputs,
        partner_lookup_grid,
        sharpness_coefficient,
        sigmoid_shift_term,
    )
    if len(bits) <= rounds + 1:
        return with_partners(bits, *operands)
    choices = list(itertools.combinations(bits, rounds))
    union = jnp.sum(partner_lookup_grid[:, 0])
    branch = jnp.int32(0)
    for number, choice in enumerate(choices):
        branch = jnp.where(union == sum(1 << bit for bit in choice), jnp.int32(number), branch)
    return lax.switch(
        branch, [functools.partial(with_partners, choice) for choice in choices], *operands
    )


def solution(mesh):
    placed = (P(("blk", "group"), None), P(("blk", "group"), None), P(), P(), P())
    return jax.shard_map(
        on_device,
        mesh=mesh,
        in_specs=placed,
        out_specs=(P(("blk", "group"), None), P(("blk", "group"), None)),
        check_vma=False,
    )
```

```python
import functools
import itertools

import jax
import jax.numpy as jnp
from jax import lax
from jax.experimental import pallas as pl
from jax.experimental.pallas import tpu as pltpu
from jax.sharding import PartitionSpec as P

epsilon = 1e-06
log2_e = 1.4426950408889634
MIB = 1024 * 1024
VMEM = pl.BlockSpec(memory_space=pltpu.VMEM)
SMEM = pl.BlockSpec(memory_space=pltpu.SMEM)
BLOCK, STRIP, COLUMNS, LANES = 256, 256, 384, 128


def cost(rows, other_rows, width):
    return pl.CostEstimate(
        flops=4 * rows * max(other_rows, 1) * width,
        bytes_accessed=8 * rows * width,
        transcendentals=2 * rows * other_rows,
    )


def call(body, name, operands, outs, work, smem=2, grid=None, out_specs=None, scratch=()):
    return pl.pallas_call(
        body,
        grid=grid or (),
        in_specs=[SMEM] * smem + [VMEM] * (len(operands) - smem),
        out_specs=out_specs or [VMEM] * len(outs),
        out_shape=[jax.ShapeDtypeStruct(shape, dtype) for shape, dtype in outs],
        scratch_shapes=list(scratch),
        name=name,
        compiler_params=pltpu.CompilerParams(vmem_limit_bytes=24 * MIB),
        cost_estimate=cost(*work),
    )(*operands)


def strips(count, size):
    return [(first, min(first + size, count)) for first in range(0, count, size)]


def normalized(raw):
    total = jnp.sum(raw * raw, axis=-1, keepdims=True)
    return (raw * lax.rsqrt(total + epsilon)).astype(jnp.bfloat16)


def coupling(own, other, scale, shift, places=None):
    products = lax.dot_general(
        own, other, (((1,), (1,)), ((), ())), preferred_element_type=jnp.float32
    )
    powers = products * (-log2_e * scale) - log2_e * shift
    if places is not None:
        row = places[0] + lax.broadcasted_iota(jnp.int32, powers.shape, 0)
        column = places[1] + lax.broadcasted_iota(jnp.int32, powers.shape, 1)
        same = row == column
        powers = jnp.where(same, -powers, powers)
    below = 1.0 + jnp.exp2(powers)
    inverse = pl.reciprocal(below, approx=True)
    weights = scale * (inverse * (2.0 - below * inverse))
    if places is not None:
        weights = jnp.where(same, -weights, weights)
    return weights.astype(jnp.bfloat16)


def add_pairs(scale, shift, own_ref, rows, others, before_ref, out_ref, weights_ref, raw_ref=None, matched=False):
    own = own_ref[rows, :]
    places, left = [], 0
    for other_ref in others:
        count, width = other_ref.shape
        for top, bottom in strips(count, STRIP):
            weights_ref[:, left + top : left + bottom] = coupling(
                own, other_ref[top:bottom, :], scale, shift, (rows.start, top) if matched else None
            )
        places.append(slice(left, left + count))
        left += count
    squares, products = 0.0, 0.0
    for top, bottom in strips(width, COLUMNS):
        total = None if before_ref is None else before_ref[rows, top:bottom]
        for place, other_ref in zip(places, others):
            added = jnp.dot(
                weights_ref[:, place], other_ref[:, top:bottom], preferred_element_type=jnp.float32
            )
            total = added if total is None else total + added
        out_ref[rows, top:bottom] = total
        if raw_ref is not None:
            raw = raw_ref[rows, top:bottom]
            for first in range(0, bottom - top, LANES):
                part = raw[:, first : first + LANES]
                squares = squares + part * part
                products = products + part * total[:, first : first + LANES]
    if raw_ref is not None:
        return (
            jnp.sum(squares, axis=-1, keepdims=True), jnp.sum(products, axis=-1, keepdims=True)
        )


def row_blocks(rows, body):
    def step(number, carry):
        body(number, pl.ds(pl.multiple_of(number * BLOCK, BLOCK), BLOCK))
        return carry

    lax.fori_loop(0, rows // BLOCK, step, 0)


def diagonal_kernel(scale_ref, shift_ref, image_ref, text_ref, image_sum_ref, text_sum_ref, weights_ref):
    scale, shift = scale_ref[0], shift_ref[0]
    row_count, width = image_ref.shape

    def for_images(number, rows):
        add_pairs(
            scale, shift, image_ref, rows, [text_ref], None, image_sum_ref, weights_ref.at[rows, :],
            matched=True,
        )

    row_blocks(row_count, for_images)
    for first, last in strips(row_count, STRIP):
        for left, right in strips(width, COLUMNS):
            text_sum_ref[first:last, left:right] = lax.dot_general(
                weights_ref[:, first:last], image_ref[:, left:right], (((0,), (0,)), ((), ())),
                preferred_element_type=jnp.float32,
            )


def diagonal(scale, shift, image_half, text_half):
    rows, width = image_half.shape
    return call(
        diagonal_kernel,
        "diagonal",
        [scale, shift, image_half, text_half],
        [((rows, width), jnp.float32)] * 2,
        (rows, 2 * rows, width),
        scratch=[pltpu.VMEM((rows, rows), jnp.bfloat16)],
    )


def add_up_kernel(scale_ref, shift_ref, own_ref, sum_ref, *refs):
    *other_refs, out_ref, weights_ref = refs

    def body(number, rows):
        add_pairs(
            scale_ref[0], shift_ref[0], own_ref, rows, other_refs, sum_ref, out_ref, weights_ref
        )

    row_blocks(own_ref.shape[0], body)


def add_up(scale, shift, own, total, others):
    rows, width = own.shape
    count = sum(x.shape[0] for x in others)
    return call(
        add_up_kernel,
        "add_up",
        [scale, shift, own, total, *others],
        [((rows, width), jnp.float32)],
        (rows, count, width),
        scratch=[pltpu.VMEM((BLOCK, count), jnp.bfloat16)],
    )[0]


def finish_kernel(scale_ref, shift_ref, own_ref, raw_ref, sum_ref, *refs):
    *other_refs, out_ref, weights_ref, total_ref, sems = refs

    def copy_of(number, rows):
        return pltpu.make_async_copy(total_ref.at[rows, :], out_ref.at[rows, :], sems.at[number])

    def body(number, rows):
        squares, products = add_pairs(
            scale_ref[0], shift_ref[0], own_ref, rows, other_refs, sum_ref, total_ref, weights_ref,
            raw_ref,
        )
        inverse = lax.rsqrt(squares + epsilon)
        radial = products * (inverse * inverse * inverse)
        total_ref[rows, :] = total_ref[rows, :] * inverse - raw_ref[rows, :] * radial
        copy_of(number, rows).start()

    row_blocks(own_ref.shape[0], body)
    row_blocks(own_ref.shape[0], lambda number, rows: copy_of(number, rows).wait())


def finish(scale, shift, own, raw, total, others):
    rows, width = own.shape
    count = sum(x.shape[0] for x in others)
    return call(
        finish_kernel,
        "finish",
        [scale, shift, own, raw, total, *others],
        [((rows, width), jnp.float32)],
        (rows, count, width),
        out_specs=[pl.BlockSpec(memory_space=pl.ANY)],
        scratch=[
            pltpu.VMEM((BLOCK, count), jnp.bfloat16),
            pltpu.VMEM((rows, width), jnp.float32),
            pltpu.SemaphoreType.DMA((rows // BLOCK,)),
        ],
    )[0]


def choose_kernel(unions, grid_ref, branch_ref):
    union = grid_ref[0, 0]
    for number in range(1, grid_ref.shape[0]):
        union = union + grid_ref[number, 0]
    branch = jnp.int32(0)
    for number, each in enumerate(unions):
        branch = jnp.where(union == each, jnp.int32(number), branch)
    branch_ref[0] = branch


def chosen(grid, unions):
    return pl.pallas_call(
        functools.partial(choose_kernel, unions),
        in_specs=[SMEM],
        out_specs=SMEM,
        out_shape=jax.ShapeDtypeStruct((1,), jnp.int32),
        name="choose",
    )(grid)[0]


def passed_along(x, axis, by):
    count = lax.axis_size(axis)
    return lax.ppermute(x, axis, [(i, (i + by) % count) for i in range(count)])


def exchanged(x, bit):
    count = lax.axis_size("blk")
    return lax.ppermute(x, "blk", [(i, i ^ (1 << bit)) for i in range(count)])


def with_partners(bits, visual, caption, scale, shift):
    cut = visual.shape[0] * 3 // 4
    near, far = [bit for bit in bits if bit == 0], [bit for bit in bits if bit != 0]
    text_half = normalized(caption)
    text_z = passed_along(text_half, "group", 1)
    far_texts = [exchanged(text_half, bit) for bit in far]
    image_half = normalized(visual)
    image_first, image_last = image_half[:cut], image_half[cut:]
    near_texts = [exchanged(text_half, bit) for bit in near]
    near_images = [exchanged(image_half, bit) for bit in near]
    image_sum, text_sum = diagonal(scale, shift, image_half, text_half)
    image_first, image_last, text_z, image_sum, text_sum = lax.optimization_barrier(
        (image_first, image_last, text_z, image_sum, text_sum)
    )
    image_z_first = passed_along(image_first, "group", -1)
    image_z_last = passed_along(image_last, "group", -1)
    image_first, image_last, far_texts = lax.optimization_barrier(
        (image_first, image_last, far_texts)
    )
    far_images_first = [exchanged(image_first, bit) for bit in far]
    image_gradient = finish(
        scale, shift, image_half, visual, image_sum, [*near_texts, *far_texts, text_z]
    )
    text_sum, image_last, image_gradient = lax.optimization_barrier(
        (text_sum, image_last, image_gradient)
    )
    far_images_last = [exchanged(image_last, bit) for bit in far[:1]]
    if near:
        text_sum = add_up(scale, shift, text_half, text_sum, near_images)
    else:
        image_last, image_z_first = lax.optimization_barrier((image_last, image_z_first))
    far_images_last += [exchanged(image_last, bit) for bit in far[1:]]
    text_sum = add_up(
        scale, shift, text_half, text_sum, [*far_images_first, image_z_first]
    )
    text_gradient = finish(
        scale, shift, text_half, caption, text_sum, [*far_images_last, image_z_last]
    )
    return image_gradient, text_gradient


def on_device(
    visual_encoder_outputs,
    caption_encoder_outputs,
    partner_lookup_grid,
    sharpness_coefficient,
    sigmoid_shift_term,
):
    rounds, peers = partner_lookup_grid.shape
    choices = list(itertools.combinations(range(peers.bit_length() - 1), rounds))
    unions = [sum(1 << bit for bit in bits) for bits in choices]
    return lax.switch(
        chosen(partner_lookup_grid, unions),
        [functools.partial(with_partners, bits) for bits in choices],
        visual_encoder_outputs,
        caption_encoder_outputs,
        sharpness_coefficient,
        sigmoid_shift_term,
    )


def solution(mesh):
    placed = (P(("blk", "group"), None), P(("blk", "group"), None), P(), P(), P())
    return jax.shard_map(
        on_device,
        mesh=mesh,
        in_specs=placed,
        out_specs=(P(("blk", "group"), None), P(("blk", "group"), None)),
        check_vma=False,
    )
```

```python
import functools
import itertools

import jax
import jax.numpy as jnp
from jax import lax
from jax.experimental import pallas as pl
from jax.experimental.pallas import tpu as pltpu
from jax.sharding import PartitionSpec as P

epsilon = 1e-06
log2_e = 1.4426950408889634
MIB = 1024 * 1024
VMEM = pl.BlockSpec(memory_space=pltpu.VMEM)
SMEM = pl.BlockSpec(memory_space=pltpu.SMEM)
BLOCK, STRIP, COLUMNS, SLICE, LANES = 256, 256, 384, 64, 128


def cost(rows, other_rows, width):
    return pl.CostEstimate(
        flops=4 * rows * max(other_rows, 1) * width,
        bytes_accessed=8 * rows * width,
        transcendentals=2 * rows * other_rows,
    )


def call(body, name, operands, outs, work, smem=2, grid=None, out_specs=None, scratch=()):
    return pl.pallas_call(
        body,
        grid=grid or (),
        in_specs=[SMEM] * smem + [VMEM] * (len(operands) - smem),
        out_specs=out_specs or [VMEM] * len(outs),
        out_shape=[jax.ShapeDtypeStruct(shape, dtype) for shape, dtype in outs],
        scratch_shapes=list(scratch),
        name=name,
        compiler_params=pltpu.CompilerParams(vmem_limit_bytes=24 * MIB),
        cost_estimate=cost(*work),
    )(*operands)


def strips(count, size):
    return [(first, min(first + size, count)) for first in range(0, count, size)]


def normalized(raw):
    total = jnp.sum(raw * raw, axis=-1, keepdims=True)
    return (raw * lax.rsqrt(total + epsilon)).astype(jnp.bfloat16)


def coupled(products, scale, factor, shift, places=None):
    powers = products * (-log2_e * scale) - log2_e * shift
    if places is not None:
        row = places[0] + lax.broadcasted_iota(jnp.int32, powers.shape, 0)
        column = places[1] + lax.broadcasted_iota(jnp.int32, powers.shape, 1)
        same = row == column
        powers = jnp.where(same, -powers, powers)
    below = 1.0 + jnp.exp2(powers)
    inverse = pl.reciprocal(below, approx=True)
    weights = factor * (inverse * (2.0 - below * inverse))
    if places is not None:
        weights = jnp.where(same, -weights, weights)
    return weights.astype(jnp.bfloat16)


def is_drawn(grid_ref, bit):
    drawn = jnp.bool_(False)
    for number in range(grid_ref.shape[0]):
        drawn = drawn | (grid_ref[number, 0] == (1 << bit))
    return drawn


def add_pairs(scales, shift, own_ref, rows, others, before_ref, out_ref, weights_ref, raw_ref=None, matched=False):
    first, block = rows
    own = own_ref[first : first + block, :]
    pieces = strips(block, SLICE)
    places, left = [], 0
    for (scale, factor), other_ref in zip(scales, others):
        count, width = other_ref.shape
        for top, bottom in strips(count, STRIP):
            products = lax.dot_general(
                own, other_ref[top:bottom, :], (((1,), (1,)), ((), ())),
                preferred_element_type=jnp.float32,
            )
            for low, high in pieces:
                weights_ref[first + low : first + high, left + top : left + bottom] = coupled(
                    products[low:high], scale, factor, shift, (first + low, top) if matched else None
                )
        places.append(slice(left, left + count))
        left += count
    sums = [[0.0, 0.0] for _ in pieces]
    for top, bottom in strips(width, COLUMNS):
        total = None
        for place, other_ref in zip(places, others):
            added = jnp.dot(
                weights_ref[first : first + block, place], other_ref[:, top:bottom],
                preferred_element_type=jnp.float32,
            )
            total = added if total is None else total + added
        for number, (low, high) in enumerate(pieces):
            part = total[low:high]
            here = slice(first + low, first + high)
            if before_ref is not None:
                part = part + before_ref[here, top:bottom]
            out_ref[here, top:bottom] = part
            if raw_ref is not None:
                raw = raw_ref[here, top:bottom]
                for side in range(0, bottom - top, LANES):
                    lanes = slice(side, side + LANES)
                    sums[number][0] += raw[:, lanes] * raw[:, lanes]
                    sums[number][1] += raw[:, lanes] * part[:, lanes]
    return sums


def blocks_of(count):
    return [(first, min(BLOCK, count - first)) for first in range(0, count, BLOCK)]


def scales_of(bits, scale_ref, grid_ref):
    scale = scale_ref[0]
    return [
        (scale, scale if bit is None else jnp.where(is_drawn(grid_ref, bit), scale, 0.0))
        for bit in bits
    ]


def diagonal_kernel(scale_ref, shift_ref, image_ref, text_ref, image_sum_ref, text_sum_ref, weights_ref):
    scale, shift = scale_ref[0], shift_ref[0]
    row_count, width = image_ref.shape
    for rows in blocks_of(row_count):
        add_pairs(
            [(scale, scale)], shift, image_ref, rows, [text_ref], None, image_sum_ref, weights_ref,
            matched=True,
        )
    for first, last in strips(row_count, STRIP):
        for left, right in strips(width, COLUMNS):
            text_sum_ref[first:last, left:right] = lax.dot_general(
                weights_ref[:, first:last], image_ref[:, left:right], (((0,), (0,)), ((), ())),
                preferred_element_type=jnp.float32,
            )


def diagonal(scale, shift, image_half, text_half):
    rows, width = image_half.shape
    return call(
        diagonal_kernel,
        "diagonal",
        [scale, shift, image_half, text_half],
        [((rows, width), jnp.float32)] * 2,
        (rows, 2 * rows, width),
        scratch=[pltpu.VMEM((rows, rows), jnp.bfloat16)],
    )


def near_kernel(
    bit, scale_ref, shift_ref, grid_ref, image_ref, text_ref, image_sum_ref, text_sum_ref, texts_ref,
    images_ref, image_out_ref, text_out_ref, weights_ref,
):
    scales, shift = scales_of([bit], scale_ref, grid_ref), shift_ref[0]
    row_count = image_ref.shape[0]
    for rows in blocks_of(row_count):
        add_pairs(
            scales, shift, image_ref, rows, [texts_ref], image_sum_ref, image_out_ref, weights_ref
        )
    for rows in blocks_of(row_count):
        add_pairs(
            scales, shift, text_ref, rows, [images_ref], text_sum_ref, text_out_ref, weights_ref
        )


def add_near(scale, shift, grid, image_half, text_half, image_sum, text_sum, texts, images, bit):
    rows, width = image_half.shape
    return call(
        functools.partial(near_kernel, bit),
        "add_near",
        [scale, shift, grid, image_half, text_half, image_sum, text_sum, texts, images],
        [((rows, width), jnp.float32)] * 2,
        (rows, 2 * rows, width),
        smem=3,
        scratch=[pltpu.VMEM((rows, rows), jnp.bfloat16)],
    )


def add_up_kernel(bits, scale_ref, shift_ref, grid_ref, own_ref, sum_ref, *refs):
    *other_refs, out_ref, weights_ref = refs
    scales = scales_of(bits, scale_ref, grid_ref)
    for rows in blocks_of(own_ref.shape[0]):
        add_pairs(scales, shift_ref[0], own_ref, rows, other_refs, sum_ref, out_ref, weights_ref)


def add_up(scale, shift, grid, own, total, others, bits):
    rows, width = own.shape
    count = sum(x.shape[0] for x in others)
    return call(
        functools.partial(add_up_kernel, tuple(bits)),
        "add_up",
        [scale, shift, grid, own, total, *others],
        [((rows, width), jnp.float32)],
        (rows, count, width),
        smem=3,
        scratch=[pltpu.VMEM((rows, count), jnp.bfloat16)],
    )[0]


def finish_kernel(bits, scale_ref, shift_ref, grid_ref, own_ref, raw_ref, sum_ref, *refs):
    *other_refs, out_ref, weights_ref, total_ref, sems = refs
    scales = scales_of(bits, scale_ref, grid_ref)
    copies = []
    for first, block in blocks_of(own_ref.shape[0]):
        sums = add_pairs(
            scales, shift_ref[0], own_ref, (first, block), other_refs, sum_ref, total_ref, weights_ref,
            raw_ref,
        )
        for (squares, products), (low, high) in zip(sums, strips(block, SLICE)):
            inverse = lax.rsqrt(jnp.sum(squares, axis=-1, keepdims=True) + epsilon)
            radial = jnp.sum(products, axis=-1, keepdims=True) * (inverse * inverse * inverse)
            here = slice(first + low, first + high)
            for top, bottom in strips(own_ref.shape[1], COLUMNS):
                total_ref[here, top:bottom] = (
                    total_ref[here, top:bottom] * inverse - raw_ref[here, top:bottom] * radial
                )
        rows = pl.ds(first, block)
        copy = pltpu.make_async_copy(
            total_ref.at[rows, :], out_ref.at[rows, :], sems.at[len(copies)]
        )
        copy.start()
        copies.append(copy)
    for copy in copies:
        copy.wait()


def finish(scale, shift, grid, own, raw, total, others, bits):
    rows, width = own.shape
    count = sum(x.shape[0] for x in others)
    return call(
        functools.partial(finish_kernel, tuple(bits)),
        "finish",
        [scale, shift, grid, own, raw, total, *others],
        [((rows, width), jnp.float32)],
        (rows, count, width),
        smem=3,
        out_specs=[pl.BlockSpec(memory_space=pl.ANY)],
        scratch=[
            pltpu.VMEM((rows, count), jnp.bfloat16),
            pltpu.VMEM((rows, width), jnp.float32),
            pltpu.SemaphoreType.DMA((len(blocks_of(rows)),)),
        ],
    )[0]


def passed_along(x, axis, by):
    count = lax.axis_size(axis)
    return lax.ppermute(x, axis, [(i, (i + by) % count) for i in range(count)])


def exchanged(x, bit):
    count = lax.axis_size("blk")
    return lax.ppermute(x, "blk", [(i, i ^ (1 << bit)) for i in range(count)])


def with_partners(bits, visual, caption, grid, scale, shift):
    cut = visual.shape[0] * 3 // 4
    near, far = [bit for bit in bits if bit == 0], [bit for bit in bits if bit != 0]
    text_half = normalized(caption)
    text_z = passed_along(text_half, "group", 1)
    far_texts = [exchanged(text_half, bit) for bit in far]
    image_half = normalized(visual)
    image_first, image_last = image_half[:cut], image_half[cut:]
    boths = [(exchanged(text_half, bit), exchanged(image_half, bit)) for bit in near]
    image_sum, text_sum = diagonal(scale, shift, image_half, text_half)
    image_first, image_last, text_z, image_sum, text_sum = lax.optimization_barrier(
        (image_first, image_last, text_z, image_sum, text_sum)
    )
    image_z_first = passed_along(image_first, "group", -1)
    image_z_last = passed_along(image_last, "group", -1)
    far_images_first = [exchanged(image_first, bit) for bit in far]
    for (texts, images), bit in zip(boths, near):
        image_sum, text_sum = add_near(
            scale, shift, grid, image_half, text_half, image_sum, text_sum, texts, images, bit
        )
    image_gradient = finish(
        scale, shift, grid, image_half, visual, image_sum, [*far_texts, text_z], [*far, None]
    )
    text_sum, image_last, image_gradient = lax.optimization_barrier(
        (text_sum, image_last, image_gradient)
    )
    far_images_last = [exchanged(image_last, bit) for bit in far[:1]]
    image_last, image_z_first = lax.optimization_barrier((image_last, image_z_first))
    far_images_last += [exchanged(image_last, bit) for bit in far[1:]]
    text_sum = add_up(
        scale, shift, grid, text_half, text_sum, [*far_images_first, image_z_first], [*far, None]
    )
    text_gradient = finish(
        scale, shift, grid, text_half, caption, text_sum,
        [*far_images_last, image_z_last], [*far, None],
    )
    return image_gradient, text_gradient


def on_device(
    visual_encoder_outputs,
    caption_encoder_outputs,
    partner_lookup_grid,
    sharpness_coefficient,
    sigmoid_shift_term,
):
    rounds, peers = partner_lookup_grid.shape
    bits = range(peers.bit_length() - 1)
    operands = (
        visual_encoder_outputs,
        caption_encoder_outputs,
        partner_lookup_grid,
        sharpness_coefficient,
        sigmoid_shift_term,
    )
    if len(bits) <= rounds + 1:
        return with_partners(bits, *operands)
    choices = list(itertools.combinations(bits, rounds))
    union = jnp.sum(partner_lookup_grid[:, 0])
    branch = jnp.int32(0)
    for number, choice in enumerate(choices):
        branch = jnp.where(union == sum(1 << bit for bit in choice), jnp.int32(number), branch)
    return lax.switch(
        branch, [functools.partial(with_partners, choice) for choice in choices], *operands
    )


def solution(mesh):
    placed = (P(("blk", "group"), None), P(("blk", "group"), None), P(), P(), P())
    return jax.shard_map(
        on_device,
        mesh=mesh,
        in_specs=placed,
        out_specs=(P(("blk", "group"), None), P(("blk", "group"), None)),
        check_vma=False,
    )
```

```python
import functools
import itertools

import jax
import jax.numpy as jnp
from jax import lax
from jax.experimental import pallas as pl
from jax.experimental.pallas import tpu as pltpu
from jax.sharding import PartitionSpec as P

epsilon = 1e-06
log2_e = 1.4426950408889634
MIB = 1024 * 1024
VMEM = pl.BlockSpec(memory_space=pltpu.VMEM)
SMEM = pl.BlockSpec(memory_space=pltpu.SMEM)
BLOCK, STRIP, COLUMNS, SLICE, LANES = 512, 256, 384, 64, 128


def cost(rows, other_rows, width):
    return pl.CostEstimate(
        flops=4 * rows * max(other_rows, 1) * width,
        bytes_accessed=8 * rows * width,
        transcendentals=2 * rows * other_rows,
    )


def call(body, name, operands, outs, work, smem=2, grid=None, out_specs=None, scratch=()):
    return pl.pallas_call(
        body,
        grid=grid or (),
        in_specs=[SMEM] * smem + [VMEM] * (len(operands) - smem),
        out_specs=out_specs or [VMEM] * len(outs),
        out_shape=[jax.ShapeDtypeStruct(shape, dtype) for shape, dtype in outs],
        scratch_shapes=list(scratch),
        name=name,
        compiler_params=pltpu.CompilerParams(vmem_limit_bytes=24 * MIB),
        cost_estimate=cost(*work),
    )(*operands)


def strips(count, size):
    return [(first, min(first + size, count)) for first in range(0, count, size)]


def normalized(raw):
    total = jnp.sum(raw * raw, axis=-1, keepdims=True)
    return (raw * lax.rsqrt(total + epsilon)).astype(jnp.bfloat16)


def coupled(products, scale, factor, shift, places=None):
    powers = products * (-log2_e * scale) - log2_e * shift
    if places is not None:
        row = places[0] + lax.broadcasted_iota(jnp.int32, powers.shape, 0)
        column = places[1] + lax.broadcasted_iota(jnp.int32, powers.shape, 1)
        same = row == column
        powers = jnp.where(same, -powers, powers)
    below = 1.0 + jnp.exp2(powers)
    inverse = pl.reciprocal(below, approx=True)
    weights = factor * (inverse * (2.0 - below * inverse))
    if places is not None:
        weights = jnp.where(same, -weights, weights)
    return weights.astype(jnp.bfloat16)


def is_drawn(grid_ref, bit):
    drawn = jnp.bool_(False)
    for number in range(grid_ref.shape[0]):
        drawn = drawn | (grid_ref[number, 0] == (1 << bit))
    return drawn


def add_pairs(scales, shift, own_ref, rows, others, before_ref, out_ref, weights_ref, raw_ref=None, matched=False):
    first, block = rows
    own = own_ref[first : first + block, :]
    pieces = strips(block, SLICE)
    places, left = [], 0
    for (scale, factor), other_ref in zip(scales, others):
        count, width = other_ref.shape
        for top, bottom in strips(count, STRIP):
            products = lax.dot_general(
                own, other_ref[top:bottom, :], (((1,), (1,)), ((), ())),
                preferred_element_type=jnp.float32,
            )
            for low, high in pieces:
                weights_ref[first + low : first + high, left + top : left + bottom] = coupled(
                    products[low:high], scale, factor, shift, (first + low, top) if matched else None
                )
        places.append(slice(left, left + count))
        left += count
    sums = [[0.0, 0.0] for _ in pieces]
    for top, bottom in strips(width, COLUMNS):
        total = None
        for place, other_ref in zip(places, others):
            added = jnp.dot(
                weights_ref[first : first + block, place], other_ref[:, top:bottom],
                preferred_element_type=jnp.float32,
            )
            total = added if total is None else total + added
        for number, (low, high) in enumerate(pieces):
            part = total[low:high]
            here = slice(first + low, first + high)
            if before_ref is not None:
                part = part + before_ref[here, top:bottom]
            out_ref[here, top:bottom] = part
            if raw_ref is not None:
                raw = raw_ref[here, top:bottom]
                for side in range(0, bottom - top, LANES):
                    lanes = slice(side, side + LANES)
                    sums[number][0] += raw[:, lanes] * raw[:, lanes]
                    sums[number][1] += raw[:, lanes] * part[:, lanes]
    return sums


def blocks_of(count):
    return [(first, min(BLOCK, count - first)) for first in range(0, count, BLOCK)]


def scales_of(bits, scale_ref, grid_ref):
    scale = scale_ref[0]
    return [
        (scale, scale if bit is None else jnp.where(is_drawn(grid_ref, bit), scale, 0.0))
        for bit in bits
    ]


def diagonal_kernel(scale_ref, shift_ref, image_ref, text_ref, image_sum_ref, text_sum_ref, weights_ref):
    scale, shift = scale_ref[0], shift_ref[0]
    row_count, width = image_ref.shape
    for rows in blocks_of(row_count):
        add_pairs(
            [(scale, scale)], shift, image_ref, rows, [text_ref], None, image_sum_ref, weights_ref,
            matched=True,
        )
    for first, last in strips(row_count, STRIP):
        for left, right in strips(width, COLUMNS):
            text_sum_ref[first:last, left:right] = lax.dot_general(
                weights_ref[:, first:last], image_ref[:, left:right], (((0,), (0,)), ((), ())),
                preferred_element_type=jnp.float32,
            )


def diagonal(scale, shift, image_half, text_half):
    rows, width = image_half.shape
    return call(
        diagonal_kernel,
        "diagonal",
        [scale, shift, image_half, text_half],
        [((rows, width), jnp.float32)] * 2,
        (rows, 2 * rows, width),
        scratch=[pltpu.VMEM((rows, rows), jnp.bfloat16)],
    )


def near_kernel(
    bit, scale_ref, shift_ref, grid_ref, image_ref, text_ref, image_sum_ref, text_sum_ref, texts_ref,
    images_ref, image_out_ref, text_out_ref, weights_ref,
):
    scales, shift = scales_of([bit], scale_ref, grid_ref), shift_ref[0]
    row_count = image_ref.shape[0]
    for rows in blocks_of(row_count):
        add_pairs(
            scales, shift, image_ref, rows, [texts_ref], image_sum_ref, image_out_ref, weights_ref
        )
    for rows in blocks_of(row_count):
        add_pairs(
            scales, shift, text_ref, rows, [images_ref], text_sum_ref, text_out_ref, weights_ref
        )


def add_near(scale, shift, grid, image_half, text_half, image_sum, text_sum, texts, images, bit):
    rows, width = image_half.shape
    return call(
        functools.partial(near_kernel, bit),
        "add_near",
        [scale, shift, grid, image_half, text_half, image_sum, text_sum, texts, images],
        [((rows, width), jnp.float32)] * 2,
        (rows, 2 * rows, width),
        smem=3,
        scratch=[pltpu.VMEM((rows, rows), jnp.bfloat16)],
    )


def add_up_kernel(bits, scale_ref, shift_ref, grid_ref, own_ref, sum_ref, *refs):
    *other_refs, out_ref, weights_ref = refs
    scales = scales_of(bits, scale_ref, grid_ref)
    for rows in blocks_of(own_ref.shape[0]):
        add_pairs(scales, shift_ref[0], own_ref, rows, other_refs, sum_ref, out_ref, weights_ref)


def add_up(scale, shift, grid, own, total, others, bits):
    rows, width = own.shape
    count = sum(x.shape[0] for x in others)
    return call(
        functools.partial(add_up_kernel, tuple(bits)),
        "add_up",
        [scale, shift, grid, own, total, *others],
        [((rows, width), jnp.float32)],
        (rows, count, width),
        smem=3,
        scratch=[pltpu.VMEM((rows, count), jnp.bfloat16)],
    )[0]


def finish_kernel(bits, scale_ref, shift_ref, grid_ref, own_ref, raw_ref, sum_ref, *refs):
    *other_refs, out_ref, weights_ref, total_ref, sems = refs
    scales = scales_of(bits, scale_ref, grid_ref)
    copies = []
    for first, block in blocks_of(own_ref.shape[0]):
        sums = add_pairs(
            scales, shift_ref[0], own_ref, (first, block), other_refs, sum_ref, total_ref, weights_ref,
            raw_ref,
        )
        for (squares, products), (low, high) in zip(sums, strips(block, SLICE)):
            inverse = lax.rsqrt(jnp.sum(squares, axis=-1, keepdims=True) + epsilon)
            radial = jnp.sum(products, axis=-1, keepdims=True) * (inverse * inverse * inverse)
            here = pl.ds(first + low, high - low)
            for top, bottom in strips(own_ref.shape[1], COLUMNS):
                total_ref[here, top:bottom] = (
                    total_ref[here, top:bottom] * inverse - raw_ref[here, top:bottom] * radial
                )
            copy = pltpu.make_async_copy(
                total_ref.at[here, :], out_ref.at[here, :], sems.at[len(copies)]
            )
            copy.start()
            copies.append(copy)
    for copy in copies:
        copy.wait()


def finish(scale, shift, grid, own, raw, total, others, bits):
    rows, width = own.shape
    count = sum(x.shape[0] for x in others)
    return call(
        functools.partial(finish_kernel, tuple(bits)),
        "finish",
        [scale, shift, grid, own, raw, total, *others],
        [((rows, width), jnp.float32)],
        (rows, count, width),
        smem=3,
        out_specs=[pl.BlockSpec(memory_space=pl.ANY)],
        scratch=[
            pltpu.VMEM((rows, count), jnp.bfloat16),
            pltpu.VMEM((rows, width), jnp.float32),
            pltpu.SemaphoreType.DMA((len(strips(rows, SLICE)),)),
        ],
    )[0]


def passed_along(x, axis, by):
    count = lax.axis_size(axis)
    return lax.ppermute(x, axis, [(i, (i + by) % count) for i in range(count)])


def exchanged(x, bit):
    count = lax.axis_size("blk")
    return lax.ppermute(x, "blk", [(i, i ^ (1 << bit)) for i in range(count)])


def with_partners(bits, visual, caption, grid, scale, shift):
    cut = visual.shape[0] * 3 // 4
    near, far = [bit for bit in bits if bit == 0], [bit for bit in bits if bit != 0]
    text_half = normalized(caption)
    text_z = passed_along(text_half, "group", 1)
    far_texts = [exchanged(text_half, bit) for bit in far]
    image_half = normalized(visual)
    image_first, image_last = image_half[:cut], image_half[cut:]
    boths = [(exchanged(text_half, bit), exchanged(image_half, bit)) for bit in near]
    image_sum, text_sum = diagonal(scale, shift, image_half, text_half)
    image_first, image_last, text_z, image_sum, text_sum = lax.optimization_barrier(
        (image_first, image_last, text_z, image_sum, text_sum)
    )
    image_z_first = passed_along(image_first, "group", -1)
    image_z_last = passed_along(image_last, "group", -1)
    far_images_first = [exchanged(image_first, bit) for bit in far]
    for (texts, images), bit in zip(boths, near):
        image_sum, text_sum = add_near(
            scale, shift, grid, image_half, text_half, image_sum, text_sum, texts, images, bit
        )
    image_gradient = finish(
        scale, shift, grid, image_half, visual, image_sum, [*far_texts, text_z], [*far, None]
    )
    text_sum, image_last, image_gradient = lax.optimization_barrier(
        (text_sum, image_last, image_gradient)
    )
    far_images_last = [exchanged(image_last, bit) for bit in far[:1]]
    image_last, image_z_first = lax.optimization_barrier((image_last, image_z_first))
    far_images_last += [exchanged(image_last, bit) for bit in far[1:]]
    text_sum = add_up(
        scale, shift, grid, text_half, text_sum, [*far_images_first, image_z_first], [*far, None]
    )
    text_gradient = finish(
        scale, shift, grid, text_half, caption, text_sum,
        [*far_images_last, image_z_last], [*far, None],
    )
    return image_gradient, text_gradient


def on_device(
    visual_encoder_outputs,
    caption_encoder_outputs,
    partner_lookup_grid,
    sharpness_coefficient,
    sigmoid_shift_term,
):
    rounds, peers = partner_lookup_grid.shape
    bits = range(peers.bit_length() - 1)
    operands = (
        visual_encoder_outputs,
        caption_encoder_outputs,
        partner_lookup_grid,
        sharpness_coefficient,
        sigmoid_shift_term,
    )
    if len(bits) <= rounds + 1:
        return with_partners(bits, *operands)
    choices = list(itertools.combinations(bits, rounds))
    union = jnp.sum(partner_lookup_grid[:, 0])
    branch = jnp.int32(0)
    for number, choice in enumerate(choices):
        branch = jnp.where(union == sum(1 << bit for bit in choice), jnp.int32(number), branch)
    return lax.switch(
        branch, [functools.partial(with_partners, choice) for choice in choices], *operands
    )


def solution(mesh):
    placed = (P(("blk", "group"), None), P(("blk", "group"), None), P(), P(), P())
    return jax.shard_map(
        on_device,
        mesh=mesh,
        in_specs=placed,
        out_specs=(P(("blk", "group"), None), P(("blk", "group"), None)),
        check_vma=False,
    )
```

```python
import functools
import itertools

import jax
import jax.numpy as jnp
from jax import lax
from jax.experimental import pallas as pl
from jax.experimental.pallas import tpu as pltpu
from jax.sharding import PartitionSpec as P

epsilon = 1e-06
log2_e = 1.4426950408889634
MIB = 1024 * 1024
VMEM = pl.BlockSpec(memory_space=pltpu.VMEM)
SMEM = pl.BlockSpec(memory_space=pltpu.SMEM)
BLOCK, STRIP, COLUMNS, SLICE, LANES = 256, 256, 256, 64, 128


def cost(rows, other_rows, width):
    return pl.CostEstimate(
        flops=4 * rows * max(other_rows, 1) * width,
        bytes_accessed=8 * rows * width,
        transcendentals=2 * rows * other_rows,
    )


def call(body, name, operands, outs, work, smem=2, grid=None, out_specs=None, scratch=()):
    return pl.pallas_call(
        body,
        grid=grid or (),
        in_specs=[SMEM] * smem + [VMEM] * (len(operands) - smem),
        out_specs=out_specs or [VMEM] * len(outs),
        out_shape=[jax.ShapeDtypeStruct(shape, dtype) for shape, dtype in outs],
        scratch_shapes=list(scratch),
        name=name,
        compiler_params=pltpu.CompilerParams(vmem_limit_bytes=24 * MIB),
        cost_estimate=cost(*work),
    )(*operands)


def strips(count, size):
    return [(first, min(first + size, count)) for first in range(0, count, size)]


def normalized(raw):
    total = jnp.sum(raw * raw, axis=-1, keepdims=True)
    return (raw * lax.rsqrt(total + epsilon)).astype(jnp.bfloat16)


def coupled(products, scale, factor, shift, places=None):
    powers = products * (-log2_e * scale) - log2_e * shift
    if places is not None:
        row = places[0] + lax.broadcasted_iota(jnp.int32, powers.shape, 0)
        column = places[1] + lax.broadcasted_iota(jnp.int32, powers.shape, 1)
        same = row == column
        powers = jnp.where(same, -powers, powers)
    below = 1.0 + jnp.exp2(powers)
    inverse = pl.reciprocal(below, approx=True)
    weights = factor * (inverse * (2.0 - below * inverse))
    if places is not None:
        weights = jnp.where(same, -weights, weights)
    return weights.astype(jnp.bfloat16)


def is_drawn(grid_ref, bit):
    drawn = jnp.bool_(False)
    for number in range(grid_ref.shape[0]):
        drawn = drawn | (grid_ref[number, 0] == (1 << bit))
    return drawn


def add_pairs(scales, shift, own_ref, rows, others, before_ref, out_ref, weights_ref, raw_ref=None, matched=False):
    first, block = rows
    own = own_ref[first : first + block, :]
    pieces = strips(block, SLICE)
    places, left = [], 0
    for (scale, factor), other_ref in zip(scales, others):
        count, width = other_ref.shape
        for top, bottom in strips(count, STRIP):
            products = lax.dot_general(
                own, other_ref[top:bottom, :], (((1,), (1,)), ((), ())),
                preferred_element_type=jnp.float32,
            )
            for low, high in pieces:
                weights_ref[first + low : first + high, left + top : left + bottom] = coupled(
                    products[low:high], scale, factor, shift, (first + low, top) if matched else None
                )
        places.append(slice(left, left + count))
        left += count
    sums = [[0.0, 0.0] for _ in pieces]
    for top, bottom in strips(width, COLUMNS):
        total = None
        for place, other_ref in zip(places, others):
            added = jnp.dot(
                weights_ref[first : first + block, place], other_ref[:, top:bottom],
                preferred_element_type=jnp.float32,
            )
            total = added if total is None else total + added
        for number, (low, high) in enumerate(pieces):
            part = total[low:high]
            here = slice(first + low, first + high)
            if before_ref is not None:
                part = part + before_ref[here, top:bottom]
            out_ref[here, top:bottom] = part
            if raw_ref is not None:
                raw = raw_ref[here, top:bottom]
                for side in range(0, bottom - top, LANES):
                    lanes = slice(side, side + LANES)
                    sums[number][0] += raw[:, lanes] * raw[:, lanes]
                    sums[number][1] += raw[:, lanes] * part[:, lanes]
    return sums


def blocks_of(count, size=BLOCK):
    return [(first, min(size, count - first)) for first in range(0, count, size)]


def scales_of(bits, scale_ref, grid_ref):
    scale = scale_ref[0]
    return [
        (scale, scale if bit is None else jnp.where(is_drawn(grid_ref, bit), scale, 0.0))
        for bit in bits
    ]


def diagonal_kernel(scale_ref, shift_ref, image_ref, text_ref, image_sum_ref, text_sum_ref, weights_ref):
    scale, shift = scale_ref[0], shift_ref[0]
    row_count, width = image_ref.shape
    for rows in blocks_of(row_count):
        add_pairs(
            [(scale, scale)], shift, image_ref, rows, [text_ref], None, image_sum_ref, weights_ref,
            matched=True,
        )
    for first, last in strips(row_count, STRIP):
        for left, right in strips(width, COLUMNS):
            text_sum_ref[first:last, left:right] = lax.dot_general(
                weights_ref[:, first:last], image_ref[:, left:right], (((0,), (0,)), ((), ())),
                preferred_element_type=jnp.float32,
            )


def diagonal(scale, shift, image_half, text_half):
    rows, width = image_half.shape
    return call(
        diagonal_kernel,
        "diagonal",
        [scale, shift, image_half, text_half],
        [((rows, width), jnp.float32)] * 2,
        (rows, 2 * rows, width),
        scratch=[pltpu.VMEM((rows, rows), jnp.bfloat16)],
    )


def near_kernel(
    bit, scale_ref, shift_ref, grid_ref, image_ref, text_ref, image_sum_ref, text_sum_ref, texts_ref,
    images_ref, image_out_ref, text_out_ref, weights_ref,
):
    scales, shift = scales_of([bit], scale_ref, grid_ref), shift_ref[0]
    row_count = image_ref.shape[0]
    for rows in blocks_of(row_count):
        add_pairs(
            scales, shift, image_ref, rows, [texts_ref], image_sum_ref, image_out_ref, weights_ref
        )
    for rows in blocks_of(row_count):
        add_pairs(
            scales, shift, text_ref, rows, [images_ref], text_sum_ref, text_out_ref, weights_ref
        )


def add_near(scale, shift, grid, image_half, text_half, image_sum, text_sum, texts, images, bit):
    rows, width = image_half.shape
    return call(
        functools.partial(near_kernel, bit),
        "add_near",
        [scale, shift, grid, image_half, text_half, image_sum, text_sum, texts, images],
        [((rows, width), jnp.float32)] * 2,
        (rows, 2 * rows, width),
        smem=3,
        scratch=[pltpu.VMEM((rows, rows), jnp.bfloat16)],
    )


def add_up_kernel(bits, scale_ref, shift_ref, grid_ref, own_ref, sum_ref, *refs):
    *other_refs, out_ref, weights_ref = refs
    scales = scales_of(bits, scale_ref, grid_ref)
    for rows in blocks_of(own_ref.shape[0]):
        add_pairs(scales, shift_ref[0], own_ref, rows, other_refs, sum_ref, out_ref, weights_ref)


def add_up(scale, shift, grid, own, total, others, bits):
    rows, width = own.shape
    count = sum(x.shape[0] for x in others)
    return call(
        functools.partial(add_up_kernel, tuple(bits)),
        "add_up",
        [scale, shift, grid, own, total, *others],
        [((rows, width), jnp.float32)],
        (rows, count, width),
        smem=3,
        scratch=[pltpu.VMEM((rows, count), jnp.bfloat16)],
    )[0]


def finish_kernel(bits, scale_ref, shift_ref, grid_ref, own_ref, raw_ref, sum_ref, *refs):
    *other_refs, out_ref, weights_ref, total_ref, sems = refs
    scales = scales_of(bits, scale_ref, grid_ref)
    copies = []
    for first, block in blocks_of(own_ref.shape[0], BLOCK // 2):
        sums = add_pairs(
            scales, shift_ref[0], own_ref, (first, block), other_refs, sum_ref, total_ref, weights_ref,
            raw_ref,
        )
        for (squares, products), (low, high) in zip(sums, strips(block, SLICE)):
            inverse = lax.rsqrt(jnp.sum(squares, axis=-1, keepdims=True) + epsilon)
            radial = jnp.sum(products, axis=-1, keepdims=True) * (inverse * inverse * inverse)
            here = slice(first + low, first + high)
            for top, bottom in strips(own_ref.shape[1], COLUMNS):
                total_ref[here, top:bottom] = (
                    total_ref[here, top:bottom] * inverse - raw_ref[here, top:bottom] * radial
                )
        rows = pl.ds(first, block)
        copy = pltpu.make_async_copy(
            total_ref.at[rows, :], out_ref.at[rows, :], sems.at[len(copies)]
        )
        copy.start()
        copies.append(copy)
    for copy in copies:
        copy.wait()


def finish(scale, shift, grid, own, raw, total, others, bits):
    rows, width = own.shape
    count = sum(x.shape[0] for x in others)
    return call(
        functools.partial(finish_kernel, tuple(bits)),
        "finish",
        [scale, shift, grid, own, raw, total, *others],
        [((rows, width), jnp.float32)],
        (rows, count, width),
        smem=3,
        out_specs=[pl.BlockSpec(memory_space=pl.ANY)],
        scratch=[
            pltpu.VMEM((rows, count), jnp.bfloat16),
            pltpu.VMEM((rows, width), jnp.float32),
            pltpu.SemaphoreType.DMA((len(blocks_of(rows, BLOCK // 2)),)),
        ],
    )[0]


def passed_along(x, axis, by):
    count = lax.axis_size(axis)
    return lax.ppermute(x, axis, [(i, (i + by) % count) for i in range(count)])


def exchanged(x, bit):
    count = lax.axis_size("blk")
    return lax.ppermute(x, "blk", [(i, i ^ (1 << bit)) for i in range(count)])


def with_partners(bits, visual, caption, grid, scale, shift):
    cut = visual.shape[0] // 2
    near, far = [bit for bit in bits if bit == 0], [bit for bit in bits if bit != 0]
    text_half = normalized(caption)
    text_z = passed_along(text_half, "group", 1)
    far_texts = [exchanged(text_half, bit) for bit in far]
    image_half = normalized(visual)
    image_first, image_last = image_half[:cut], image_half[cut:]
    boths = [(exchanged(text_half, bit), exchanged(image_half, bit)) for bit in near]
    image_sum, text_sum = diagonal(scale, shift, image_half, text_half)
    image_half, image_first, image_last, text_z, image_sum, text_sum = lax.optimization_barrier(
        (image_half, image_first, image_last, text_z, image_sum, text_sum)
    )
    image_z = passed_along(image_half, "group", -1)
    far_images_first = [exchanged(image_first, bit) for bit in far]
    for (texts, images), bit in zip(boths, near):
        image_sum, text_sum = add_near(
            scale, shift, grid, image_half, text_half, image_sum, text_sum, texts, images, bit
        )
    image_last, far_texts = lax.optimization_barrier((image_last, far_texts))
    far_images_last = [exchanged(image_last, bit) for bit in far]
    image_gradient = finish(
        scale, shift, grid, image_half, visual, image_sum, [*far_texts, text_z], [*far, None]
    )
    text_sum, image_gradient = lax.optimization_barrier((text_sum, image_gradient))
    if far:
        text_sum = add_up(scale, shift, grid, text_half, text_sum, far_images_first, far)
    text_gradient = finish(
        scale, shift, grid, text_half, caption, text_sum, [*far_images_last, image_z], [*far, None]
    )
    return image_gradient, text_gradient


def on_device(
    visual_encoder_outputs,
    caption_encoder_outputs,
    partner_lookup_grid,
    sharpness_coefficient,
    sigmoid_shift_term,
):
    rounds, peers = partner_lookup_grid.shape
    bits = range(peers.bit_length() - 1)
    operands = (
        visual_encoder_outputs,
        caption_encoder_outputs,
        partner_lookup_grid,
        sharpness_coefficient,
        sigmoid_shift_term,
    )
    if len(bits) <= rounds + 1:
        return with_partners(bits, *operands)
    choices = list(itertools.combinations(bits, rounds))
    union = jnp.sum(partner_lookup_grid[:, 0])
    branch = jnp.int32(0)
    for number, choice in enumerate(choices):
        branch = jnp.where(union == sum(1 << bit for bit in choice), jnp.int32(number), branch)
    return lax.switch(
        branch, [functools.partial(with_partners, choice) for choice in choices], *operands
    )


def solution(mesh):
    placed = (P(("blk", "group"), None), P(("blk", "group"), None), P(), P(), P())
    return jax.shard_map(
        on_device,
        mesh=mesh,
        in_specs=placed,
        out_specs=(P(("blk", "group"), None), P(("blk", "group"), None)),
        check_vma=False,
    )
```

```python
import functools
import itertools

import jax
import jax.numpy as jnp
from jax import lax
from jax.experimental import pallas as pl
from jax.experimental.pallas import tpu as pltpu
from jax.sharding import PartitionSpec as P

epsilon = 1e-06
log2_e = 1.4426950408889634
MIB = 1024 * 1024
VMEM = pl.BlockSpec(memory_space=pltpu.VMEM)
SMEM = pl.BlockSpec(memory_space=pltpu.SMEM)
BLOCK, STRIP, COLUMNS, SLICE, LANES = 256, 256, 256, 64, 128


def cost(rows, other_rows, width):
    return pl.CostEstimate(
        flops=4 * rows * max(other_rows, 1) * width,
        bytes_accessed=8 * rows * width,
        transcendentals=2 * rows * other_rows,
    )


def call(body, name, operands, outs, work, smem=2, grid=None, out_specs=None, scratch=()):
    return pl.pallas_call(
        body,
        grid=grid or (),
        in_specs=[SMEM] * smem + [VMEM] * (len(operands) - smem),
        out_specs=out_specs or [VMEM] * len(outs),
        out_shape=[jax.ShapeDtypeStruct(shape, dtype) for shape, dtype in outs],
        scratch_shapes=list(scratch),
        name=name,
        compiler_params=pltpu.CompilerParams(vmem_limit_bytes=24 * MIB),
        cost_estimate=cost(*work),
    )(*operands)


def strips(count, size):
    return [(first, min(first + size, count)) for first in range(0, count, size)]


def normalized(raw):
    total = jnp.sum(raw * raw, axis=-1, keepdims=True)
    return (raw * lax.rsqrt(total + epsilon)).astype(jnp.bfloat16)


def coupled(products, scale, factor, shift, places=None):
    powers = products * (-log2_e * scale) - log2_e * shift
    if places is not None:
        row = places[0] + lax.broadcasted_iota(jnp.int32, powers.shape, 0)
        column = places[1] + lax.broadcasted_iota(jnp.int32, powers.shape, 1)
        same = row == column
        powers = jnp.where(same, -powers, powers)
    below = 1.0 + jnp.exp2(powers)
    inverse = pl.reciprocal(below, approx=True)
    weights = factor * (inverse * (2.0 - below * inverse))
    if places is not None:
        weights = jnp.where(same, -weights, weights)
    return weights.astype(jnp.bfloat16)


def is_drawn(grid_ref, bit):
    drawn = jnp.bool_(False)
    for number in range(grid_ref.shape[0]):
        drawn = drawn | (grid_ref[number, 0] == (1 << bit))
    return drawn


def side_by_side(others, all_ref):
    if all_ref is None:
        return others
    left = 0
    for other_ref in others:
        count = other_ref.shape[0]
        all_ref[left : left + count, :] = other_ref[...]
        left += count
    return [all_ref]


def factors_of(factors, counts, top, bottom):
    last, column = None, None
    edge = 0
    for factor, count in zip(factors, counts):
        if top < edge + count and edge < bottom:
            if last is None:
                last = factor
            else:
                if column is None:
                    column = top + lax.broadcasted_iota(jnp.int32, (1, bottom - top), 1)
                last = jnp.where(column < edge, last, factor)
        edge += count
    return last


def add_pairs(
    scale, factors, shift, own_ref, rows, counts, others, before_ref, out_ref, weights_ref,
    raw_ref=None, matched=False,
):
    first, block = rows
    own = own_ref[first : first + block, :]
    pieces = strips(block, SLICE)
    places, left = [], 0
    for other_ref in others:
        count, width = other_ref.shape
        for top, bottom in strips(count, STRIP):
            products = lax.dot_general(
                own, other_ref[top:bottom, :], (((1,), (1,)), ((), ())),
                preferred_element_type=jnp.float32,
            )
            factor = factors_of(factors, counts, left + top, left + bottom)
            for low, high in pieces:
                weights_ref[first + low : first + high, left + top : left + bottom] = coupled(
                    products[low:high], scale, factor, shift, (first + low, top) if matched else None
                )
        places.append(slice(left, left + count))
        left += count
    sums = [[0.0, 0.0] for _ in pieces]
    for top, bottom in strips(width, COLUMNS):
        total = None
        for place, other_ref in zip(places, others):
            added = jnp.dot(
                weights_ref[first : first + block, place], other_ref[:, top:bottom],
                preferred_element_type=jnp.float32,
            )
            total = added if total is None else total + added
        for number, (low, high) in enumerate(pieces):
            part = total[low:high]
            here = slice(first + low, first + high)
            if before_ref is not None:
                part = part + before_ref[here, top:bottom]
            out_ref[here, top:bottom] = part
            if raw_ref is not None:
                raw = raw_ref[here, top:bottom]
                for side in range(0, bottom - top, LANES):
                    lanes = slice(side, side + LANES)
                    sums[number][0] += raw[:, lanes] * raw[:, lanes]
                    sums[number][1] += raw[:, lanes] * part[:, lanes]
    return sums


def blocks_of(count):
    return [(first, min(BLOCK, count - first)) for first in range(0, count, BLOCK)]


def drawn_factors(bits, scale_ref, grid_ref):
    scale = scale_ref[0]
    return [
        scale if bit is None else jnp.where(is_drawn(grid_ref, bit), scale, 0.0) for bit in bits
    ]


def all_scratch(others):
    count, width = sum(x.shape[0] for x in others), others[0].shape[1]
    if all(x.shape[0] % STRIP == 0 for x in others):
        return []
    return [pltpu.VMEM((count, width), jnp.bfloat16)]


def diagonal_kernel(scale_ref, shift_ref, image_ref, text_ref, image_sum_ref, text_sum_ref, weights_ref):
    scale, shift = scale_ref[0], shift_ref[0]
    row_count, width = image_ref.shape
    for rows in blocks_of(row_count):
        add_pairs(
            scale, [scale], shift, image_ref, rows, [row_count], [text_ref], None, image_sum_ref,
            weights_ref, matched=True,
        )
    for first, last in strips(row_count, STRIP):
        for left, right in strips(width, COLUMNS):
            text_sum_ref[first:last, left:right] = lax.dot_general(
                weights_ref[:, first:last], image_ref[:, left:right], (((0,), (0,)), ((), ())),
                preferred_element_type=jnp.float32,
            )


def diagonal(scale, shift, image_half, text_half):
    rows, width = image_half.shape
    return call(
        diagonal_kernel,
        "diagonal",
        [scale, shift, image_half, text_half],
        [((rows, width), jnp.float32)] * 2,
        (rows, 2 * rows, width),
        scratch=[pltpu.VMEM((rows, rows), jnp.bfloat16)],
    )


def near_kernel(
    bit, scale_ref, shift_ref, grid_ref, image_ref, text_ref, image_sum_ref, text_sum_ref, texts_ref,
    images_ref, image_out_ref, text_out_ref, weights_ref,
):
    scale, shift = scale_ref[0], shift_ref[0]
    factors = drawn_factors([bit], scale_ref, grid_ref)
    row_count = image_ref.shape[0]
    for own_ref, other_ref, sum_ref, out_ref in (
        (image_ref, texts_ref, image_sum_ref, image_out_ref),
        (text_ref, images_ref, text_sum_ref, text_out_ref),
    ):
        for rows in blocks_of(row_count):
            add_pairs(
                scale, factors, shift, own_ref, rows, [row_count], [other_ref], sum_ref, out_ref,
                weights_ref,
            )


def add_near(scale, shift, grid, image_half, text_half, image_sum, text_sum, texts, images, bit):
    rows, width = image_half.shape
    return call(
        functools.partial(near_kernel, bit),
        "add_near",
        [scale, shift, grid, image_half, text_half, image_sum, text_sum, texts, images],
        [((rows, width), jnp.float32)] * 2,
        (rows, 2 * rows, width),
        smem=3,
        scratch=[pltpu.VMEM((rows, rows), jnp.bfloat16)],
    )


def add_up_kernel(bits, scale_ref, shift_ref, grid_ref, own_ref, sum_ref, *refs):
    other_refs, (out_ref, weights_ref, *all_refs) = refs[: len(bits)], refs[len(bits) :]
    factors = drawn_factors(bits, scale_ref, grid_ref)
    counts = [x.shape[0] for x in other_refs]
    others = side_by_side(other_refs, *(all_refs or [None]))
    for rows in blocks_of(own_ref.shape[0]):
        add_pairs(
            scale_ref[0], factors, shift_ref[0], own_ref, rows, counts, others, sum_ref, out_ref,
            weights_ref,
        )


def add_up(scale, shift, grid, own, total, others, bits):
    rows, width = own.shape
    count = sum(x.shape[0] for x in others)
    return call(
        functools.partial(add_up_kernel, tuple(bits)),
        "add_up",
        [scale, shift, grid, own, total, *others],
        [((rows, width), jnp.float32)],
        (rows, count, width),
        smem=3,
        scratch=[pltpu.VMEM((rows, count), jnp.bfloat16), *all_scratch(others)],
    )[0]


def finish_kernel(bits, scale_ref, shift_ref, grid_ref, own_ref, raw_ref, sum_ref, *refs):
    other_refs, (out_ref, weights_ref, total_ref, sems, *all_refs) = refs[: len(bits)], refs[len(bits) :]
    factors = drawn_factors(bits, scale_ref, grid_ref)
    counts = [x.shape[0] for x in other_refs]
    others = side_by_side(other_refs, *(all_refs or [None]))
    copies = []
    for first, block in blocks_of(own_ref.shape[0]):
        sums = add_pairs(
            scale_ref[0], factors, shift_ref[0], own_ref, (first, block), counts, others, sum_ref,
            total_ref, weights_ref, raw_ref,
        )
        for (squares, products), (low, high) in zip(sums, strips(block, SLICE)):
            inverse = lax.rsqrt(jnp.sum(squares, axis=-1, keepdims=True) + epsilon)
            radial = jnp.sum(products, axis=-1, keepdims=True) * (inverse * inverse * inverse)
            here = pl.ds(first + low, high - low)
            for top, bottom in strips(own_ref.shape[1], COLUMNS):
                total_ref[here, top:bottom] = (
                    total_ref[here, top:bottom] * inverse - raw_ref[here, top:bottom] * radial
                )
            copy = pltpu.make_async_copy(
                total_ref.at[here, :], out_ref.at[here, :], sems.at[len(copies)]
            )
            copy.start()
            copies.append(copy)
    for copy in copies:
        copy.wait()


def finish(scale, shift, grid, own, raw, total, others, bits):
    rows, width = own.shape
    count = sum(x.shape[0] for x in others)
    return call(
        functools.partial(finish_kernel, tuple(bits)),
        "finish",
        [scale, shift, grid, own, raw, total, *others],
        [((rows, width), jnp.float32)],
        (rows, count, width),
        smem=3,
        out_specs=[pl.BlockSpec(memory_space=pl.ANY)],
        scratch=[
            pltpu.VMEM((rows, count), jnp.bfloat16),
            pltpu.VMEM((rows, width), jnp.float32),
            pltpu.SemaphoreType.DMA((len(strips(rows, SLICE)),)),
            *all_scratch(others),
        ],
    )[0]


def passed_along(x, axis, by):
    count = lax.axis_size(axis)
    return lax.ppermute(x, axis, [(i, (i + by) % count) for i in range(count)])


def exchanged(x, bit):
    count = lax.axis_size("blk")
    return lax.ppermute(x, "blk", [(i, i ^ (1 << bit)) for i in range(count)])


def with_partners(bits, visual, caption, grid, scale, shift):
    cut = visual.shape[0] * 3 // 4
    near, far = [bit for bit in bits if bit == 0], [bit for bit in bits if bit != 0]
    text_half = normalized(caption)
    text_z = passed_along(text_half, "group", 1)
    far_texts = [exchanged(text_half, bit) for bit in far]
    image_half = normalized(visual)
    image_first, image_last = image_half[:cut], image_half[cut:]
    boths = [(exchanged(text_half, bit), exchanged(image_half, bit)) for bit in near]
    image_sum, text_sum = diagonal(scale, shift, image_half, text_half)
    image_first, image_last, text_z, image_sum, text_sum = lax.optimization_barrier(
        (image_first, image_last, text_z, image_sum, text_sum)
    )
    image_z_first = passed_along(image_first, "group", -1)
    image_z_last = passed_along(image_last, "group", -1)
    far_images_first = [exchanged(image_first, bit) for bit in far]
    for (texts, images), bit in zip(boths, near):
        image_sum, text_sum = add_near(
            scale, shift, grid, image_half, text_half, image_sum, text_sum, texts, images, bit
        )
    image_gradient = finish(
        scale, shift, grid, image_half, visual, image_sum, [*far_texts, text_z], [*far, None]
    )
    text_sum, image_last, image_gradient = lax.optimization_barrier(
        (text_sum, image_last, image_gradient)
    )
    far_images_last = [exchanged(image_last, bit) for bit in far[:1]]
    image_last, image_z_first = lax.optimization_barrier((image_last, image_z_first))
    far_images_last += [exchanged(image_last, bit) for bit in far[1:]]
    text_sum = add_up(
        scale, shift, grid, text_half, text_sum, [*far_images_first, image_z_first], [*far, None]
    )
    text_gradient = finish(
        scale, shift, grid, text_half, caption, text_sum,
        [*far_images_last, image_z_last], [*far, None],
    )
    return image_gradient, text_gradient


def on_device(
    visual_encoder_outputs,
    caption_encoder_outputs,
    partner_lookup_grid,
    sharpness_coefficient,
    sigmoid_shift_term,
):
    rounds, peers = partner_lookup_grid.shape
    bits = range(peers.bit_length() - 1)
    operands = (
        visual_encoder_outputs,
        caption_encoder_outputs,
        partner_lookup_grid,
        sharpness_coefficient,
        sigmoid_shift_term,
    )
    if len(bits) <= rounds + 1:
        return with_partners(bits, *operands)
    choices = list(itertools.combinations(bits, rounds))
    union = jnp.sum(partner_lookup_grid[:, 0])
    branch = jnp.int32(0)
    for number, choice in enumerate(choices):
        branch = jnp.where(union == sum(1 << bit for bit in choice), jnp.int32(number), branch)
    return lax.switch(
        branch, [functools.partial(with_partners, choice) for choice in choices], *operands
    )


def solution(mesh):
    placed = (P(("blk", "group"), None), P(("blk", "group"), None), P(), P(), P())
    return jax.shard_map(
        on_device,
        mesh=mesh,
        in_specs=placed,
        out_specs=(P(("blk", "group"), None), P(("blk", "group"), None)),
        check_vma=False,
    )
```

```python
import functools
import itertools

import jax
import jax.numpy as jnp
from jax import lax
from jax.experimental import pallas as pl
from jax.experimental.pallas import tpu as pltpu
from jax.sharding import PartitionSpec as P

epsilon = 1e-06
log2_e = 1.4426950408889634
MIB = 1024 * 1024
VMEM = pl.BlockSpec(memory_space=pltpu.VMEM)
SMEM = pl.BlockSpec(memory_space=pltpu.SMEM)
BLOCK, STRIP, COLUMNS, SLICE, LANES = 256, 256, 256, 64, 128


def cost(rows, other_rows, width):
    return pl.CostEstimate(
        flops=4 * rows * max(other_rows, 1) * width,
        bytes_accessed=8 * rows * width,
        transcendentals=2 * rows * other_rows,
    )


def call(body, name, operands, outs, work, smem=2, grid=None, out_specs=None, scratch=()):
    return pl.pallas_call(
        body,
        grid=grid or (),
        in_specs=[SMEM] * smem + [VMEM] * (len(operands) - smem),
        out_specs=out_specs or [VMEM] * len(outs),
        out_shape=[jax.ShapeDtypeStruct(shape, dtype) for shape, dtype in outs],
        scratch_shapes=list(scratch),
        name=name,
        compiler_params=pltpu.CompilerParams(vmem_limit_bytes=24 * MIB),
        cost_estimate=cost(*work),
    )(*operands)


def strips(count, size):
    return [(first, min(first + size, count)) for first in range(0, count, size)]


def normalized(raw):
    total = jnp.sum(raw * raw, axis=-1, keepdims=True)
    return (raw * lax.rsqrt(total + epsilon)).astype(jnp.bfloat16)


def halves_kernel(raw_ref, half_ref, held_ref, ready_ref, in_sems, out_sems):
    chunks = [pl.ds(first, last - first) for first, last in strips(raw_ref.shape[0], SLICE)]
    reads = [
        pltpu.make_async_copy(raw_ref.at[rows, :], held_ref.at[rows, :], in_sems.at[number])
        for number, rows in enumerate(chunks)
    ]
    writes = [
        pltpu.make_async_copy(ready_ref.at[rows, :], half_ref.at[rows, :], out_sems.at[number])
        for number, rows in enumerate(chunks)
    ]
    for read in reads:
        read.start()
    for read, write, rows in zip(reads, writes, chunks):
        read.wait()
        for first, last in strips(rows.size, SLICE // 2):
            part = pl.ds(rows.start + first, last - first)
            raw = held_ref[part, :]
            total = jnp.sum(raw * raw, axis=-1, keepdims=True)
            ready_ref[part, :] = (raw * lax.rsqrt(total + epsilon)).astype(jnp.bfloat16)
        write.start()
    for write in writes:
        write.wait()


def halves(raw):
    rows, width = raw.shape
    count = len(strips(rows, SLICE))
    return pl.pallas_call(
        halves_kernel,
        in_specs=[pl.BlockSpec(memory_space=pl.ANY)],
        out_specs=pl.BlockSpec(memory_space=pl.ANY),
        out_shape=jax.ShapeDtypeStruct((rows, width), jnp.bfloat16),
        scratch_shapes=[
            pltpu.VMEM((rows, width), jnp.float32),
            pltpu.VMEM((rows, width), jnp.bfloat16),
            pltpu.SemaphoreType.DMA((count,)),
            pltpu.SemaphoreType.DMA((count,)),
        ],
        name="halves",
        compiler_params=pltpu.CompilerParams(vmem_limit_bytes=125 * MIB // 2),
        cost_estimate=cost(rows, 1, width),
    )(raw)


def coupled(products, scale, factor, shift, places=None):
    powers = products * (-log2_e * scale) - log2_e * shift
    if places is not None:
        row = places[0] + lax.broadcasted_iota(jnp.int32, powers.shape, 0)
        column = places[1] + lax.broadcasted_iota(jnp.int32, powers.shape, 1)
        same = row == column
        powers = jnp.where(same, -powers, powers)
    below = 1.0 + jnp.exp2(powers)
    inverse = pl.reciprocal(below, approx=True)
    weights = factor * (inverse * (2.0 - below * inverse))
    if places is not None:
        weights = jnp.where(same, -weights, weights)
    return weights.astype(jnp.bfloat16)


def is_drawn(grid_ref, bit):
    drawn = jnp.bool_(False)
    for number in range(grid_ref.shape[0]):
        drawn = drawn | (grid_ref[number, 0] == (1 << bit))
    return drawn


def side_by_side(others, all_ref):
    if all_ref is None:
        return others
    left = 0
    for other_ref in others:
        count = other_ref.shape[0]
        all_ref[left : left + count, :] = other_ref[...]
        left += count
    return [all_ref]


def factors_of(factors, counts, top, bottom):
    last, column = None, None
    edge = 0
    for factor, count in zip(factors, counts):
        if top < edge + count and edge < bottom:
            if last is None:
                last = factor
            else:
                if column is None:
                    column = top + lax.broadcasted_iota(jnp.int32, (1, bottom - top), 1)
                last = jnp.where(column < edge, last, factor)
        edge += count
    return last


def add_pairs(
    scale, factors, shift, own_ref, rows, counts, others, before_ref, out_ref, weights_ref,
    raw_ref=None, matched=False,
):
    first, block = rows
    own = own_ref[first : first + block, :]
    pieces = strips(block, SLICE)
    places, left = [], 0
    for other_ref in others:
        count, width = other_ref.shape
        for top, bottom in strips(count, STRIP):
            products = lax.dot_general(
                own, other_ref[top:bottom, :], (((1,), (1,)), ((), ())),
                preferred_element_type=jnp.float32,
            )
            factor = factors_of(factors, counts, left + top, left + bottom)
            for low, high in pieces:
                weights_ref[first + low : first + high, left + top : left + bottom] = coupled(
                    products[low:high], scale, factor, shift, (first + low, top) if matched else None
                )
        places.append(slice(left, left + count))
        left += count
    sums = [[0.0, 0.0] for _ in pieces]
    for top, bottom in strips(width, COLUMNS):
        total = None
        for place, other_ref in zip(places, others):
            added = jnp.dot(
                weights_ref[first : first + block, place], other_ref[:, top:bottom],
                preferred_element_type=jnp.float32,
            )
            total = added if total is None else total + added
        for number, (low, high) in enumerate(pieces):
            part = total[low:high]
            here = slice(first + low, first + high)
            if before_ref is not None:
                part = part + before_ref[here, top:bottom]
            out_ref[here, top:bottom] = part
            if raw_ref is not None:
                raw = raw_ref[here, top:bottom]
                for side in range(0, bottom - top, LANES):
                    lanes = slice(side, side + LANES)
                    sums[number][0] += raw[:, lanes] * raw[:, lanes]
                    sums[number][1] += raw[:, lanes] * part[:, lanes]
    return sums


def blocks_of(count):
    return [(first, min(BLOCK, count - first)) for first in range(0, count, BLOCK)]


def drawn_factors(bits, scale_ref, grid_ref):
    scale = scale_ref[0]
    return [
        scale if bit is None else jnp.where(is_drawn(grid_ref, bit), scale, 0.0) for bit in bits
    ]


def all_scratch(others):
    count, width = sum(x.shape[0] for x in others), others[0].shape[1]
    if all(x.shape[0] % STRIP == 0 for x in others):
        return []
    return [pltpu.VMEM((count, width), jnp.bfloat16)]


def diagonal_kernel(scale_ref, shift_ref, image_ref, text_ref, image_sum_ref, text_sum_ref, weights_ref):
    scale, shift = scale_ref[0], shift_ref[0]
    row_count, width = image_ref.shape
    for rows in blocks_of(row_count):
        add_pairs(
            scale, [scale], shift, image_ref, rows, [row_count], [text_ref], None, image_sum_ref,
            weights_ref, matched=True,
        )
    for first, last in strips(row_count, STRIP):
        for left, right in strips(width, COLUMNS):
            text_sum_ref[first:last, left:right] = lax.dot_general(
                weights_ref[:, first:last], image_ref[:, left:right], (((0,), (0,)), ((), ())),
                preferred_element_type=jnp.float32,
            )


def diagonal(scale, shift, image_half, text_half):
    rows, width = image_half.shape
    return call(
        diagonal_kernel,
        "diagonal",
        [scale, shift, image_half, text_half],
        [((rows, width), jnp.float32)] * 2,
        (rows, 2 * rows, width),
        scratch=[pltpu.VMEM((rows, rows), jnp.bfloat16)],
    )


def near_kernel(
    bit, scale_ref, shift_ref, grid_ref, image_ref, text_ref, image_sum_ref, text_sum_ref, texts_ref,
    images_ref, image_out_ref, text_out_ref, weights_ref,
):
    scale, shift = scale_ref[0], shift_ref[0]
    factors = drawn_factors([bit], scale_ref, grid_ref)
    row_count = image_ref.shape[0]
    for own_ref, other_ref, sum_ref, out_ref in (
        (image_ref, texts_ref, image_sum_ref, image_out_ref),
        (text_ref, images_ref, text_sum_ref, text_out_ref),
    ):
        for rows in blocks_of(row_count):
            add_pairs(
                scale, factors, shift, own_ref, rows, [row_count], [other_ref], sum_ref, out_ref,
                weights_ref,
            )


def add_near(scale, shift, grid, image_half, text_half, image_sum, text_sum, texts, images, bit):
    rows, width = image_half.shape
    return call(
        functools.partial(near_kernel, bit),
        "add_near",
        [scale, shift, grid, image_half, text_half, image_sum, text_sum, texts, images],
        [((rows, width), jnp.float32)] * 2,
        (rows, 2 * rows, width),
        smem=3,
        scratch=[pltpu.VMEM((rows, rows), jnp.bfloat16)],
    )


def add_up_kernel(bits, scale_ref, shift_ref, grid_ref, own_ref, sum_ref, *refs):
    other_refs, (out_ref, weights_ref, *all_refs) = refs[: len(bits)], refs[len(bits) :]
    factors = drawn_factors(bits, scale_ref, grid_ref)
    counts = [x.shape[0] for x in other_refs]
    others = side_by_side(other_refs, *(all_refs or [None]))
    for rows in blocks_of(own_ref.shape[0]):
        add_pairs(
            scale_ref[0], factors, shift_ref[0], own_ref, rows, counts, others, sum_ref, out_ref,
            weights_ref,
        )


def add_up(scale, shift, grid, own, total, others, bits):
    rows, width = own.shape
    count = sum(x.shape[0] for x in others)
    return call(
        functools.partial(add_up_kernel, tuple(bits)),
        "add_up",
        [scale, shift, grid, own, total, *others],
        [((rows, width), jnp.float32)],
        (rows, count, width),
        smem=3,
        scratch=[pltpu.VMEM((rows, count), jnp.bfloat16), *all_scratch(others)],
    )[0]


def finish_kernel(bits, scale_ref, shift_ref, grid_ref, own_ref, raw_ref, sum_ref, *refs):
    other_refs, (out_ref, weights_ref, total_ref, sems, *all_refs) = refs[: len(bits)], refs[len(bits) :]
    factors = drawn_factors(bits, scale_ref, grid_ref)
    counts = [x.shape[0] for x in other_refs]
    others = side_by_side(other_refs, *(all_refs or [None]))
    copies = []
    for first, block in blocks_of(own_ref.shape[0]):
        sums = add_pairs(
            scale_ref[0], factors, shift_ref[0], own_ref, (first, block), counts, others, sum_ref,
            total_ref, weights_ref, raw_ref,
        )
        for (squares, products), (low, high) in zip(sums, strips(block, SLICE)):
            inverse = lax.rsqrt(jnp.sum(squares, axis=-1, keepdims=True) + epsilon)
            radial = jnp.sum(products, axis=-1, keepdims=True) * (inverse * inverse * inverse)
            here = pl.ds(first + low, high - low)
            for top, bottom in strips(own_ref.shape[1], COLUMNS):
                total_ref[here, top:bottom] = (
                    total_ref[here, top:bottom] * inverse - raw_ref[here, top:bottom] * radial
                )
            copy = pltpu.make_async_copy(
                total_ref.at[here, :], out_ref.at[here, :], sems.at[len(copies)]
            )
            copy.start()
            copies.append(copy)
    for copy in copies:
        copy.wait()


def finish(scale, shift, grid, own, raw, total, others, bits):
    rows, width = own.shape
    count = sum(x.shape[0] for x in others)
    return call(
        functools.partial(finish_kernel, tuple(bits)),
        "finish",
        [scale, shift, grid, own, raw, total, *others],
        [((rows, width), jnp.float32)],
        (rows, count, width),
        smem=3,
        out_specs=[pl.BlockSpec(memory_space=pl.ANY)],
        scratch=[
            pltpu.VMEM((rows, count), jnp.bfloat16),
            pltpu.VMEM((rows, width), jnp.float32),
            pltpu.SemaphoreType.DMA((len(strips(rows, SLICE)),)),
            *all_scratch(others),
        ],
    )[0]


def passed_along(x, axis, by):
    count = lax.axis_size(axis)
    return lax.ppermute(x, axis, [(i, (i + by) % count) for i in range(count)])


def exchanged(x, bit):
    count = lax.axis_size("blk")
    return lax.ppermute(x, "blk", [(i, i ^ (1 << bit)) for i in range(count)])


def with_partners(bits, visual, caption, grid, scale, shift):
    cut = visual.shape[0] * 3 // 4
    near, far = [bit for bit in bits if bit == 0], [bit for bit in bits if bit != 0]
    text_half = halves(caption)
    text_z = passed_along(text_half, "group", 1)
    far_texts = [exchanged(text_half, bit) for bit in far]
    image_half = normalized(visual)
    image_first, image_last = image_half[:cut], image_half[cut:]
    boths = [(exchanged(text_half, bit), exchanged(image_half, bit)) for bit in near]
    image_sum, text_sum = diagonal(scale, shift, image_half, text_half)
    image_first, image_last, text_z, image_sum, text_sum = lax.optimization_barrier(
        (image_first, image_last, text_z, image_sum, text_sum)
    )
    image_z_first = passed_along(image_first, "group", -1)
    image_z_last = passed_along(image_last, "group", -1)
    image_first, image_last, far_texts = lax.optimization_barrier(
        (image_first, image_last, far_texts)
    )
    far_images_first = [exchanged(image_first, bit) for bit in far]
    for (texts, images), bit in zip(boths, near):
        image_sum, text_sum = add_near(
            scale, shift, grid, image_half, text_half, image_sum, text_sum, texts, images, bit
        )
    image_gradient = finish(
        scale, shift, grid, image_half, visual, image_sum, [*far_texts, text_z], [*far, None]
    )
    text_sum, image_last, image_gradient = lax.optimization_barrier(
        (text_sum, image_last, image_gradient)
    )
    far_images_last = [exchanged(image_last, bit) for bit in far[:1]]
    image_last, image_z_first = lax.optimization_barrier((image_last, image_z_first))
    far_images_last += [exchanged(image_last, bit) for bit in far[1:]]
    text_sum = add_up(
        scale, shift, grid, text_half, text_sum, [*far_images_first, image_z_first], [*far, None]
    )
    text_gradient = finish(
        scale, shift, grid, text_half, caption, text_sum,
        [*far_images_last, image_z_last], [*far, None],
    )
    return image_gradient, text_gradient


def on_device(
    visual_encoder_outputs,
    caption_encoder_outputs,
    partner_lookup_grid,
    sharpness_coefficient,
    sigmoid_shift_term,
):
    rounds, peers = partner_lookup_grid.shape
    bits = range(peers.bit_length() - 1)
    operands = (
        visual_encoder_outputs,
        caption_encoder_outputs,
        partner_lookup_grid,
        sharpness_coefficient,
        sigmoid_shift_term,
    )
    if len(bits) <= rounds + 1:
        return with_partners(bits, *operands)
    choices = list(itertools.combinations(bits, rounds))
    union = jnp.sum(partner_lookup_grid[:, 0])
    branch = jnp.int32(0)
    for number, choice in enumerate(choices):
        branch = jnp.where(union == sum(1 << bit for bit in choice), jnp.int32(number), branch)
    return lax.switch(
        branch, [functools.partial(with_partners, choice) for choice in choices], *operands
    )


def solution(mesh):
    placed = (P(("blk", "group"), None), P(("blk", "group"), None), P(), P(), P())
    return jax.shard_map(
        on_device,
        mesh=mesh,
        in_specs=placed,
        out_specs=(P(("blk", "group"), None), P(("blk", "group"), None)),
        check_vma=False,
    )
```

```python
import functools
import itertools

import jax
import jax.numpy as jnp
from jax import lax
from jax.experimental import pallas as pl
from jax.experimental.pallas import tpu as pltpu
from jax.sharding import PartitionSpec as P

epsilon = 1e-06
log2_e = 1.4426950408889634
MIB = 1024 * 1024
VMEM = pl.BlockSpec(memory_space=pltpu.VMEM)
SMEM = pl.BlockSpec(memory_space=pltpu.SMEM)
BLOCK, STRIP, COLUMNS, SLICE, LANES = 256, 256, 256, 64, 128


def cost(rows, other_rows, width):
    return pl.CostEstimate(
        flops=4 * rows * max(other_rows, 1) * width,
        bytes_accessed=8 * rows * width,
        transcendentals=2 * rows * other_rows,
    )


def call(body, name, operands, outs, work, smem=2, grid=None, out_specs=None, scratch=()):
    return pl.pallas_call(
        body,
        grid=grid or (),
        in_specs=[SMEM] * smem + [VMEM] * (len(operands) - smem),
        out_specs=out_specs or [VMEM] * len(outs),
        out_shape=[jax.ShapeDtypeStruct(shape, dtype) for shape, dtype in outs],
        scratch_shapes=list(scratch),
        name=name,
        compiler_params=pltpu.CompilerParams(vmem_limit_bytes=24 * MIB),
        cost_estimate=cost(*work),
    )(*operands)


def strips(count, size):
    return [(first, min(first + size, count)) for first in range(0, count, size)]


def normalized(raw):
    total = jnp.sum(raw * raw, axis=-1, keepdims=True)
    return (raw * lax.rsqrt(total + epsilon)).astype(jnp.bfloat16)


def coupled(products, scale, factor, shift, places=None):
    powers = products * (-log2_e * scale) - log2_e * shift
    if places is not None:
        row = places[0] + lax.broadcasted_iota(jnp.int32, powers.shape, 0)
        column = places[1] + lax.broadcasted_iota(jnp.int32, powers.shape, 1)
        same = row == column
        powers = jnp.where(same, -powers, powers)
    below = 1.0 + jnp.exp2(powers)
    inverse = pl.reciprocal(below, approx=True)
    weights = factor * (inverse * (2.0 - below * inverse))
    if places is not None:
        weights = jnp.where(same, -weights, weights)
    return weights.astype(jnp.bfloat16)


def is_drawn(grid_ref, bit):
    drawn = jnp.bool_(False)
    for number in range(grid_ref.shape[0]):
        drawn = drawn | (grid_ref[number, 0] == (1 << bit))
    return drawn


def side_by_side(others, all_ref):
    if all(x.shape[0] % STRIP == 0 for x in others):
        return list(others)
    left = 0
    for other_ref in others:
        count = other_ref.shape[0]
        all_ref[left : left + count, :] = other_ref[...]
        left += count
    return [all_ref.at[:left, :]]


def for_drawn(bits, scale_ref, grid_ref, other_refs, all_ref, run):
    scale = scale_ref[0]
    flagged = [(ref, bit) for ref, bit in zip(other_refs, bits) if bit is not None]
    if len(flagged) != 2:
        run(
            side_by_side(other_refs, all_ref), [x.shape[0] for x in other_refs],
            drawn_factors(bits, scale_ref, grid_ref),
        )
        return
    (one_ref, one), (two_ref, two) = flagged
    first, second = is_drawn(grid_ref, one), is_drawn(grid_ref, two)
    fixed = [ref for ref, bit in zip(other_refs, bits) if bit is None]
    count = one_ref.shape[0]

    @pl.when(first & second)
    def _():
        others = side_by_side([*fixed, one_ref, two_ref], all_ref)
        run(others, [sum(x.shape[0] for x in others)], [scale])

    @pl.when(jnp.logical_not(first & second))
    def _():
        left, others = 0, list(fixed)
        if any(x.shape[0] % STRIP for x in (*fixed, one_ref)):
            others = []
            for ref in fixed:
                all_ref[left : left + ref.shape[0], :] = ref[...]
                left += ref.shape[0]

        @pl.when(first)
        def _():
            all_ref[left : left + count, :] = one_ref[...]

        @pl.when(jnp.logical_not(first))
        def _():
            all_ref[left : left + count, :] = two_ref[...]

        others.append(all_ref.at[: left + count, :])
        run(others, [sum(x.shape[0] for x in others)], [scale])


def factors_of(factors, counts, top, bottom):
    last, column = None, None
    edge = 0
    for factor, count in zip(factors, counts):
        if top < edge + count and edge < bottom:
            if last is None:
                last = factor
            else:
                if column is None:
                    column = top + lax.broadcasted_iota(jnp.int32, (1, bottom - top), 1)
                last = jnp.where(column < edge, last, factor)
        edge += count
    return last


def add_pairs(
    scale, factors, shift, own_ref, rows, counts, others, before_ref, out_ref, weights_ref,
    raw_ref=None, matched=False,
):
    first, block = rows
    own = own_ref[first : first + block, :]
    pieces = strips(block, SLICE)
    places, left = [], 0
    for other_ref in others:
        count, width = other_ref.shape
        for top, bottom in strips(count, STRIP):
            products = lax.dot_general(
                own, other_ref[top:bottom, :], (((1,), (1,)), ((), ())),
                preferred_element_type=jnp.float32,
            )
            factor = factors_of(factors, counts, left + top, left + bottom)
            for low, high in pieces:
                weights_ref[first + low : first + high, left + top : left + bottom] = coupled(
                    products[low:high], scale, factor, shift, (first + low, top) if matched else None
                )
        places.append(slice(left, left + count))
        left += count
    sums = [[0.0, 0.0] for _ in pieces]
    for top, bottom in strips(width, COLUMNS):
        total = None
        for place, other_ref in zip(places, others):
            added = jnp.dot(
                weights_ref[first : first + block, place], other_ref[:, top:bottom],
                preferred_element_type=jnp.float32,
            )
            total = added if total is None else total + added
        for number, (low, high) in enumerate(pieces):
            part = total[low:high]
            here = slice(first + low, first + high)
            if before_ref is not None:
                part = part + before_ref[here, top:bottom]
            out_ref[here, top:bottom] = part
            if raw_ref is not None:
                raw = raw_ref[here, top:bottom]
                for side in range(0, bottom - top, LANES):
                    lanes = slice(side, side + LANES)
                    sums[number][0] += raw[:, lanes] * raw[:, lanes]
                    sums[number][1] += raw[:, lanes] * part[:, lanes]
    return sums


def blocks_of(count):
    return [(first, min(BLOCK, count - first)) for first in range(0, count, BLOCK)]


def drawn_factors(bits, scale_ref, grid_ref):
    scale = scale_ref[0]
    return [
        scale if bit is None else jnp.where(is_drawn(grid_ref, bit), scale, 0.0) for bit in bits
    ]


def all_scratch(others):
    return pltpu.VMEM((sum(x.shape[0] for x in others), others[0].shape[1]), jnp.bfloat16)


def diagonal_kernel(scale_ref, shift_ref, image_ref, text_ref, image_sum_ref, text_sum_ref, weights_ref):
    scale, shift = scale_ref[0], shift_ref[0]
    row_count, width = image_ref.shape
    for rows in blocks_of(row_count):
        add_pairs(
            scale, [scale], shift, image_ref, rows, [row_count], [text_ref], None, image_sum_ref,
            weights_ref, matched=True,
        )
    for first, last in strips(row_count, STRIP):
        for left, right in strips(width, COLUMNS):
            text_sum_ref[first:last, left:right] = lax.dot_general(
                weights_ref[:, first:last], image_ref[:, left:right], (((0,), (0,)), ((), ())),
                preferred_element_type=jnp.float32,
            )


def diagonal(scale, shift, image_half, text_half):
    rows, width = image_half.shape
    return call(
        diagonal_kernel,
        "diagonal",
        [scale, shift, image_half, text_half],
        [((rows, width), jnp.float32)] * 2,
        (rows, 2 * rows, width),
        scratch=[pltpu.VMEM((rows, rows), jnp.bfloat16)],
    )


def near_kernel(
    bit, scale_ref, shift_ref, grid_ref, image_ref, text_ref, image_sum_ref, text_sum_ref, texts_ref,
    images_ref, image_out_ref, text_out_ref, weights_ref,
):
    scale, shift = scale_ref[0], shift_ref[0]
    factors = drawn_factors([bit], scale_ref, grid_ref)
    row_count = image_ref.shape[0]
    for own_ref, other_ref, sum_ref, out_ref in (
        (image_ref, texts_ref, image_sum_ref, image_out_ref),
        (text_ref, images_ref, text_sum_ref, text_out_ref),
    ):
        for rows in blocks_of(row_count):
            add_pairs(
                scale, factors, shift, own_ref, rows, [row_count], [other_ref], sum_ref, out_ref,
                weights_ref,
            )


def add_near(scale, shift, grid, image_half, text_half, image_sum, text_sum, texts, images, bit):
    rows, width = image_half.shape
    return call(
        functools.partial(near_kernel, bit),
        "add_near",
        [scale, shift, grid, image_half, text_half, image_sum, text_sum, texts, images],
        [((rows, width), jnp.float32)] * 2,
        (rows, 2 * rows, width),
        smem=3,
        scratch=[pltpu.VMEM((rows, rows), jnp.bfloat16)],
    )


def add_up_kernel(bits, scale_ref, shift_ref, grid_ref, own_ref, sum_ref, *refs):
    other_refs, (out_ref, weights_ref, all_ref) = refs[: len(bits)], refs[len(bits) :]

    def run(others, counts, factors):
        for rows in blocks_of(own_ref.shape[0]):
            add_pairs(
                scale_ref[0], factors, shift_ref[0], own_ref, rows, counts, others, sum_ref, out_ref,
                weights_ref,
            )

    for_drawn(bits, scale_ref, grid_ref, other_refs, all_ref, run)


def add_up(scale, shift, grid, own, total, others, bits):
    rows, width = own.shape
    count = sum(x.shape[0] for x in others)
    return call(
        functools.partial(add_up_kernel, tuple(bits)),
        "add_up",
        [scale, shift, grid, own, total, *others],
        [((rows, width), jnp.float32)],
        (rows, count, width),
        smem=3,
        scratch=[pltpu.VMEM((rows, count), jnp.bfloat16), all_scratch(others)],
    )[0]


def finish_kernel(bits, scale_ref, shift_ref, grid_ref, own_ref, raw_ref, sum_ref, *refs):
    other_refs, (out_ref, weights_ref, total_ref, sems, all_ref) = refs[: len(bits)], refs[len(bits) :]

    def run(others, counts, factors):
        copies = []
        for first, block in blocks_of(own_ref.shape[0]):
            sums = add_pairs(
                scale_ref[0], factors, shift_ref[0], own_ref, (first, block), counts, others, sum_ref,
                total_ref, weights_ref, raw_ref,
            )
            for (squares, products), (low, high) in zip(sums, strips(block, SLICE)):
                inverse = lax.rsqrt(jnp.sum(squares, axis=-1, keepdims=True) + epsilon)
                radial = jnp.sum(products, axis=-1, keepdims=True) * (inverse * inverse * inverse)
                here = pl.ds(first + low, high - low)
                for top, bottom in strips(own_ref.shape[1], COLUMNS):
                    total_ref[here, top:bottom] = (
                        total_ref[here, top:bottom] * inverse - raw_ref[here, top:bottom] * radial
                    )
                copy = pltpu.make_async_copy(
                    total_ref.at[here, :], out_ref.at[here, :], sems.at[len(copies)]
                )
                copy.start()
                copies.append(copy)
        for copy in copies:
            copy.wait()

    for_drawn(bits, scale_ref, grid_ref, other_refs, all_ref, run)


def finish(scale, shift, grid, own, raw, total, others, bits):
    rows, width = own.shape
    count = sum(x.shape[0] for x in others)
    return call(
        functools.partial(finish_kernel, tuple(bits)),
        "finish",
        [scale, shift, grid, own, raw, total, *others],
        [((rows, width), jnp.float32)],
        (rows, count, width),
        smem=3,
        out_specs=[pl.BlockSpec(memory_space=pl.ANY)],
        scratch=[
            pltpu.VMEM((rows, count), jnp.bfloat16),
            pltpu.VMEM((rows, width), jnp.float32),
            pltpu.SemaphoreType.DMA((len(strips(rows, SLICE)),)),
            all_scratch(others),
        ],
    )[0]


def passed_along(x, axis, by):
    count = lax.axis_size(axis)
    return lax.ppermute(x, axis, [(i, (i + by) % count) for i in range(count)])


def exchanged(x, bit):
    count = lax.axis_size("blk")
    return lax.ppermute(x, "blk", [(i, i ^ (1 << bit)) for i in range(count)])


def with_partners(bits, visual, caption, grid, scale, shift):
    cut = visual.shape[0] * 3 // 4
    near, far = [bit for bit in bits if bit == 0], [bit for bit in bits if bit != 0]
    text_half = normalized(caption)
    text_z = passed_along(text_half, "group", 1)
    far_texts = [exchanged(text_half, bit) for bit in far]
    image_half = normalized(visual)
    image_first, image_last = image_half[:cut], image_half[cut:]
    boths = [(exchanged(text_half, bit), exchanged(image_half, bit)) for bit in near]
    image_sum, text_sum = diagonal(scale, shift, image_half, text_half)
    image_first, image_last, text_z, image_sum, text_sum = lax.optimization_barrier(
        (image_first, image_last, text_z, image_sum, text_sum)
    )
    image_z_first = passed_along(image_first, "group", -1)
    image_z_last = passed_along(image_last, "group", -1)
    far_images_first = [exchanged(image_first, bit) for bit in far]
    for (texts, images), bit in zip(boths, near):
        image_sum, text_sum = add_near(
            scale, shift, grid, image_half, text_half, image_sum, text_sum, texts, images, bit
        )
    image_gradient = finish(
        scale, shift, grid, image_half, visual, image_sum, [*far_texts, text_z], [*far, None]
    )
    text_sum, image_last, image_gradient = lax.optimization_barrier(
        (text_sum, image_last, image_gradient)
    )
    far_images_last = [exchanged(image_last, bit) for bit in far[:1]]
    image_last, image_z_first = lax.optimization_barrier((image_last, image_z_first))
    far_images_last += [exchanged(image_last, bit) for bit in far[1:]]
    text_sum = add_up(
        scale, shift, grid, text_half, text_sum, [*far_images_first, image_z_first], [*far, None]
    )
    text_gradient = finish(
        scale, shift, grid, text_half, caption, text_sum,
        [*far_images_last, image_z_last], [*far, None],
    )
    return image_gradient, text_gradient


def on_device(
    visual_encoder_outputs,
    caption_encoder_outputs,
    partner_lookup_grid,
    sharpness_coefficient,
    sigmoid_shift_term,
):
    rounds, peers = partner_lookup_grid.shape
    bits = range(peers.bit_length() - 1)
    operands = (
        visual_encoder_outputs,
        caption_encoder_outputs,
        partner_lookup_grid,
        sharpness_coefficient,
        sigmoid_shift_term,
    )
    if len(bits) <= rounds + 1:
        return with_partners(bits, *operands)
    choices = list(itertools.combinations(bits, rounds))
    union = jnp.sum(partner_lookup_grid[:, 0])
    branch = jnp.int32(0)
    for number, choice in enumerate(choices):
        branch = jnp.where(union == sum(1 << bit for bit in choice), jnp.int32(number), branch)
    return lax.switch(
        branch, [functools.partial(with_partners, choice) for choice in choices], *operands
    )


def solution(mesh):
    placed = (P(("blk", "group"), None), P(("blk", "group"), None), P(), P(), P())
    return jax.shard_map(
        on_device,
        mesh=mesh,
        in_specs=placed,
        out_specs=(P(("blk", "group"), None), P(("blk", "group"), None)),
        check_vma=False,
    )
```

```python
import functools
import itertools

import jax
import jax.numpy as jnp
from jax import lax
from jax.experimental import pallas as pl
from jax.experimental.pallas import tpu as pltpu
from jax.sharding import PartitionSpec as P

epsilon = 1e-06
log2_e = 1.4426950408889634
MIB = 1024 * 1024
VMEM = pl.BlockSpec(memory_space=pltpu.VMEM)
SMEM = pl.BlockSpec(memory_space=pltpu.SMEM)
BLOCK, STRIP, COLUMNS, SLICE, LANES = 256, 256, 256, 64, 128


def cost(rows, other_rows, width):
    return pl.CostEstimate(
        flops=4 * rows * max(other_rows, 1) * width,
        bytes_accessed=8 * rows * width,
        transcendentals=2 * rows * other_rows,
    )


def call(body, name, operands, outs, work, smem=2, grid=None, out_specs=None, scratch=()):
    return pl.pallas_call(
        body,
        grid=grid or (),
        in_specs=[SMEM] * smem + [VMEM] * (len(operands) - smem),
        out_specs=out_specs or [VMEM] * len(outs),
        out_shape=[jax.ShapeDtypeStruct(shape, dtype) for shape, dtype in outs],
        scratch_shapes=list(scratch),
        name=name,
        compiler_params=pltpu.CompilerParams(vmem_limit_bytes=24 * MIB),
        cost_estimate=cost(*work),
    )(*operands)


def strips(count, size):
    return [(first, min(first + size, count)) for first in range(0, count, size)]


def normalized(raw):
    total = jnp.sum(raw * raw, axis=-1, keepdims=True)
    return (raw * lax.rsqrt(total + epsilon)).astype(jnp.bfloat16)


def coupled(products, scale, factor, shift, places=None):
    powers = products * (-log2_e * scale) - log2_e * shift
    if places is not None:
        row = places[0] + lax.broadcasted_iota(jnp.int32, powers.shape, 0)
        column = places[1] + lax.broadcasted_iota(jnp.int32, powers.shape, 1)
        same = row == column
        powers = jnp.where(same, -powers, powers)
    below = 1.0 + jnp.exp2(powers)
    inverse = pl.reciprocal(below, approx=True)
    weights = factor * (inverse * (2.0 - below * inverse))
    if places is not None:
        weights = jnp.where(same, -weights, weights)
    return weights.astype(jnp.bfloat16)


def is_drawn(grid_ref, bit):
    drawn = jnp.bool_(False)
    for number in range(grid_ref.shape[0]):
        drawn = drawn | (grid_ref[number, 0] == (1 << bit))
    return drawn


def side_by_side(others, all_ref):
    if all(x.shape[0] % STRIP == 0 for x in others):
        return list(others)
    left = 0
    for other_ref in others:
        count = other_ref.shape[0]
        all_ref[left : left + count, :] = other_ref[...]
        left += count
    return [all_ref.at[:left, :]]


def for_drawn(bits, scale_ref, grid_ref, other_refs, all_ref, run):
    scale = scale_ref[0]
    flagged = [(ref, bit) for ref, bit in zip(other_refs, bits) if bit is not None]
    if len(flagged) != 2:
        run(
            side_by_side(other_refs, all_ref), [x.shape[0] for x in other_refs],
            drawn_factors(bits, scale_ref, grid_ref),
        )
        return
    (one_ref, one), (two_ref, two) = flagged
    first, second = is_drawn(grid_ref, one), is_drawn(grid_ref, two)
    fixed = [ref for ref, bit in zip(other_refs, bits) if bit is None]
    count = one_ref.shape[0]

    @pl.when(first & second)
    def _():
        others = side_by_side([*fixed, one_ref, two_ref], all_ref)
        run(others, [sum(x.shape[0] for x in others)], [scale])

    @pl.when(jnp.logical_not(first & second))
    def _():
        left, others = 0, list(fixed)
        if any(x.shape[0] % STRIP for x in (*fixed, one_ref)):
            others = []
            for ref in fixed:
                all_ref[left : left + ref.shape[0], :] = ref[...]
                left += ref.shape[0]

        @pl.when(first)
        def _():
            all_ref[left : left + count, :] = one_ref[...]

        @pl.when(jnp.logical_not(first))
        def _():
            all_ref[left : left + count, :] = two_ref[...]

        others.append(all_ref.at[: left + count, :])
        run(others, [sum(x.shape[0] for x in others)], [scale])


def factors_of(factors, counts, top, bottom):
    last, column = None, None
    edge = 0
    for factor, count in zip(factors, counts):
        if top < edge + count and edge < bottom:
            if last is None:
                last = factor
            else:
                if column is None:
                    column = top + lax.broadcasted_iota(jnp.int32, (1, bottom - top), 1)
                last = jnp.where(column < edge, last, factor)
        edge += count
    return last


def add_pairs(
    scale, factors, shift, own_ref, rows, counts, others, before_ref, out_ref, weights_ref,
    raw_ref=None, matched=False,
):
    first, block = rows
    own = own_ref[first : first + block, :]
    pieces = strips(block, SLICE)
    places, left = [], 0
    for other_ref in others:
        count, width = other_ref.shape
        for top, bottom in strips(count, STRIP):
            products = lax.dot_general(
                own, other_ref[top:bottom, :], (((1,), (1,)), ((), ())),
                preferred_element_type=jnp.float32,
            )
            factor = factors_of(factors, counts, left + top, left + bottom)
            for low, high in pieces:
                weights_ref[first + low : first + high, left + top : left + bottom] = coupled(
                    products[low:high], scale, factor, shift, (first + low, top) if matched else None
                )
        places.append(slice(left, left + count))
        left += count
    sums = [[0.0, 0.0] for _ in pieces]
    for top, bottom in strips(width, COLUMNS):
        total = None
        for place, other_ref in zip(places, others):
            added = jnp.dot(
                weights_ref[first : first + block, place], other_ref[:, top:bottom],
                preferred_element_type=jnp.float32,
            )
            total = added if total is None else total + added
        for number, (low, high) in enumerate(pieces):
            part = total[low:high]
            here = slice(first + low, first + high)
            if before_ref is not None:
                part = part + before_ref[here, top:bottom]
            out_ref[here, top:bottom] = part
            if raw_ref is not None:
                raw = raw_ref[here, top:bottom]
                for side in range(0, bottom - top, LANES):
                    lanes = slice(side, side + LANES)
                    sums[number][0] += raw[:, lanes] * raw[:, lanes]
                    sums[number][1] += raw[:, lanes] * part[:, lanes]
    return sums


def blocks_of(count, size=BLOCK):
    return [(first, min(size, count - first)) for first in range(0, count, size)]


def drawn_factors(bits, scale_ref, grid_ref):
    scale = scale_ref[0]
    return [
        scale if bit is None else jnp.where(is_drawn(grid_ref, bit), scale, 0.0) for bit in bits
    ]


def all_scratch(others):
    return pltpu.VMEM((sum(x.shape[0] for x in others), others[0].shape[1]), jnp.bfloat16)


def diagonal_kernel(scale_ref, shift_ref, image_ref, text_ref, image_sum_ref, text_sum_ref, weights_ref):
    scale, shift = scale_ref[0], shift_ref[0]
    row_count, width = image_ref.shape
    for rows in blocks_of(row_count):
        add_pairs(
            scale, [scale], shift, image_ref, rows, [row_count], [text_ref], None, image_sum_ref,
            weights_ref, matched=True,
        )
    for first, last in strips(row_count, STRIP):
        for left, right in strips(width, COLUMNS):
            text_sum_ref[first:last, left:right] = lax.dot_general(
                weights_ref[:, first:last], image_ref[:, left:right], (((0,), (0,)), ((), ())),
                preferred_element_type=jnp.float32,
            )


def diagonal(scale, shift, image_half, text_half):
    rows, width = image_half.shape
    return call(
        diagonal_kernel,
        "diagonal",
        [scale, shift, image_half, text_half],
        [((rows, width), jnp.float32)] * 2,
        (rows, 2 * rows, width),
        scratch=[pltpu.VMEM((rows, rows), jnp.bfloat16)],
    )


def near_kernel(
    bit, scale_ref, shift_ref, grid_ref, image_ref, text_ref, image_sum_ref, text_sum_ref, texts_ref,
    images_ref, image_out_ref, text_out_ref, weights_ref,
):
    scale, shift = scale_ref[0], shift_ref[0]
    factors = drawn_factors([bit], scale_ref, grid_ref)
    row_count = image_ref.shape[0]
    for own_ref, other_ref, sum_ref, out_ref in (
        (image_ref, texts_ref, image_sum_ref, image_out_ref),
        (text_ref, images_ref, text_sum_ref, text_out_ref),
    ):
        for rows in blocks_of(row_count):
            add_pairs(
                scale, factors, shift, own_ref, rows, [row_count], [other_ref], sum_ref, out_ref,
                weights_ref,
            )


def add_near(scale, shift, grid, image_half, text_half, image_sum, text_sum, texts, images, bit):
    rows, width = image_half.shape
    return call(
        functools.partial(near_kernel, bit),
        "add_near",
        [scale, shift, grid, image_half, text_half, image_sum, text_sum, texts, images],
        [((rows, width), jnp.float32)] * 2,
        (rows, 2 * rows, width),
        smem=3,
        scratch=[pltpu.VMEM((rows, rows), jnp.bfloat16)],
    )


def add_up_kernel(bits, scale_ref, shift_ref, grid_ref, own_ref, sum_ref, *refs):
    other_refs, (out_ref, weights_ref, all_ref) = refs[: len(bits)], refs[len(bits) :]

    def run(others, counts, factors):
        for rows in blocks_of(own_ref.shape[0]):
            add_pairs(
                scale_ref[0], factors, shift_ref[0], own_ref, rows, counts, others, sum_ref, out_ref,
                weights_ref,
            )

    for_drawn(bits, scale_ref, grid_ref, other_refs, all_ref, run)


def add_up(scale, shift, grid, own, total, others, bits):
    rows, width = own.shape
    count = sum(x.shape[0] for x in others)
    return call(
        functools.partial(add_up_kernel, tuple(bits)),
        "add_up",
        [scale, shift, grid, own, total, *others],
        [((rows, width), jnp.float32)],
        (rows, count, width),
        smem=3,
        scratch=[pltpu.VMEM((rows, count), jnp.bfloat16), all_scratch(others)],
    )[0]


def finish_kernel(bits, size, scale_ref, shift_ref, grid_ref, own_ref, raw_ref, sum_ref, *refs):
    other_refs, (out_ref, weights_ref, total_ref, sems, all_ref) = refs[: len(bits)], refs[len(bits) :]

    def run(others, counts, factors):
        copies = []
        for first, block in blocks_of(own_ref.shape[0], size):
            sums = add_pairs(
                scale_ref[0], factors, shift_ref[0], own_ref, (first, block), counts, others, sum_ref,
                total_ref, weights_ref, raw_ref,
            )
            for (squares, products), (low, high) in zip(sums, strips(block, SLICE)):
                inverse = lax.rsqrt(jnp.sum(squares, axis=-1, keepdims=True) + epsilon)
                radial = jnp.sum(products, axis=-1, keepdims=True) * (inverse * inverse * inverse)
                here = pl.ds(first + low, high - low)
                for top, bottom in strips(own_ref.shape[1], COLUMNS):
                    total_ref[here, top:bottom] = (
                        total_ref[here, top:bottom] * inverse - raw_ref[here, top:bottom] * radial
                    )
                copy = pltpu.make_async_copy(
                    total_ref.at[here, :], out_ref.at[here, :], sems.at[len(copies)]
                )
                copy.start()
                copies.append(copy)
        for copy in copies:
            copy.wait()

    for_drawn(bits, scale_ref, grid_ref, other_refs, all_ref, run)


def finish(scale, shift, grid, own, raw, total, others, bits, size=BLOCK):
    rows, width = own.shape
    count = sum(x.shape[0] for x in others)
    return call(
        functools.partial(finish_kernel, tuple(bits), size),
        "finish",
        [scale, shift, grid, own, raw, total, *others],
        [((rows, width), jnp.float32)],
        (rows, count, width),
        smem=3,
        out_specs=[pl.BlockSpec(memory_space=pl.ANY)],
        scratch=[
            pltpu.VMEM((rows, count), jnp.bfloat16),
            pltpu.VMEM((rows, width), jnp.float32),
            pltpu.SemaphoreType.DMA((len(strips(rows, SLICE)),)),
            all_scratch(others),
        ],
    )[0]


def passed_along(x, axis, by):
    count = lax.axis_size(axis)
    return lax.ppermute(x, axis, [(i, (i + by) % count) for i in range(count)])


def exchanged(x, bit):
    count = lax.axis_size("blk")
    return lax.ppermute(x, "blk", [(i, i ^ (1 << bit)) for i in range(count)])


def with_partners(bits, visual, caption, grid, scale, shift):
    cut = visual.shape[0] * 3 // 4
    near, far = [bit for bit in bits if bit == 0], [bit for bit in bits if bit != 0]
    text_half = normalized(caption)
    text_z = passed_along(text_half, "group", 1)
    far_texts = [exchanged(text_half, bit) for bit in far]
    image_half = normalized(visual)
    image_first, image_last = image_half[:cut], image_half[cut:]
    boths = [(exchanged(text_half, bit), exchanged(image_half, bit)) for bit in near]
    image_sum, text_sum = diagonal(scale, shift, image_half, text_half)
    image_first, image_last, text_z, image_sum, text_sum = lax.optimization_barrier(
        (image_first, image_last, text_z, image_sum, text_sum)
    )
    image_z_first = passed_along(image_first, "group", -1)
    image_z_last = passed_along(image_last, "group", -1)
    far_images_first = [exchanged(image_first, bit) for bit in far]
    for (texts, images), bit in zip(boths, near):
        image_sum, text_sum = add_near(
            scale, shift, grid, image_half, text_half, image_sum, text_sum, texts, images, bit
        )
    image_gradient = finish(
        scale, shift, grid, image_half, visual, image_sum, [*far_texts, text_z], [*far, None]
    )
    text_sum, image_last, image_gradient = lax.optimization_barrier(
        (text_sum, image_last, image_gradient)
    )
    far_images_last = [exchanged(image_last, bit) for bit in far[:1]]
    image_last, image_z_first = lax.optimization_barrier((image_last, image_z_first))
    far_images_last += [exchanged(image_last, bit) for bit in far[1:]]
    text_sum = add_up(
        scale, shift, grid, text_half, text_sum, [*far_images_first, image_z_first], [*far, None]
    )
    text_gradient = finish(
        scale, shift, grid, text_half, caption, text_sum,
        [*far_images_last, image_z_last], [*far, None], BLOCK // 2,
    )
    return image_gradient, text_gradient


def on_device(
    visual_encoder_outputs,
    caption_encoder_outputs,
    partner_lookup_grid,
    sharpness_coefficient,
    sigmoid_shift_term,
):
    rounds, peers = partner_lookup_grid.shape
    bits = range(peers.bit_length() - 1)
    operands = (
        visual_encoder_outputs,
        caption_encoder_outputs,
        partner_lookup_grid,
        sharpness_coefficient,
        sigmoid_shift_term,
    )
    if len(bits) <= rounds + 1:
        return with_partners(bits, *operands)
    choices = list(itertools.combinations(bits, rounds))
    union = jnp.sum(partner_lookup_grid[:, 0])
    branch = jnp.int32(0)
    for number, choice in enumerate(choices):
        branch = jnp.where(union == sum(1 << bit for bit in choice), jnp.int32(number), branch)
    return lax.switch(
        branch, [functools.partial(with_partners, choice) for choice in choices], *operands
    )


def solution(mesh):
    placed = (P(("blk", "group"), None), P(("blk", "group"), None), P(), P(), P())
    return jax.shard_map(
        on_device,
        mesh=mesh,
        in_specs=placed,
        out_specs=(P(("blk", "group"), None), P(("blk", "group"), None)),
        check_vma=False,
    )
```

```python
import functools
import itertools

import jax
import jax.numpy as jnp
from jax import lax
from jax.experimental import pallas as pl
from jax.experimental.pallas import tpu as pltpu
from jax.sharding import PartitionSpec as P

epsilon = 1e-06
log2_e = 1.4426950408889634
MIB = 1024 * 1024
VMEM = pl.BlockSpec(memory_space=pltpu.VMEM)
SMEM = pl.BlockSpec(memory_space=pltpu.SMEM)
BLOCK, STRIP, COLUMNS, SLICE, LANES = 256, 256, 256, 64, 128


def cost(rows, other_rows, width):
    return pl.CostEstimate(
        flops=4 * rows * max(other_rows, 1) * width,
        bytes_accessed=8 * rows * width,
        transcendentals=2 * rows * other_rows,
    )


def call(body, name, operands, outs, work, smem=2, grid=None, out_specs=None, scratch=()):
    return pl.pallas_call(
        body,
        grid=grid or (),
        in_specs=[SMEM] * smem + [VMEM] * (len(operands) - smem),
        out_specs=out_specs or [VMEM] * len(outs),
        out_shape=[jax.ShapeDtypeStruct(shape, dtype) for shape, dtype in outs],
        scratch_shapes=list(scratch),
        name=name,
        compiler_params=pltpu.CompilerParams(vmem_limit_bytes=24 * MIB),
        cost_estimate=cost(*work),
    )(*operands)


def strips(count, size):
    return [(first, min(first + size, count)) for first in range(0, count, size)]


def normalized(raw):
    total = jnp.sum(raw * raw, axis=-1, keepdims=True)
    return (raw * lax.rsqrt(total + epsilon)).astype(jnp.bfloat16)


def coupled(products, scale, factor, shift, places=None):
    powers = products * (-log2_e * scale) - log2_e * shift
    if places is not None:
        row = places[0] + lax.broadcasted_iota(jnp.int32, powers.shape, 0)
        column = places[1] + lax.broadcasted_iota(jnp.int32, powers.shape, 1)
        same = row == column
        powers = jnp.where(same, -powers, powers)
    below = 1.0 + jnp.exp2(powers)
    inverse = pl.reciprocal(below, approx=True)
    weights = factor * (inverse * (2.0 - below * inverse))
    if places is not None:
        weights = jnp.where(same, -weights, weights)
    return weights.astype(jnp.bfloat16)


def is_drawn(grid_ref, bit):
    drawn = jnp.bool_(False)
    for number in range(grid_ref.shape[0]):
        drawn = drawn | (grid_ref[number, 0] == (1 << bit))
    return drawn


def side_by_side(others, all_ref):
    if all(x.shape[0] % STRIP == 0 for x in others):
        return list(others)
    left = 0
    for other_ref in others:
        count = other_ref.shape[0]
        all_ref[left : left + count, :] = other_ref[...]
        left += count
    return [all_ref.at[:left, :]]


def for_drawn(bits, scale_ref, grid_ref, other_refs, all_ref, run):
    scale = scale_ref[0]
    flagged = [(ref, bit) for ref, bit in zip(other_refs, bits) if bit is not None]
    if len(flagged) != 2:
        run(
            side_by_side(other_refs, all_ref), [x.shape[0] for x in other_refs],
            drawn_factors(bits, scale_ref, grid_ref),
        )
        return
    (one_ref, one), (two_ref, two) = flagged
    first, second = is_drawn(grid_ref, one), is_drawn(grid_ref, two)
    fixed = [ref for ref, bit in zip(other_refs, bits) if bit is None]
    count = one_ref.shape[0]

    @pl.when(first & second)
    def _():
        others = side_by_side([*fixed, one_ref, two_ref], all_ref)
        run(others, [sum(x.shape[0] for x in others)], [scale])

    @pl.when(jnp.logical_not(first & second))
    def _():
        left, others = 0, list(fixed)
        if any(x.shape[0] % STRIP for x in (*fixed, one_ref)):
            others = []
            for ref in fixed:
                all_ref[left : left + ref.shape[0], :] = ref[...]
                left += ref.shape[0]

        @pl.when(first)
        def _():
            all_ref[left : left + count, :] = one_ref[...]

        @pl.when(jnp.logical_not(first))
        def _():
            all_ref[left : left + count, :] = two_ref[...]

        others.append(all_ref.at[: left + count, :])
        run(others, [sum(x.shape[0] for x in others)], [scale])


def factors_of(factors, counts, top, bottom):
    last, column = None, None
    edge = 0
    for factor, count in zip(factors, counts):
        if top < edge + count and edge < bottom:
            if last is None:
                last = factor
            else:
                if column is None:
                    column = top + lax.broadcasted_iota(jnp.int32, (1, bottom - top), 1)
                last = jnp.where(column < edge, last, factor)
        edge += count
    return last


def add_pairs(
    scale, factors, shift, own_ref, rows, counts, others, before_ref, out_ref, weights_ref,
    raw_ref=None, matched=False,
):
    first, block = rows
    own = own_ref[first : first + block, :]
    pieces = strips(block, SLICE)
    places, left = [], 0
    for other_ref in others:
        count, width = other_ref.shape
        for top, bottom in strips(count, STRIP):
            products = lax.dot_general(
                own, other_ref[top:bottom, :], (((1,), (1,)), ((), ())),
                preferred_element_type=jnp.float32,
            )
            factor = factors_of(factors, counts, left + top, left + bottom)
            for low, high in pieces:
                weights_ref[first + low : first + high, left + top : left + bottom] = coupled(
                    products[low:high], scale, factor, shift, (first + low, top) if matched else None
                )
        places.append(slice(left, left + count))
        left += count
    sums = [[0.0, 0.0] for _ in pieces]
    for top, bottom in strips(width, COLUMNS):
        total = None
        for place, other_ref in zip(places, others):
            added = jnp.dot(
                weights_ref[first : first + block, place], other_ref[:, top:bottom],
                preferred_element_type=jnp.float32,
            )
            total = added if total is None else total + added
        for number, (low, high) in enumerate(pieces):
            part = total[low:high]
            here = slice(first + low, first + high)
            if before_ref is not None:
                part = part + before_ref[here, top:bottom]
            out_ref[here, top:bottom] = part
            if raw_ref is not None:
                raw = raw_ref[here, top:bottom]
                for side in range(0, bottom - top, LANES):
                    lanes = slice(side, side + LANES)
                    sums[number][0] += raw[:, lanes] * raw[:, lanes]
                    sums[number][1] += raw[:, lanes] * part[:, lanes]
    return sums


def blocks_of(count):
    return [(first, min(BLOCK, count - first)) for first in range(0, count, BLOCK)]


def drawn_factors(bits, scale_ref, grid_ref):
    scale = scale_ref[0]
    return [
        scale if bit is None else jnp.where(is_drawn(grid_ref, bit), scale, 0.0) for bit in bits
    ]


def all_scratch(others):
    return pltpu.VMEM((sum(x.shape[0] for x in others), others[0].shape[1]), jnp.bfloat16)


def diagonal_kernel(scale_ref, shift_ref, image_ref, text_ref, image_sum_ref, text_sum_ref, weights_ref):
    scale, shift = scale_ref[0], shift_ref[0]
    row_count, width = image_ref.shape
    for rows in blocks_of(row_count):
        add_pairs(
            scale, [scale], shift, image_ref, rows, [row_count], [text_ref], None, image_sum_ref,
            weights_ref, matched=True,
        )
    for first, last in strips(row_count, STRIP):
        for left, right in strips(width, COLUMNS):
            text_sum_ref[first:last, left:right] = lax.dot_general(
                weights_ref[:, first:last], image_ref[:, left:right], (((0,), (0,)), ((), ())),
                preferred_element_type=jnp.float32,
            )


def diagonal(scale, shift, image_half, text_half):
    rows, width = image_half.shape
    return call(
        diagonal_kernel,
        "diagonal",
        [scale, shift, image_half, text_half],
        [((rows, width), jnp.float32)] * 2,
        (rows, 2 * rows, width),
        scratch=[pltpu.VMEM((rows, rows), jnp.bfloat16)],
    )


def near_kernel(
    bit, scale_ref, shift_ref, grid_ref, image_ref, text_ref, image_sum_ref, text_sum_ref, texts_ref,
    images_ref, image_out_ref, text_out_ref, weights_ref,
):
    scale, shift = scale_ref[0], shift_ref[0]
    factors = drawn_factors([bit], scale_ref, grid_ref)
    row_count = image_ref.shape[0]
    for own_ref, other_ref, sum_ref, out_ref in (
        (image_ref, texts_ref, image_sum_ref, image_out_ref),
        (text_ref, images_ref, text_sum_ref, text_out_ref),
    ):
        for rows in blocks_of(row_count):
            add_pairs(
                scale, factors, shift, own_ref, rows, [row_count], [other_ref], sum_ref, out_ref,
                weights_ref,
            )


def add_near(scale, shift, grid, image_half, text_half, image_sum, text_sum, texts, images, bit):
    rows, width = image_half.shape
    return call(
        functools.partial(near_kernel, bit),
        "add_near",
        [scale, shift, grid, image_half, text_half, image_sum, text_sum, texts, images],
        [((rows, width), jnp.float32)] * 2,
        (rows, 2 * rows, width),
        smem=3,
        scratch=[pltpu.VMEM((rows, rows), jnp.bfloat16)],
    )


def add_up_kernel(bits, scale_ref, shift_ref, grid_ref, own_ref, sum_ref, *refs):
    other_refs, (out_ref, weights_ref, all_ref) = refs[: len(bits)], refs[len(bits) :]

    def run(others, counts, factors):
        for rows in blocks_of(own_ref.shape[0]):
            add_pairs(
                scale_ref[0], factors, shift_ref[0], own_ref, rows, counts, others, sum_ref, out_ref,
                weights_ref,
            )

    for_drawn(bits, scale_ref, grid_ref, other_refs, all_ref, run)


def add_up(scale, shift, grid, own, total, others, bits):
    rows, width = own.shape
    count = sum(x.shape[0] for x in others)
    return call(
        functools.partial(add_up_kernel, tuple(bits)),
        "add_up",
        [scale, shift, grid, own, total, *others],
        [((rows, width), jnp.float32)],
        (rows, count, width),
        smem=3,
        scratch=[pltpu.VMEM((rows, count), jnp.bfloat16), all_scratch(others)],
    )[0]


def finish_kernel(bits, scale_ref, shift_ref, grid_ref, own_ref, raw_ref, sum_ref, *refs):
    other_refs, (out_ref, weights_ref, total_ref, sems, all_ref) = refs[: len(bits)], refs[len(bits) :]

    def run(others, counts, factors):
        copies = []
        for first, block in blocks_of(own_ref.shape[0]):
            sums = add_pairs(
                scale_ref[0], factors, shift_ref[0], own_ref, (first, block), counts, others, sum_ref,
                total_ref, weights_ref, raw_ref,
            )
            for (squares, products), (low, high) in zip(sums, strips(block, SLICE)):
                inverse = lax.rsqrt(jnp.sum(squares, axis=-1, keepdims=True) + epsilon)
                radial = jnp.sum(products, axis=-1, keepdims=True) * (inverse * inverse * inverse)
                here = pl.ds(first + low, high - low)
                for top, bottom in strips(own_ref.shape[1], COLUMNS):
                    total_ref[here, top:bottom] = (
                        total_ref[here, top:bottom] * inverse - raw_ref[here, top:bottom] * radial
                    )
                copy = pltpu.make_async_copy(
                    total_ref.at[here, :], out_ref.at[here, :], sems.at[len(copies)]
                )
                copy.start()
                copies.append(copy)
        for copy in copies:
            copy.wait()

    for_drawn(bits, scale_ref, grid_ref, other_refs, all_ref, run)


def finish(scale, shift, grid, own, raw, total, others, bits):
    rows, width = own.shape
    count = sum(x.shape[0] for x in others)
    return call(
        functools.partial(finish_kernel, tuple(bits)),
        "finish",
        [scale, shift, grid, own, raw, total, *others],
        [((rows, width), jnp.float32)],
        (rows, count, width),
        smem=3,
        out_specs=[pl.BlockSpec(memory_space=pl.ANY)],
        scratch=[
            pltpu.VMEM((rows, count), jnp.bfloat16),
            pltpu.VMEM((rows, width), jnp.float32),
            pltpu.SemaphoreType.DMA((len(strips(rows, SLICE)),)),
            all_scratch(others),
        ],
    )[0]


def passed_along(x, axis, by):
    count = lax.axis_size(axis)
    return lax.ppermute(x, axis, [(i, (i + by) % count) for i in range(count)])


def exchanged(x, bit):
    count = lax.axis_size("blk")
    return lax.ppermute(x, "blk", [(i, i ^ (1 << bit)) for i in range(count)])


def with_partners(bits, visual, caption, grid, scale, shift):
    cut = visual.shape[0] * 11 // 16
    near, far = [bit for bit in bits if bit == 0], [bit for bit in bits if bit != 0]
    text_half = normalized(caption)
    text_z = passed_along(text_half, "group", 1)
    far_texts = [exchanged(text_half, bit) for bit in far]
    image_half = normalized(visual)
    image_first, image_last = image_half[:cut], image_half[cut:]
    boths = [(exchanged(text_half, bit), exchanged(image_half, bit)) for bit in near]
    image_sum, text_sum = diagonal(scale, shift, image_half, text_half)
    image_first, image_last, text_z, image_sum, text_sum = lax.optimization_barrier(
        (image_first, image_last, text_z, image_sum, text_sum)
    )
    image_z_first = passed_along(image_first, "group", -1)
    image_z_last = passed_along(image_last, "group", -1)
    far_images_first = [exchanged(image_first, bit) for bit in far]
    for (texts, images), bit in zip(boths, near):
        image_sum, text_sum = add_near(
            scale, shift, grid, image_half, text_half, image_sum, text_sum, texts, images, bit
        )
    image_gradient = finish(
        scale, shift, grid, image_half, visual, image_sum, [*far_texts, text_z], [*far, None]
    )
    text_sum, image_last, image_gradient = lax.optimization_barrier(
        (text_sum, image_last, image_gradient)
    )
    far_images_last = [exchanged(image_last, bit) for bit in far[:1]]
    image_last, image_z_first = lax.optimization_barrier((image_last, image_z_first))
    far_images_last += [exchanged(image_last, bit) for bit in far[1:]]
    text_sum = add_up(
        scale, shift, grid, text_half, text_sum, [*far_images_first, image_z_first], [*far, None]
    )
    text_gradient = finish(
        scale, shift, grid, text_half, caption, text_sum,
        [*far_images_last, image_z_last], [*far, None],
    )
    return image_gradient, text_gradient


def on_device(
    visual_encoder_outputs,
    caption_encoder_outputs,
    partner_lookup_grid,
    sharpness_coefficient,
    sigmoid_shift_term,
):
    rounds, peers = partner_lookup_grid.shape
    bits = range(peers.bit_length() - 1)
    operands = (
        visual_encoder_outputs,
        caption_encoder_outputs,
        partner_lookup_grid,
        sharpness_coefficient,
        sigmoid_shift_term,
    )
    if len(bits) <= rounds + 1:
        return with_partners(bits, *operands)
    choices = list(itertools.combinations(bits, rounds))
    union = jnp.sum(partner_lookup_grid[:, 0])
    branch = jnp.int32(0)
    for number, choice in enumerate(choices):
        branch = jnp.where(union == sum(1 << bit for bit in choice), jnp.int32(number), branch)
    return lax.switch(
        branch, [functools.partial(with_partners, choice) for choice in choices], *operands
    )


def solution(mesh):
    placed = (P(("blk", "group"), None), P(("blk", "group"), None), P(), P(), P())
    return jax.shard_map(
        on_device,
        mesh=mesh,
        in_specs=placed,
        out_specs=(P(("blk", "group"), None), P(("blk", "group"), None)),
        check_vma=False,
    )
```
